256 devices in a mesh: comp: 16 (over z, core), sect: 4 (over y), slab: 4 (over x).
Axes of the slice: x: 4, y: 4, z: 8, core: 2. Of those that a mesh axis runs over, the one named last changes fastest.
Arguments:
- spectrum: float32 [1296, 256, 512], P('comp', 'slab', 'sect'), may hold values from 0 to 1
- land_mask: int32 [256, 512], P('slab', 'sect'), may hold values 0 or 1
- ice_mask: int32 [256, 512], P('slab', 'sect'), may hold values 0 or 1
- wind_u: float32 [256, 512], P('slab', 'sect'), may hold values from -6 to 6
- wind_v: float32 [256, 512], P('slab', 'sect'), may hold values from -6 to 6
- depth: float32 [256, 512], P('slab', 'sect'), may hold values from 2 to 20
Outputs:
- damped: float32 [1296, 256, 512], P('comp', 'slab', 'sect')
- level: float32 [256, 512], P('slab', 'sect')
The draws below stay inside these ranges and needn't reach their ends.
All inputs are finite; a program needn't handle non-finite values. No bound on the sum of `land_mask` or of `ice_mask` on one device may be relied on, other than what follows from the above.
Results may differ from the reference program's by a relative error of at most 0.00011.
Values sent between devices are 32-bit elements; how exact they have to be, the bound alone decides.
A program may use at most 64 MiB of HBM per device.

```python
import math
import jax
import jax.numpy as jnp
from jax import lax

ND = 36
NF = 36
STEPS = 2
JAC = 4
K = 1296
NX = 256
NY = 512


def place_ends(entries, own_key, smallest, largest):
    longest = entries.shape.index(max(entries.shape))
    spots = []
    for shift in (0, 1):
        where = [jax.random.randint(jax.random.fold_in(own_key, axis), (), 0, length) for axis, length in enumerate(entries.shape)]
        where[longest] = (where[longest] + shift) % entries.shape[longest]
        spots.append(tuple(where))
    return entries.at[spots[0]].set(smallest).at[spots[1]].set(largest)


def block_levels(own_key, shape, pieces, smallest, high):
    level = 1.0
    for axis_at, parts in pieces:
        draws = jax.random.uniform(jax.random.fold_in(jax.random.fold_in(own_key, 6), axis_at), (parts,), jnp.float32, smallest / len(pieces), high / len(pieces))
        level = level * jnp.repeat(jnp.exp(draws), shape[axis_at] // parts).reshape((-1,) + (1,) * (len(shape) - 1 - axis_at))
    return level


def noise(rng, shape, scale, bound, split=(), kind=jnp.bfloat16):
    gain = block_levels(rng, shape, split, -0.22, 0.18) if split else 1.0
    result = jax.random.normal(rng, shape, jnp.float32) * scale * gain
    return jnp.minimum(jnp.maximum(result, -bound), bound).astype(kind)


def setup_inputs(seed: int = 0) -> dict:
    keys = jax.random.split(jax.random.key(seed), 7)
    return {
        "spectrum": jnp.clip(1.0 * jax.random.uniform(keys[0], (K, NX, NY), jnp.float32) ** block_levels(keys[0], (K, NX, NY), ((0, 16), (1, 4), (2, 4)), -0.2, 0.2), 0.0, 1.0),
        "land_mask": place_ends((jax.random.randint(keys[1], (NX, NY), 0, 5) < 1).astype(jnp.int32), jax.random.fold_in(keys[1], 1), 0, 1),
        "ice_mask": place_ends((jax.random.randint(keys[2], (NX, NY), 0, 8) < 1).astype(jnp.int32), jax.random.fold_in(keys[2], 1), 0, 1),
        "wind_u": noise(keys[3], (NX, NY), 1.5, 6.0, ((0, 4), (1, 4)), jnp.float32),
        "wind_v": noise(keys[4], (NX, NY), 1.5, 6.0, ((0, 4), (1, 4)), jnp.float32),
        "depth": jnp.clip(jnp.exp(math.log(20.0) - 2.3025851 * jax.random.uniform(keys[5], (NX, NY), jnp.float32) ** block_levels(keys[5], (NX, NY), ((0, 4), (1, 4)), -0.2, 0.2)), 2.0, 20.0),
    }


def tables(index):
    freq_index = (index // ND).astype(jnp.float32)
    angle_index = (index % ND).astype(jnp.float32)
    heading = 2.0 * math.pi * angle_index / ND
    return (jnp.cos(heading), jnp.sin(heading), jnp.power(1.1, -freq_index),
            jnp.power(1.1, freq_index - (NF - 1)), 0.5 + 0.5 * freq_index / (NF - 1))


def upwind(spectra, padded, wet_cells, speed_x, speed_y):
    upper_rows = padded[:, :-2, 1:-1]
    lower_rows = padded[:, 2:, 1:-1]
    left_cells = padded[:, 1:-1, :-2]
    right_cells = padded[:, 1:-1, 2:]
    change = (jnp.maximum(speed_x, 0.0) * (spectra - upper_rows) + jnp.minimum(speed_x, 0.0) * (lower_rows - spectra)
              + jnp.maximum(speed_y, 0.0) * (spectra - left_cells) + jnp.minimum(speed_y, 0.0) * (right_cells - spectra))
    return (spectra - change) * wet_cells


def forcing(spectra, energy, wind_east, wind_north, ice_cover, cosine, sine, high_ratio):
    project = cosine * wind_east + sine * wind_north
    growth = 0.5 * high_ratio * jnp.square(jnp.maximum(project, 0.0)) * (1.0 - ice_cover)
    return spectra * (1.0 + growth) / (1.0 + 2.0 * high_ratio * jnp.square(energy))


def stress_weights(cosine, sine, shoaling):
    return jnp.stack([shoaling * (cosine * cosine + 1.0) - 0.5, shoaling * (sine * sine + 1.0) - 0.5])


def solve(stress):
    padded = jnp.pad(stress, ((0, 0), (1, 1), (1, 1)))
    source_term = -((padded[0, 2:, 1:-1] + padded[0, :-2, 1:-1] - 2.0 * stress[0])
                    + (padded[1, 1:-1, 2:] + padded[1, 1:-1, :-2] - 2.0 * stress[1]))
    surge_level = source_term / 4.5
    for _ in range(JAC):
        neighbours = jnp.pad(surge_level, 1)
        surge_level = (source_term + neighbours[2:, 1:-1] + neighbours[:-2, 1:-1]
                       + neighbours[1:-1, 2:] + neighbours[1:-1, :-2]) / 4.5
    return surge_level


def reference(spectrum, land_mask, ice_mask, wind_u, wind_v, depth):
    total_comp = ND * NF
    wet_cells = (1 - land_mask).astype(jnp.float32)
    ice_cover = ice_mask.astype(jnp.float32)
    cosine, sine, low_ratio, high_ratio, shoaling = tables(jnp.arange(total_comp, dtype=jnp.int32))
    speed_x = (0.7 * low_ratio * cosine).reshape(NF, ND)
    speed_y = (0.7 * low_ratio * sine).reshape(NF, ND)
    blocks = spectrum.reshape(NF, ND, NX, NY)

    def propagate(packed):
        spectra, along_x, along_y = packed
        spectra = spectra * wet_cells
        for _ in range(STEPS):
            padded = jnp.pad(spectra, ((0, 0), (1, 1), (1, 1)))
            spectra = upwind(spectra, padded, wet_cells, along_x[:, None, None], along_y[:, None, None])
        return spectra

    spectra = lax.map(propagate, (blocks, speed_x, speed_y)).reshape(total_comp, NX, NY)
    energy = jnp.sum(spectra, axis=0) / total_comp
    sourced = forcing(spectra, energy, wind_u, wind_v, ice_cover, cosine[:, None, None],
                      sine[:, None, None], high_ratio[:, None, None])
    stress = jnp.einsum("sk,krc->src", stress_weights(cosine, sine, shoaling), sourced,
                        precision=lax.Precision.HIGHEST) / total_comp
    surge_level = solve(stress)
    final_energy = jnp.sum(sourced, axis=0) / total_comp
    damped = sourced / (1.0 + 4.0 * final_energy / (jnp.square(depth + surge_level) + 1.0))
    return damped, surge_level
```

```python
import functools
import math

import jax
import jax.numpy as jnp
import numpy as np
from jax import lax
from jax.experimental import pallas as pl
from jax.experimental.pallas import tpu as pltpu
from jax.sharding import PartitionSpec as P

ND = 36
NF = 36
K = ND * NF
JAC = 4
LOCAL = 81
GROUPS = 9
COMPS = 16
SIDE = 4
MESH = pl.DeviceIdType.MESH
HIGHEST = lax.Precision.HIGHEST

ROW_DIR = (0, 1, 1, 0)
COL_DIR = (0, 0, 1, 1)
ROW_SLOT = (0, 0, 2, 2)
COL_SLOT = (0, 2, 0, 2)
EXTRA_SLOT = 4

LANE_ROWS = 16
T_LANE = 0
T_ROW = T_LANE + 2 * LANE_ROWS
T_PICK = T_ROW + 2 * 96
T_SUM = T_PICK + 2 * 96
T_END = T_SUM + 2 * 64


def direction(index):
    heading = 2.0 * math.pi * index / ND
    return math.cos(heading), math.sin(heading)


@functools.cache
def table():
    whole = np.zeros((COMPS, T_END, 128), np.float64)
    for member in range(COMPS):
        first = member % 4
        start = 9 * member // 4
        for group in range(GROUPS):
            quad = (first + group) % 4
            turn = group // 4
            freq_slot = (first + group) // 4
            freq = start + freq_slot
            row_dir, col_dir = ROW_DIR[quad], COL_DIR[quad]
            row_slot = ROW_SLOT[quad] + turn if turn < 2 else EXTRA_SLOT
            col_slot = COL_SLOT[quad] + turn if turn < 2 else EXTRA_SLOT
            low = 1.1 ** (-freq)
            scale = math.sqrt(0.5 * 1.1 ** (freq - (NF - 1)))
            for i in range(9):
                cosine, sine = direction(9 * quad + i)
                along_x, along_y = 0.7 * low * abs(cosine), 0.7 * low * abs(sine)
                values = [1.0 - along_x - along_y, along_x, along_y, scale * cosine, scale * sine]
                row = 2 * (9 * row_slot + i)
                lane = 2 * (9 * col_slot + i)
                pair = slice(lane, lane + 2)
                at = T_LANE + LANE_ROWS * col_dir
                for v, value in enumerate(values):
                    whole[member, at + v, pair] = value
                whole[member, at + 5, pair] = 1.0 if row_dir == 0 else 0.0
                whole[member, at + 6 + freq_slot, pair] = 1.0
                whole[member, at + 9 + freq_slot, pair] = cosine * cosine
                at = T_ROW + 96 * row_dir + row
                for v, value in enumerate(values):
                    whole[member, at : at + 2, v] = value
                whole[member, at : at + 2, 5] = 1.0 if col_dir == 0 else 0.0
                near = lane + 1 if col_dir == 0 else lane
                whole[member, T_PICK + 96 * row_dir + row + row_dir, near] = 1.0
                at = T_SUM + 64 * row_dir
                for side in (0, 1):
                    out = side if row_dir == 0 else 6 + side
                    whole[member, at + 16 * freq_slot + out, row + side] = 1.0
                    whole[member, at + 16 * freq_slot + 8 + out, row + side] = cosine * cosine
                    whole[member, at + 48 + out, row + side] = 1.0
    return whole.astype(np.float32)


def power(base, exponent):
    result = jnp.float32(1.0)
    for bit in range(6):
        odd = (exponent // (2**bit)) % 2
        result = result * jnp.where(odd == 1, jnp.float32(base ** (2**bit)), jnp.float32(1.0))
    return result


def from_above(cells, above=None):
    turned = pltpu.roll(cells, 1, 1)
    if above is None:
        top = jnp.zeros((1, 8, 128), jnp.float32)
    else:
        top = pltpu.roll(above, 1, 0)[None]
    before = jnp.concatenate([top, turned[:-1]], axis=0)
    sub = lax.broadcasted_iota(jnp.int32, cells.shape, 1)
    return jnp.where(sub == 0, before, turned)


def from_below(cells, below=None):
    turned = pltpu.roll(cells, 7, 1)
    if below is None:
        bottom = jnp.zeros((1, 8, 128), jnp.float32)
    else:
        bottom = pltpu.roll(below, 7, 0)[None]
    after = jnp.concatenate([turned[1:], bottom], axis=0)
    sub = lax.broadcasted_iota(jnp.int32, cells.shape, 1)
    return jnp.where(sub == 7, after, turned)


def lanes(cells, shift):
    return pltpu.roll(cells, shift % 128, cells.ndim - 1)


def lane_index(shape):
    return lax.broadcasted_iota(jnp.int32, shape, len(shape) - 1)


def from_left(cells):
    return jnp.where(lane_index(cells.shape) == 0, 0.0, lanes(cells, 1))


def from_right(cells):
    return jnp.where(lane_index(cells.shape) == 127, 0.0, lanes(cells, 127))


def step_kernel(
    spec_ref, land_ref, ice_ref, wu_ref, wv_ref, depth_ref, table_ref,
    grown_ref, factor_ref, level_ref,
    x, land, ice, wu, wv, depth, tab, wet,
    row_send, row_recv, col_send, col_recv, corner_recv,
    acc, row_fix, col_fix,
    rs_send, rs_recv, ag_send, ag_recv,
    edge_send, edge_recv, strip_send, strip_recv, tip_recv,
    fac,
    load_sem, small_sem, out_sem,
    halo_ssem, halo_rsem, rs_ssem, rs_rsem, ag_ssem, ag_rsem, rim_ssem, rim_rsem,
):
    comp = lax.axis_index("comp")
    slab = lax.axis_index("slab")
    sect = lax.axis_index("sect")
    first = comp % 4

    def place(down, right):
        return {"slab": (slab + down + SIDE) % SIDE, "sect": (sect + right + SIDE) % SIDE}

    around = [place(a, b) for a in (-1, 0, 1) for b in (-1, 0, 1) if (a, b) != (0, 0)]
    others = [{"comp": (comp + shift) % COMPS} for shift in range(1, COMPS)]
    barrier = pltpu.get_barrier_semaphore()
    for peer in around + others:
        pl.semaphore_signal(barrier, 1, device_id=peer, device_id_type=MESH)

    small = [
        pltpu.make_async_copy(src, dst, small_sem.at[n])
        for n, (src, dst) in enumerate(
            [(land_ref, land), (ice_ref, ice), (wu_ref, wu), (wv_ref, wv), (depth_ref, depth),
             (table_ref.at[comp], tab)]
        )
    ]
    for copy in small:
        copy.start()

    def load(group):
        rows = pl.ds(9 * group, 9)
        return pltpu.make_async_copy(spec_ref.at[rows], x.at[rows], load_sem.at[group])

    for group in range(GROUPS):
        load(group).start()

    lane = lane_index((8, 128))
    lane_pair = lane // 2
    sub = lax.broadcasted_iota(jnp.int32, (8, 128), 0)
    even_lane = lane % 2 == 0
    even_sub = sub % 2 == 0

    row_send[0, 9:12] = jnp.zeros((3, 8, 128), jnp.float32)
    row_send[1, 9:12] = jnp.zeros((3, 8, 128), jnp.float32)
    acc[...] = jnp.zeros_like(acc)
    for copy in small:
        copy.wait()
    wet[...] = (1 - land[...]).astype(jnp.float32)
    open_sea = (1 - ice[...]).astype(jnp.float32)
    wu[...] = wu[...] * open_sea
    wv[...] = wv[...] * open_sea

    def group_of(quad, turn):
        return (quad - first + 4) % 4 + 4 * turn

    def pack(quad, turn, packed):
        group = group_of(quad, turn)
        row_slot = ROW_SLOT[quad] + turn if turn < 2 else EXTRA_SLOT
        col_slot = COL_SLOT[quad] + turn if turn < 2 else EXTRA_SLOT
        load(group).wait()
        for i in range(9):
            cells = x[9 * group + i]
            row = 2 * (9 * row_slot + i)
            to = (ROW_DIR[quad], row // 8, pl.ds(row % 8, 2))
            if ROW_DIR[quad] == 0:
                row_send[to] = cells[7, 6:8] * wet[7, 6:8, :]
            else:
                row_send[to] = cells[0, 0:2] * wet[0, 0:2, :]
            pair = 9 * col_slot + i
            shift = 2 * pair + 2 if COL_DIR[quad] == 0 else 2 * pair
            packed = jnp.where(lane_pair == pair, lanes(cells, shift), packed)
        return packed

    for way in (0, 1):
        packed = jnp.zeros((8, 8, 128), jnp.float32)
        for quad in range(4):
            if COL_DIR[quad] == way:
                for turn in (0, 1):
                    packed = pack(quad, turn, packed)
        col_send[way] = packed
    for quad in range(4):
        @pl.when(first == quad)
        def _(quad=quad):
            col_send[COL_DIR[quad]] = pack(quad, 2, col_send[COL_DIR[quad]])

    wet_now = wet[...]
    for way in (0, 1):
        at = 126 if way == 0 else 0
        one, two = wet_now[:, :, at : at + 1], wet_now[:, :, at + 1 : at + 2]
        pair_wet = jnp.where(even_lane, one, two)
        col_send[way] = jnp.where(lane_pair == 63, pair_wet, col_send[way] * pair_wet)
    row_send[0, 11, 2:4] = wet[7, 6:8, :]
    row_send[1, 11, 2:4] = wet[0, 0:2, :]

    pl.semaphore_wait(barrier, len(around) + len(others))

    def remote(src, dst, ssem, rsem, peer):
        return pltpu.make_async_remote_copy(
            src_ref=src, dst_ref=dst, send_sem=ssem, recv_sem=rsem, device_id=peer, device_id_type=MESH
        )

    halo = [
        remote(col_send.at[0], col_recv.at[0], halo_ssem.at[0], halo_rsem.at[0], place(0, 1)),
        remote(col_send.at[1], col_recv.at[1], halo_ssem.at[1], halo_rsem.at[1], place(0, -1)),
    ]
    for way in (0, 1):
        step = 1 if way == 0 else -1
        halo.append(
            remote(col_send.at[way, 7], corner_recv.at[way, 0], halo_ssem.at[2 + way], halo_rsem.at[2 + way],
                   place(1, step))
        )
        halo.append(
            remote(col_send.at[way, 0], corner_recv.at[way, 1], halo_ssem.at[4 + way], halo_rsem.at[4 + way],
                   place(-1, step))
        )
    halo.append(remote(row_send.at[0], row_recv.at[0], halo_ssem.at[6], halo_rsem.at[6], place(1, 0)))
    halo.append(remote(row_send.at[1], row_recv.at[1], halo_ssem.at[7], halo_rsem.at[7], place(-1, 0)))
    for copy in halo:
        copy.start()

    for quad in range(4):
        upwind_row = from_above if ROW_DIR[quad] == 0 else from_below
        upwind_col = from_left if COL_DIR[quad] == 0 else from_right

        def body(turn, carry, quad=quad, upwind_row=upwind_row, upwind_col=upwind_col):
            group = group_of(quad, turn)
            freq = (9 * comp + group) // 4
            slot = (first + group) // 4
            low = 0.7 * power(1.0 / 1.1, freq)
            scale = math.sqrt(0.5 * 1.1 ** (-(NF - 1))) * power(math.sqrt(1.1), freq)
            total_e = jnp.zeros((8, 8, 128), jnp.float32)
            total_f = jnp.zeros((8, 8, 128), jnp.float32)
            total_c = jnp.zeros((8, 8, 128), jnp.float32)
            for i in range(9):
                cosine, sine = direction(9 * quad + i)
                along_x, along_y = low * abs(cosine), low * abs(sine)
                stay = 1.0 - along_x - along_y
                cells = x[9 * group + i] * wet[...]
                for _ in range(2):
                    cells = wet[...] * (
                        stay * cells + along_x * upwind_row(cells) + along_y * upwind_col(cells)
                    )
                push = jnp.maximum((scale * cosine) * wu[...] + (scale * sine) * wv[...], 0.0)
                grown = cells + cells * (push * push)
                x[9 * group + i] = grown
                total_e += cells
                total_f += grown
                total_c += (cosine * cosine) * grown
            acc[6] += total_e
            acc[2 * slot] += total_f
            acc[2 * slot + 1] += total_c
            return carry

        lax.fori_loop(0, 2 + (first == quad).astype(jnp.int32), body, 0)

    for copy in halo:
        copy.wait_recv()

    has = {
        "up": (slab > 0).astype(jnp.float32), "down": (slab < SIDE - 1).astype(jnp.float32),
        "left": (sect > 0).astype(jnp.float32), "right": (sect < SIDE - 1).astype(jnp.float32),
    }
    col_terms = []
    for way in (0, 1):
        lane_row = lambda n: tab[T_LANE + LANE_ROWS * way + n : T_LANE + LANE_ROWS * way + n + 1, :][None]
        stay, along_x, along_y, push_u, push_v, is_up = [lane_row(n) for n in range(6)]
        side = has["left"] if way == 0 else has["right"]
        got = col_recv[way] * side
        above = corner_recv[way, 0] * (side * has["up"])
        below = corner_recv[way, 1] * (side * has["down"])
        turn = 127 if way == 0 else 1
        near, near_above, near_below = lanes(got, turn), lanes(above, turn), lanes(below, turn)
        halo_wet = got[:, :, 127:128] if way == 0 else got[:, :, 126:127]
        at_near, at_far = (0, 1) if way == 0 else (127, 126)
        wet_near, wet_far = wet_now[:, :, at_near : at_near + 1], wet_now[:, :, at_far : at_far + 1]
        up_now = jnp.where(is_up > 0.5, from_above(near, near_above), from_below(near, near_below))
        outside = halo_wet * (stay * near + along_x * up_now + along_y * got)
        one = wet_near * (along_y * near)
        up_one = jnp.where(is_up > 0.5, from_above(one), from_below(one))
        two = wet_near * (stay * one + along_x * up_one + along_y * outside)
        far = lanes(wet_far * (along_y * one), 1 if way == 0 else 127)
        fix = jnp.where(even_lane, two, far) if way == 0 else jnp.where(even_lane, far, two)
        low_at = 0 if way == 0 else 126
        wind = [
            jnp.where(even_lane, w[:, :, low_at : low_at + 1], w[:, :, low_at + 1 : low_at + 2])
            for w in (wu, wv)
        ]
        push = jnp.maximum(push_u * wind[0] + push_v * wind[1], 0.0)
        fix_grown = fix + fix * (push * push)
        col_fix[way] = fix_grown
        terms = []
        for slot in range(3):
            terms += [fix_grown * lane_row(6 + slot), fix_grown * lane_row(9 + slot)]
        terms.append(fix)
        stacked = jnp.concatenate([term.reshape(64, 128) for term in terms], axis=0)
        k_index = lax.broadcasted_iota(jnp.int32, (128, 128), 0)
        to_lane = lane_index((128, 128))
        pick = ((to_lane == k_index % 2 + low_at) & (k_index < 90)).astype(jnp.float32)
        col_terms.append(jnp.dot(stacked, pick, precision=HIGHEST, preferred_element_type=jnp.float32))
    col_sum = (col_terms[0] + col_terms[1]).reshape(7, 8, 8, 128)
    acc[...] += col_sum

    for way in (0, 1):
        at = T_ROW + 96 * way
        spread = lambda n: jnp.broadcast_to(tab[at : at + 96, n : n + 1], (96, 128)).reshape(12, 8, 128)
        stay, along_x, along_y, push_u, push_v, is_left = [spread(n) for n in range(6)]
        side = has["up"] if way == 0 else has["down"]
        got = row_recv[way] * side
        near = pltpu.roll(got, 7 if way == 0 else 1, 1)
        edge = 7 if way == 0 else 0
        left_corner = corner_recv[0, way, edge : edge + 1, :] * (side * has["left"])
        right_corner = corner_recv[1, way, edge : edge + 1, :] * (side * has["right"])
        choose = tab[T_PICK + 96 * way : T_PICK + 96 * way + 96, :].reshape(12, 8, 128)
        corner = jnp.sum(
            choose * jnp.where(is_left > 0.5, left_corner[None], right_corner[None]), axis=2, keepdims=True
        )
        halo_wet = got[11, 3:4, :] if way == 0 else got[11, 2:3, :]
        tile, near_row, far_row = (0, 0, 1) if way == 0 else (7, 7, 6)
        wet_near, wet_far = wet[tile, near_row : near_row + 1, :], wet[tile, far_row : far_row + 1, :]
        lane3 = lane_index((12, 8, 128))
        beside = jnp.where(
            is_left > 0.5,
            jnp.where(lane3 == 0, corner, lanes(near, 1)),
            jnp.where(lane3 == 127, corner, lanes(near, 127)),
        )
        outside = halo_wet * (stay * near + along_x * got + along_y * beside)
        one = wet_near * (along_x * near)
        beside_one = jnp.where(is_left > 0.5, from_left(one), from_right(one))
        two = wet_near * (stay * one + along_y * beside_one + along_x * outside)
        far = pltpu.roll(wet_far * (along_x * one), 1 if way == 0 else 7, 1)
        fix = jnp.where(even_sub, two, far) if way == 0 else jnp.where(even_sub, far, two)
        low_at = 0 if way == 0 else 6
        wind = [
            jnp.where(even_sub, w[tile, low_at : low_at + 1, :], w[tile, low_at + 1 : low_at + 2, :])
            for w in (wu, wv)
        ]
        push = jnp.maximum(push_u * wind[0] + push_v * wind[1], 0.0)
        fix_grown = fix + fix * (push * push)
        row_fix[way] = fix_grown
        at = T_SUM + 64 * way
        weights = tab[at : at + 48, 0:96]
        sum_grown = jnp.dot(weights, fix_grown.reshape(96, 128), precision=HIGHEST,
                            preferred_element_type=jnp.float32)
        sum_moved = jnp.dot(tab[at + 48 : at + 56, 0:96], fix.reshape(96, 128), precision=HIGHEST,
                            preferred_element_type=jnp.float32)
        for v in range(6):
            acc[v, tile] += sum_grown[8 * v : 8 * v + 8]
        acc[6, tile] += sum_moved

    low_half = sub < 4
    for slot in range(4):
        if slot < 3:
            one, two = acc[2 * slot], acc[2 * slot + 1]
            even_tile = jnp.where(low_half, one, pltpu.roll(two, 4, 1))
            odd_tile = jnp.where(low_half, pltpu.roll(one, 4, 1), two)
        else:
            even_tile, odd_tile = acc[6], pltpu.roll(acc[6], 4, 1)
        for tile in range(8):
            rs_send[2 * tile, 8 * slot : 8 * slot + 8] = even_tile[tile]
            rs_send[2 * tile + 1, 8 * slot : 8 * slot + 8] = odd_tile[tile]
    rs = []
    for shift in range(1, COMPS):
        peer = (comp + shift) % COMPS
        rs.append(
            remote(rs_send.at[peer, pl.ds(0, 28)], rs_recv.at[comp, pl.ds(0, 28)], rs_ssem.at[shift],
                   rs_rsem.at[shift], {"comp": peer})
        )
    for copy in rs:
        copy.start()
    rs_recv[comp] = rs_send[comp]

    def store(group):
        rows = pl.ds(9 * group, 9)
        return pltpu.make_async_copy(x.at[rows], grown_ref.at[rows], out_sem.at[group])

    def amend(quad, turn):
        group = group_of(quad, turn)
        row_slot = ROW_SLOT[quad] + turn if turn < 2 else EXTRA_SLOT
        col_slot = COL_SLOT[quad] + turn if turn < 2 else EXTRA_SLOT
        way = COL_DIR[quad]
        fixes = col_fix[way]
        inside = lane < 2 if way == 0 else lane >= 126
        for i in range(9):
            at = 9 * group + i
            pair = 2 * (9 * col_slot + i)
            moved = lanes(fixes, -pair if way == 0 else 126 - pair)
            x[at] = x[at] + jnp.where(inside, moved, 0.0)
            row = 2 * (9 * row_slot + i)
            rows = row_fix[ROW_DIR[quad], row // 8, row % 8 : row % 8 + 2, :]
            if ROW_DIR[quad] == 0:
                x[at, 0, 0:2, :] += rows
            else:
                x[at, 7, 6:8, :] += rows
        store(group).start()

    for quad in range(4):
        for turn in (0, 1):
            amend(quad, turn)
        @pl.when(first == quad)
        def _(quad=quad):
            amend(quad, 2)

    for copy in rs:
        copy.wait_recv()

    energy = rs_recv[0, 24:28, :]
    for source in range(1, COMPS):
        energy = energy + rs_recv[source, 24:28, :]
    energy = energy / K
    energy = jnp.concatenate([energy, energy], axis=0)
    square = energy * energy
    plain = jnp.zeros((8, 128), jnp.float32)
    shoaled = jnp.zeros((8, 128), jnp.float32)
    for freq in range(NF):
        part = None
        for source in range(COMPS):
            slot = freq - 9 * source // 4
            if 0 <= slot < 3:
                tile = rs_recv[source, 8 * slot : 8 * slot + 8, :]
                part = tile if part is None else part + tile
        part = part / (1.0 + (2.0 * 1.1 ** (freq - (NF - 1))) * square)
        plain = plain + part
        shoaled = shoaled + (0.5 + 0.5 * freq / (NF - 1)) * part
    turned = pltpu.roll(shoaled, 4, 0)
    final = plain / K
    stress_x = (turned + shoaled - 0.5 * plain) / K
    stress_y = (2.0 * shoaled - turned - 0.5 * plain) / K
    ag_send[0:8] = jnp.where(low_half, energy, pltpu.roll(final, 4, 0))
    ag_send[8:16] = jnp.where(low_half, stress_x, pltpu.roll(stress_y, 4, 0))
    ag = [
        remote(ag_send, ag_recv.at[comp], ag_ssem.at[shift], ag_rsem.at[shift], {"comp": (comp + shift) % COMPS})
        for shift in range(1, COMPS)
    ]
    for copy in ag:
        copy.start()
    ag_recv[comp] = ag_send[...]
    for copy in ag:
        copy.wait_recv()

    gathered = ag_recv[...].reshape(8, 2, 16, 128)

    def low_of(at):
        one, two = gathered[:, 0, at : at + 8], gathered[:, 1, at : at + 8]
        return jnp.where(low_half, one, pltpu.roll(two, 4, 1))

    def high_of(at):
        one, two = gathered[:, 0, at : at + 8], gathered[:, 1, at : at + 8]
        return jnp.where(low_half, pltpu.roll(one, 4, 1), two)

    stress_x, stress_y = low_of(8), high_of(8)

    edge_send[0] = stress_x
    edge_send[1] = stress_y
    strip_send[...] = jnp.where(
        (lane < 8) | (lane >= 120), stress_x, jnp.where(lane < 64, lanes(stress_y, 8), lanes(stress_y, 120))
    )
    rim = [
        remote(strip_send, strip_recv.at[0], rim_ssem.at[0], rim_rsem.at[0], place(0, 1)),
        remote(strip_send, strip_recv.at[1], rim_ssem.at[1], rim_rsem.at[1], place(0, -1)),
        remote(edge_send.at[:, 7], edge_recv.at[0], rim_ssem.at[2], rim_rsem.at[2], place(1, 0)),
        remote(edge_send.at[:, 0], edge_recv.at[1], rim_ssem.at[3], rim_rsem.at[3], place(-1, 0)),
        remote(strip_send.at[7], tip_recv.at[0, 0], rim_ssem.at[4], rim_rsem.at[4], place(1, 1)),
        remote(strip_send.at[7], tip_recv.at[1, 0], rim_ssem.at[5], rim_rsem.at[5], place(1, -1)),
        remote(strip_send.at[0], tip_recv.at[0, 1], rim_ssem.at[6], rim_rsem.at[6], place(-1, 1)),
        remote(strip_send.at[0], tip_recv.at[1, 1], rim_ssem.at[7], rim_rsem.at[7], place(-1, -1)),
    ]
    for copy in rim:
        copy.start()
    energy, final = low_of(0), high_of(0)
    start = (9 * comp) // 4
    high = 1.1 ** (-(NF - 1)) * power(1.1, start)
    rates = [
        1.0 / (1.0 + (2.0 * 1.1**slot * high) * (energy * energy)) for slot in range(3)
    ]
    for copy in rim:
        copy.wait_recv()

    big_lane = lane_index((80, 128))
    big_row = lax.broadcasted_iota(jnp.int32, (80, 128), 0)
    first_row = jnp.where(slab > 0, 0, 8)
    last_row = jnp.where(slab < SIDE - 1, 80, 72)
    in_rows = (big_row >= first_row) & (big_row < last_row)
    right_end = jnp.where(sect < SIDE - 1, 8, 0)
    left_start = jnp.where(sect > 0, 120, 128)
    in_strip = in_rows & ((big_lane < right_end) | (big_lane >= left_start))

    def middle(n, cells):
        return jnp.where(
            in_rows,
            jnp.concatenate([edge_recv[0, n], cells.reshape(64, 128), edge_recv[1, n]], axis=0),
            0.0,
        )

    left_strip = jnp.concatenate([tip_recv[0, 0], strip_recv[0].reshape(64, 128), tip_recv[0, 1]], axis=0)
    right_strip = jnp.concatenate([tip_recv[1, 0], strip_recv[1].reshape(64, 128), tip_recv[1, 1]], axis=0)
    xx = middle(0, stress_x)
    yy = middle(1, stress_y)
    xx_strip = jnp.where(in_strip, jnp.where(big_lane < 64, right_strip, left_strip), 0.0)
    yy_strip = jnp.where(
        in_strip, jnp.where(big_lane < 64, lanes(right_strip, 120), lanes(left_strip, 8)), 0.0
    )

    def beside(center, strip):
        center_up, strip_up = lanes(center, 127), lanes(strip, 127)
        center_down, strip_down = lanes(center, 1), lanes(strip, 1)
        last, head = big_lane == 127, big_lane == 0
        return (
            jnp.where(last, strip_up, center_up) + jnp.where(head, strip_down, center_down),
            jnp.where(last, center_up, strip_up) + jnp.where(head, center_down, strip_down),
        )

    def above_below(cells):
        return pltpu.roll(cells, 1, 0) + pltpu.roll(cells, 79, 0)

    yy_sides = beside(yy, yy_strip)
    source = jnp.where(in_rows, -((above_below(xx) - 2.0 * xx) + (yy_sides[0] - 2.0 * yy)), 0.0)
    source_strip = jnp.where(
        in_strip, -((above_below(xx_strip) - 2.0 * xx_strip) + (yy_sides[1] - 2.0 * yy_strip)), 0.0
    )
    surge, surge_strip = source / 4.5, source_strip / 4.5
    for _ in range(JAC):
        sides = beside(surge, surge_strip)
        surge, surge_strip = (
            jnp.where(in_rows, (source + above_below(surge) + sides[0]) / 4.5, 0.0),
            jnp.where(in_strip, (source_strip + above_below(surge_strip) + sides[1]) / 4.5, 0.0),
        )
    surge = surge[8:72].reshape(8, 8, 128)
    reach = depth[...] + surge
    damping = 1.0 / (1.0 + 4.0 * final / (reach * reach + 1.0))
    for slot in range(3):
        fac[slot] = rates[slot] * damping
    for group in range(GROUPS):
        factor_ref[group] = fac[(first + group) // 4]
    level_ref[...] = surge

    for group in range(GROUPS):
        store(group).wait()
    for copy in halo + rs + ag + rim:
        copy.wait_send()


def damp_kernel(grown_ref, factor_ref, level_ref, out_ref, level_out):
    for group in range(grown_ref.shape[0] // 9):
        factor = factor_ref[group]
        for i in range(9):
            out_ref[9 * group + i] = grown_ref[9 * group + i] * factor
    level_out[...] = level_ref[...]


def local(spectrum, land_mask, ice_mask, wind_u, wind_v, depth):
    f32 = jnp.float32
    block = (8, 8, 128)
    anywhere = pl.BlockSpec(memory_space=pltpu.HBM)
    vmem = pl.BlockSpec(memory_space=pltpu.VMEM)
    dma = pltpu.SemaphoreType.DMA
    grown, factor, level = pl.pallas_call(
        step_kernel,
        out_shape=(
            jax.ShapeDtypeStruct((LOCAL, *block), f32),
            jax.ShapeDtypeStruct((GROUPS, *block), f32),
            jax.ShapeDtypeStruct(block, f32),
        ),
        in_specs=[anywhere] * 7,
        out_specs=(anywhere, vmem, vmem),
        scratch_shapes=[
            pltpu.VMEM((LOCAL, *block), f32),
            pltpu.VMEM(block, jnp.int32),
            pltpu.VMEM(block, jnp.int32),
            pltpu.VMEM(block, f32),
            pltpu.VMEM(block, f32),
            pltpu.VMEM(block, f32),
            pltpu.VMEM((T_END, 128), f32),
            pltpu.VMEM(block, f32),
            pltpu.VMEM((2, 12, 8, 128), f32),
            pltpu.VMEM((2, 12, 8, 128), f32),
            pltpu.VMEM((2, *block), f32),
            pltpu.VMEM((2, *block), f32),
            pltpu.VMEM((2, 2, 8, 128), f32),
            pltpu.VMEM((7, *block), f32),
            pltpu.VMEM((2, 12, 8, 128), f32),
            pltpu.VMEM((2, *block), f32),
            pltpu.VMEM((COMPS, 32, 128), f32),
            pltpu.VMEM((COMPS, 32, 128), f32),
            pltpu.VMEM((16, 128), f32),
            pltpu.VMEM((COMPS, 16, 128), f32),
            pltpu.VMEM((2, *block), f32),
            pltpu.VMEM((2, 2, 8, 128), f32),
            pltpu.VMEM(block, f32),
            pltpu.VMEM((2, *block), f32),
            pltpu.VMEM((2, 2, 8, 128), f32),
            pltpu.VMEM((3, *block), f32),
            dma((GROUPS,)),
            dma((6,)),
            dma((GROUPS,)),
            dma((8,)),
            dma((8,)),
            dma((COMPS,)),
            dma((COMPS,)),
            dma((COMPS,)),
            dma((COMPS,)),
            dma((8,)),
            dma((8,)),
        ],
        compiler_params=pltpu.CompilerParams(
            collective_id=0, has_side_effects=True, vmem_limit_bytes=60 * 1024 * 1024
        ),
        name="wave_step",
    )(
        spectrum.reshape(LOCAL, *block),
        land_mask.reshape(block),
        ice_mask.reshape(block),
        wind_u.reshape(block),
        wind_v.reshape(block),
        depth.reshape(block),
        jnp.asarray(table()),
    )
    parts = 3
    damped, level = pl.pallas_call(
        damp_kernel,
        grid=(parts,),
        out_shape=(jax.ShapeDtypeStruct((LOCAL, *block), f32), jax.ShapeDtypeStruct(block, f32)),
        in_specs=[
            pl.BlockSpec((LOCAL // parts, *block), lambda n: (n, 0, 0, 0)),
            pl.BlockSpec((GROUPS // parts, *block), lambda n: (n, 0, 0, 0)),
            pl.BlockSpec(block, lambda n: (0, 0, 0)),
        ],
        out_specs=(
            pl.BlockSpec((LOCAL // parts, *block), lambda n: (n, 0, 0, 0)),
            pl.BlockSpec(block, lambda n: (0, 0, 0)),
        ),
        compiler_params=pltpu.CompilerParams(vmem_limit_bytes=60 * 1024 * 1024),
        name="damp",
    )(grown, factor, level)
    return damped.reshape(spectrum.shape), level.reshape(depth.shape)


def solution(mesh):
    cells = P("slab", "sect")
    spectra = P("comp", "slab", "sect")
    return jax.shard_map(
        local,
        mesh=mesh,
        in_specs=(spectra, cells, cells, cells, cells, cells),
        out_specs=(spectra, cells),
        check_vma=False,
    )
```

```python
import functools
import math

import jax
import jax.numpy as jnp
import numpy as np
from jax import lax
from jax.experimental import pallas as pl
from jax.experimental.pallas import tpu as pltpu
from jax.sharding import PartitionSpec as P

ND = 36
NF = 36
K = ND * NF
JAC = 4
LOCAL = 81
GROUPS = 9
COMPS = 16
SIDE = 4
FAR_FIRST = (8, 7, 9, 6, 10, 5, 11, 4, 12, 3, 13, 2, 14, 1, 15)
MESH = pl.DeviceIdType.MESH
HIGHEST = lax.Precision.HIGHEST

ROW_DIR = (0, 1, 1, 0)
COL_DIR = (0, 0, 1, 1)
ROW_SLOT = (0, 0, 2, 2)
COL_SLOT = (0, 2, 0, 2)
EXTRA_SLOT = 4

LANE_ROWS = 16
T_LANE = 0
T_ROW = T_LANE + 2 * LANE_ROWS
T_PICK = T_ROW + 2 * 96
T_SUM = T_PICK + 2 * 96
T_END = T_SUM + 2 * 64


def direction(index):
    heading = 2.0 * math.pi * index / ND
    return math.cos(heading), math.sin(heading)


@functools.cache
def table():
    whole = np.zeros((COMPS, T_END, 128), np.float64)
    for member in range(COMPS):
        first = member % 4
        start = 9 * member // 4
        for group in range(GROUPS):
            quad = (first + group) % 4
            turn = group // 4
            freq_slot = (first + group) // 4
            freq = start + freq_slot
            row_dir, col_dir = ROW_DIR[quad], COL_DIR[quad]
            row_slot = ROW_SLOT[quad] + turn if turn < 2 else EXTRA_SLOT
            col_slot = COL_SLOT[quad] + turn if turn < 2 else EXTRA_SLOT
            low = 1.1 ** (-freq)
            scale = math.sqrt(0.5 * 1.1 ** (freq - (NF - 1)))
            for i in range(9):
                cosine, sine = direction(9 * quad + i)
                along_x, along_y = 0.7 * low * abs(cosine), 0.7 * low * abs(sine)
                values = [1.0 - along_x - along_y, along_x, along_y, scale * cosine, scale * sine]
                row = 2 * (9 * row_slot + i)
                lane = 2 * (9 * col_slot + i)
                pair = slice(lane, lane + 2)
                at = T_LANE + LANE_ROWS * col_dir
                for v, value in enumerate(values):
                    whole[member, at + v, pair] = value
                whole[member, at + 5, pair] = 1.0 if row_dir == 0 else 0.0
                whole[member, at + 6 + freq_slot, pair] = 1.0
                whole[member, at + 9 + freq_slot, pair] = cosine * cosine
                at = T_ROW + 96 * row_dir + row
                for v, value in enumerate(values):
                    whole[member, at : at + 2, v] = value
                whole[member, at : at + 2, 5] = 1.0 if col_dir == 0 else 0.0
                near = lane + 1 if col_dir == 0 else lane
                whole[member, T_PICK + 96 * row_dir + row + row_dir, near] = 1.0
                at = T_SUM + 64 * row_dir
                for side in (0, 1):
                    out = side if row_dir == 0 else 6 + side
                    whole[member, at + 16 * freq_slot + out, row + side] = 1.0
                    whole[member, at + 16 * freq_slot + 8 + out, row + side] = cosine * cosine
                    whole[member, at + 48 + out, row + side] = 1.0
    return whole.astype(np.float32)


def power(base, exponent):
    result = jnp.float32(1.0)
    for bit in range(6):
        odd = (exponent // (2**bit)) % 2
        result = result * jnp.where(odd == 1, jnp.float32(base ** (2**bit)), jnp.float32(1.0))
    return result


def from_above(cells, above=None):
    turned = pltpu.roll(cells, 1, 1)
    if above is None:
        top = jnp.zeros((1, 8, 128), jnp.float32)
    else:
        top = pltpu.roll(above, 1, 0)[None]
    before = jnp.concatenate([top, turned[:-1]], axis=0)
    sub = lax.broadcasted_iota(jnp.int32, cells.shape, 1)
    return jnp.where(sub == 0, before, turned)


def from_below(cells, below=None):
    turned = pltpu.roll(cells, 7, 1)
    if below is None:
        bottom = jnp.zeros((1, 8, 128), jnp.float32)
    else:
        bottom = pltpu.roll(below, 7, 0)[None]
    after = jnp.concatenate([turned[1:], bottom], axis=0)
    sub = lax.broadcasted_iota(jnp.int32, cells.shape, 1)
    return jnp.where(sub == 7, after, turned)


def lanes(cells, shift):
    return pltpu.roll(cells, shift % 128, cells.ndim - 1)


def lane_index(shape):
    return lax.broadcasted_iota(jnp.int32, shape, len(shape) - 1)


def from_left(cells):
    return jnp.where(lane_index(cells.shape) == 0, 0.0, lanes(cells, 1))


def from_right(cells):
    return jnp.where(lane_index(cells.shape) == 127, 0.0, lanes(cells, 127))


def step_kernel(
    spec_ref, land_ref, ice_ref, wu_ref, wv_ref, depth_ref, table_ref,
    x, factor_ref, level_ref,
    land, ice, wu, wv, depth, tab, wet,
    row_send, row_recv, col_send, col_recv, corner_recv,
    acc, row_fix, col_fix,
    rs_send, rs_recv, ag_send, ag_recv,
    edge_send, edge_recv, strip_send, strip_recv, tip_recv,
    load_sem, small_sem,
    halo_ssem, halo_rsem, rs_ssem, rs_rsem, ag_ssem, ag_rsem, rim_ssem, rim_rsem,
):
    comp = lax.axis_index("comp")
    slab = lax.axis_index("slab")
    sect = lax.axis_index("sect")
    first = comp % 4

    def place(down, right):
        return {"slab": (slab + down + SIDE) % SIDE, "sect": (sect + right + SIDE) % SIDE}

    around = [place(a, b) for a in (-1, 0, 1) for b in (-1, 0, 1) if (a, b) != (0, 0)]
    others = [{"comp": (comp + shift) % COMPS} for shift in FAR_FIRST]
    barrier = pltpu.get_barrier_semaphore()
    for peer in others + around:
        pl.semaphore_signal(barrier, 1, device_id=peer, device_id_type=MESH)

    small = [
        pltpu.make_async_copy(src, dst, small_sem.at[n])
        for n, (src, dst) in enumerate(
            [(land_ref, land), (ice_ref, ice), (wu_ref, wu), (wv_ref, wv), (depth_ref, depth),
             (table_ref.at[comp], tab)]
        )
    ]
    for copy in small:
        copy.start()

    def load(group):
        rows = pl.ds(9 * group, 9)
        return pltpu.make_async_copy(spec_ref.at[rows], x.at[rows], load_sem.at[group])

    def group_of(quad, turn):
        return (quad - first + 4) % 4 + 4 * turn

    order = [(0, 0), (1, 0), (0, 1), (1, 1), (2, 0), (3, 0), (2, 1), (3, 1)]
    for quad, turn in order:
        load(group_of(quad, turn)).start()
    load(8).start()

    lane = lane_index((8, 128))
    lane_pair = lane // 2
    sub = lax.broadcasted_iota(jnp.int32, (8, 128), 0)
    even_lane = lane % 2 == 0
    even_sub = sub % 2 == 0

    row_send[0, 9:12] = jnp.zeros((3, 8, 128), jnp.float32)
    row_send[1, 9:12] = jnp.zeros((3, 8, 128), jnp.float32)
    acc[...] = jnp.zeros_like(acc)
    for copy in small:
        copy.wait()
    wet[...] = (1 - land[...]).astype(jnp.float32)
    open_sea = (1 - ice[...]).astype(jnp.float32)
    wu[...] = wu[...] * open_sea
    wv[...] = wv[...] * open_sea

    def pack(quad, turn, packed):
        group = group_of(quad, turn)
        row_slot = ROW_SLOT[quad] + turn if turn < 2 else EXTRA_SLOT
        col_slot = COL_SLOT[quad] + turn if turn < 2 else EXTRA_SLOT
        load(group).wait()
        for i in range(9):
            cells = x[9 * group + i]
            row = 2 * (9 * row_slot + i)
            to = (ROW_DIR[quad], row // 8, pl.ds(row % 8, 2))
            if ROW_DIR[quad] == 0:
                row_send[to] = cells[7, 6:8] * wet[7, 6:8, :]
            else:
                row_send[to] = cells[0, 0:2] * wet[0, 0:2, :]
            pair = 9 * col_slot + i
            shift = 2 * pair + 2 if COL_DIR[quad] == 0 else 2 * pair
            packed = jnp.where(lane_pair == pair, lanes(cells, shift), packed)
        return packed

    for way in (0, 1):
        packed = jnp.zeros((8, 8, 128), jnp.float32)
        for quad, turn in order:
            if COL_DIR[quad] == way:
                packed = pack(quad, turn, packed)
        col_send[way] = packed
    for quad in range(4):
        @pl.when(first == quad)
        def _(quad=quad):
            col_send[COL_DIR[quad]] = pack(quad, 2, col_send[COL_DIR[quad]])

    wet_now = wet[...]
    for way in (0, 1):
        at = 126 if way == 0 else 0
        one, two = wet_now[:, :, at : at + 1], wet_now[:, :, at + 1 : at + 2]
        pair_wet = jnp.where(even_lane, one, two)
        col_send[way] = jnp.where(lane_pair == 63, pair_wet, col_send[way] * pair_wet)
    row_send[0, 11, 2:4] = wet[7, 6:8, :]
    row_send[1, 11, 2:4] = wet[0, 0:2, :]

    pl.semaphore_wait(barrier, len(around) + len(others))

    def remote(src, dst, ssem, rsem, peer):
        return pltpu.make_async_remote_copy(
            src_ref=src, dst_ref=dst, send_sem=ssem, recv_sem=rsem, device_id=peer, device_id_type=MESH
        )

    halo = [
        remote(col_send.at[0], col_recv.at[0], halo_ssem.at[0], halo_rsem.at[0], place(0, 1)),
        remote(col_send.at[1], col_recv.at[1], halo_ssem.at[1], halo_rsem.at[1], place(0, -1)),
    ]
    for way in (0, 1):
        step = 1 if way == 0 else -1
        halo.append(
            remote(col_send.at[way, 7], corner_recv.at[way, 0], halo_ssem.at[2 + way], halo_rsem.at[2 + way],
                   place(1, step))
        )
        halo.append(
            remote(col_send.at[way, 0], corner_recv.at[way, 1], halo_ssem.at[4 + way], halo_rsem.at[4 + way],
                   place(-1, step))
        )
    halo.append(remote(row_send.at[0], row_recv.at[0], halo_ssem.at[6], halo_rsem.at[6], place(1, 0)))
    halo.append(remote(row_send.at[1], row_recv.at[1], halo_ssem.at[7], halo_rsem.at[7], place(-1, 0)))
    for copy in halo:
        copy.start()

    for quad in range(4):
        upwind_row = from_above if ROW_DIR[quad] == 0 else from_below
        upwind_col = from_left if COL_DIR[quad] == 0 else from_right

        def body(turn, carry, quad=quad, upwind_row=upwind_row, upwind_col=upwind_col):
            group = group_of(quad, turn)
            freq = (9 * comp + group) // 4
            slot = (first + group) // 4
            low = 0.7 * power(1.0 / 1.1, freq)
            scale = math.sqrt(0.5 * 1.1 ** (-(NF - 1))) * power(math.sqrt(1.1), freq)
            total_e = jnp.zeros((8, 8, 128), jnp.float32)
            total_f = jnp.zeros((8, 8, 128), jnp.float32)
            total_c = jnp.zeros((8, 8, 128), jnp.float32)
            for i in range(9):
                cosine, sine = direction(9 * quad + i)
                along_x, along_y = low * abs(cosine), low * abs(sine)
                stay = 1.0 - along_x - along_y
                cells = x[9 * group + i] * wet[...]
                for _ in range(2):
                    cells = wet[...] * (
                        stay * cells + along_x * upwind_row(cells) + along_y * upwind_col(cells)
                    )
                push = jnp.maximum((scale * cosine) * wu[...] + (scale * sine) * wv[...], 0.0)
                grown = cells + cells * (push * push)
                x[9 * group + i] = grown
                total_e += cells
                total_f += grown
                total_c += (cosine * cosine) * grown
            acc[6] += total_e
            acc[2 * slot] += total_f
            acc[2 * slot + 1] += total_c
            return carry

        lax.fori_loop(0, 2 + (first == quad).astype(jnp.int32), body, 0)

    for copy in halo:
        copy.wait_recv()

    has = {
        "up": (slab > 0).astype(jnp.float32), "down": (slab < SIDE - 1).astype(jnp.float32),
        "left": (sect > 0).astype(jnp.float32), "right": (sect < SIDE - 1).astype(jnp.float32),
    }
    col_terms = []
    for way in (0, 1):
        lane_row = lambda n: tab[T_LANE + LANE_ROWS * way + n : T_LANE + LANE_ROWS * way + n + 1, :][None]
        stay, along_x, along_y, push_u, push_v, is_up = [lane_row(n) for n in range(6)]
        side = has["left"] if way == 0 else has["right"]
        got = col_recv[way] * side
        above = corner_recv[way, 0] * (side * has["up"])
        below = corner_recv[way, 1] * (side * has["down"])
        turn = 127 if way == 0 else 1
        near, near_above, near_below = lanes(got, turn), lanes(above, turn), lanes(below, turn)
        halo_wet = got[:, :, 127:128] if way == 0 else got[:, :, 126:127]
        at_near, at_far = (0, 1) if way == 0 else (127, 126)
        wet_near, wet_far = wet_now[:, :, at_near : at_near + 1], wet_now[:, :, at_far : at_far + 1]
        up_now = jnp.where(is_up > 0.5, from_above(near, near_above), from_below(near, near_below))
        outside = halo_wet * (stay * near + along_x * up_now + along_y * got)
        one = wet_near * (along_y * near)
        up_one = jnp.where(is_up > 0.5, from_above(one), from_below(one))
        two = wet_near * (stay * one + along_x * up_one + along_y * outside)
        far = lanes(wet_far * (along_y * one), 1 if way == 0 else 127)
        fix = jnp.where(even_lane, two, far) if way == 0 else jnp.where(even_lane, far, two)
        low_at = 0 if way == 0 else 126
        wind = [
            jnp.where(even_lane, w[:, :, low_at : low_at + 1], w[:, :, low_at + 1 : low_at + 2])
            for w in (wu, wv)
        ]
        push = jnp.maximum(push_u * wind[0] + push_v * wind[1], 0.0)
        fix_grown = fix + fix * (push * push)
        col_fix[way] = fix_grown
        terms = []
        for slot in range(3):
            terms += [fix_grown * lane_row(6 + slot), fix_grown * lane_row(9 + slot)]
        terms.append(fix)
        stacked = jnp.concatenate([term.reshape(64, 128) for term in terms], axis=0)
        k_index = lax.broadcasted_iota(jnp.int32, (128, 128), 0)
        to_lane = lane_index((128, 128))
        pick = ((to_lane == k_index % 2 + low_at) & (k_index < 90)).astype(jnp.float32)
        col_terms.append(jnp.dot(stacked, pick, precision=HIGHEST, preferred_element_type=jnp.float32))
    col_sum = (col_terms[0] + col_terms[1]).reshape(7, 8, 8, 128)
    acc[...] += col_sum

    for way in (0, 1):
        at = T_ROW + 96 * way
        spread = lambda n: jnp.broadcast_to(tab[at : at + 96, n : n + 1], (96, 128)).reshape(12, 8, 128)
        stay, along_x, along_y, push_u, push_v, is_left = [spread(n) for n in range(6)]
        side = has["up"] if way == 0 else has["down"]
        got = row_recv[way] * side
        near = pltpu.roll(got, 7 if way == 0 else 1, 1)
        edge = 7 if way == 0 else 0
        left_corner = corner_recv[0, way, edge : edge + 1, :] * (side * has["left"])
        right_corner = corner_recv[1, way, edge : edge + 1, :] * (side * has["right"])
        choose = tab[T_PICK + 96 * way : T_PICK + 96 * way + 96, :].reshape(12, 8, 128)
        corner = jnp.sum(
            choose * jnp.where(is_left > 0.5, left_corner[None], right_corner[None]), axis=2, keepdims=True
        )
        halo_wet = got[11, 3:4, :] if way == 0 else got[11, 2:3, :]
        tile, near_row, far_row = (0, 0, 1) if way == 0 else (7, 7, 6)
        wet_near, wet_far = wet[tile, near_row : near_row + 1, :], wet[tile, far_row : far_row + 1, :]
        lane3 = lane_index((12, 8, 128))
        beside = jnp.where(
            is_left > 0.5,
            jnp.where(lane3 == 0, corner, lanes(near, 1)),
            jnp.where(lane3 == 127, corner, lanes(near, 127)),
        )
        outside = halo_wet * (stay * near + along_x * got + along_y * beside)
        one = wet_near * (along_x * near)
        beside_one = jnp.where(is_left > 0.5, from_left(one), from_right(one))
        two = wet_near * (stay * one + along_y * beside_one + along_x * outside)
        far = pltpu.roll(wet_far * (along_x * one), 1 if way == 0 else 7, 1)
        fix = jnp.where(even_sub, two, far) if way == 0 else jnp.where(even_sub, far, two)
        low_at = 0 if way == 0 else 6
        wind = [
            jnp.where(even_sub, w[tile, low_at : low_at + 1, :], w[tile, low_at + 1 : low_at + 2, :])
            for w in (wu, wv)
        ]
        push = jnp.maximum(push_u * wind[0] + push_v * wind[1], 0.0)
        fix_grown = fix + fix * (push * push)
        row_fix[way] = fix_grown
        at = T_SUM + 64 * way
        weights = tab[at : at + 48, 0:96]
        sum_grown = jnp.dot(weights, fix_grown.reshape(96, 128), precision=HIGHEST,
                            preferred_element_type=jnp.float32)
        sum_moved = jnp.dot(tab[at + 48 : at + 56, 0:96], fix.reshape(96, 128), precision=HIGHEST,
                            preferred_element_type=jnp.float32)
        for v in range(6):
            acc[v, tile] += sum_grown[8 * v : 8 * v + 8]
        acc[6, tile] += sum_moved

    low_half = sub < 4
    for slot in range(4):
        if slot < 3:
            one, two = acc[2 * slot], acc[2 * slot + 1]
            even_tile = jnp.where(low_half, one, pltpu.roll(two, 4, 1))
            odd_tile = jnp.where(low_half, pltpu.roll(one, 4, 1), two)
        else:
            even_tile, odd_tile = acc[6], pltpu.roll(acc[6], 4, 1)
        for tile in range(8):
            rs_send[2 * tile, 8 * slot : 8 * slot + 8] = even_tile[tile]
            rs_send[2 * tile + 1, 8 * slot : 8 * slot + 8] = odd_tile[tile]
    rs = []
    for shift in FAR_FIRST:
        peer = (comp + shift) % COMPS
        rs.append(
            remote(rs_send.at[peer, pl.ds(0, 28)], rs_recv.at[comp, pl.ds(0, 28)], rs_ssem.at[shift],
                   rs_rsem.at[shift], {"comp": peer})
        )
    for copy in rs:
        copy.start()
    rs_recv[comp] = rs_send[comp]

    def amend(quad, turn):
        group = group_of(quad, turn)
        row_slot = ROW_SLOT[quad] + turn if turn < 2 else EXTRA_SLOT
        col_slot = COL_SLOT[quad] + turn if turn < 2 else EXTRA_SLOT
        way = COL_DIR[quad]
        fixes = col_fix[way]
        inside = lane < 2 if way == 0 else lane >= 126
        for i in range(9):
            at = 9 * group + i
            pair = 2 * (9 * col_slot + i)
            moved = lanes(fixes, -pair if way == 0 else 126 - pair)
            x[at] = x[at] + jnp.where(inside, moved, 0.0)
            row = 2 * (9 * row_slot + i)
            rows = row_fix[ROW_DIR[quad], row // 8, row % 8 : row % 8 + 2, :]
            if ROW_DIR[quad] == 0:
                x[at, 0, 0:2, :] += rows
            else:
                x[at, 7, 6:8, :] += rows

    for quad in range(4):
        for turn in (0, 1):
            amend(quad, turn)
        @pl.when(first == quad)
        def _(quad=quad):
            amend(quad, 2)

    for copy in rs:
        copy.wait_recv()

    energy = rs_recv[0, 24:28, :]
    for source in range(1, COMPS):
        energy = energy + rs_recv[source, 24:28, :]
    energy = energy / K
    energy = jnp.concatenate([energy, energy], axis=0)
    square = energy * energy
    plain = jnp.zeros((8, 128), jnp.float32)
    shoaled = jnp.zeros((8, 128), jnp.float32)
    for freq in range(NF):
        part = None
        for source in range(COMPS):
            slot = freq - 9 * source // 4
            if 0 <= slot < 3:
                tile = rs_recv[source, 8 * slot : 8 * slot + 8, :]
                part = tile if part is None else part + tile
        part = part / (1.0 + (2.0 * 1.1 ** (freq - (NF - 1))) * square)
        plain = plain + part
        shoaled = shoaled + (0.5 + 0.5 * freq / (NF - 1)) * part
    turned = pltpu.roll(shoaled, 4, 0)
    final = plain / K
    stress_x = (turned + shoaled - 0.5 * plain) / K
    stress_y = (2.0 * shoaled - turned - 0.5 * plain) / K
    ag_send[0] = jnp.where(low_half, stress_x, pltpu.roll(stress_y, 4, 0))
    ag_send[1] = jnp.where(low_half, energy, pltpu.roll(final, 4, 0))
    ag = [
        [
            remote(ag_send.at[n], ag_recv.at[n, comp], ag_ssem.at[n, shift], ag_rsem.at[n, shift],
                   {"comp": (comp + shift) % COMPS})
            for shift in FAR_FIRST
        ]
        for n in (0, 1)
    ]
    for copy in ag[0] + ag[1]:
        copy.start()
    ag_recv[0, comp] = ag_send[0]
    ag_recv[1, comp] = ag_send[1]
    for copy in ag[0]:
        copy.wait_recv()

    def whole(n):
        gathered = ag_recv[n].reshape(8, 2, 8, 128)
        one, two = gathered[:, 0], gathered[:, 1]
        return (
            jnp.where(low_half, one, pltpu.roll(two, 4, 1)),
            jnp.where(low_half, pltpu.roll(one, 4, 1), two),
        )

    stress_x, stress_y = whole(0)

    edge_send[0] = stress_x
    edge_send[1] = stress_y
    strip_send[...] = jnp.where(
        (lane < 8) | (lane >= 120), stress_x, jnp.where(lane < 64, lanes(stress_y, 8), lanes(stress_y, 120))
    )
    rim = [
        remote(strip_send, strip_recv.at[0], rim_ssem.at[0], rim_rsem.at[0], place(0, 1)),
        remote(strip_send, strip_recv.at[1], rim_ssem.at[1], rim_rsem.at[1], place(0, -1)),
        remote(edge_send.at[:, 7], edge_recv.at[0], rim_ssem.at[2], rim_rsem.at[2], place(1, 0)),
        remote(edge_send.at[:, 0], edge_recv.at[1], rim_ssem.at[3], rim_rsem.at[3], place(-1, 0)),
        remote(strip_send.at[7], tip_recv.at[0, 0], rim_ssem.at[4], rim_rsem.at[4], place(1, 1)),
        remote(strip_send.at[7], tip_recv.at[1, 0], rim_ssem.at[5], rim_rsem.at[5], place(1, -1)),
        remote(strip_send.at[0], tip_recv.at[0, 1], rim_ssem.at[6], rim_rsem.at[6], place(-1, 1)),
        remote(strip_send.at[0], tip_recv.at[1, 1], rim_ssem.at[7], rim_rsem.at[7], place(-1, -1)),
    ]
    for copy in rim:
        copy.start()
    for copy in ag[1]:
        copy.wait_recv()
    energy, final = whole(1)
    start = (9 * comp) // 4
    high = 1.1 ** (-(NF - 1)) * power(1.1, start)
    rates = [
        1.0 / (1.0 + (2.0 * 1.1**slot * high) * (energy * energy)) for slot in range(3)
    ]
    for copy in rim:
        copy.wait_recv()

    big_lane = lane_index((80, 128))
    big_row = lax.broadcasted_iota(jnp.int32, (80, 128), 0)
    first_row = jnp.where(slab > 0, 0, 8)
    last_row = jnp.where(slab < SIDE - 1, 80, 72)
    in_rows = (big_row >= first_row) & (big_row < last_row)
    right_end = jnp.where(sect < SIDE - 1, 8, 0)
    left_start = jnp.where(sect > 0, 120, 128)
    in_strip = in_rows & ((big_lane < right_end) | (big_lane >= left_start))

    def middle(n, cells):
        return jnp.where(
            in_rows,
            jnp.concatenate([edge_recv[0, n], cells.reshape(64, 128), edge_recv[1, n]], axis=0),
            0.0,
        )

    left_strip = jnp.concatenate([tip_recv[0, 0], strip_recv[0].reshape(64, 128), tip_recv[0, 1]], axis=0)
    right_strip = jnp.concatenate([tip_recv[1, 0], strip_recv[1].reshape(64, 128), tip_recv[1, 1]], axis=0)
    xx = middle(0, stress_x)
    yy = middle(1, stress_y)
    xx_strip = jnp.where(in_strip, jnp.where(big_lane < 64, right_strip, left_strip), 0.0)
    yy_strip = jnp.where(
        in_strip, jnp.where(big_lane < 64, lanes(right_strip, 120), lanes(left_strip, 8)), 0.0
    )

    def beside(center, strip):
        center_up, strip_up = lanes(center, 127), lanes(strip, 127)
        center_down, strip_down = lanes(center, 1), lanes(strip, 1)
        last, head = big_lane == 127, big_lane == 0
        return (
            jnp.where(last, strip_up, center_up) + jnp.where(head, strip_down, center_down),
            jnp.where(last, center_up, strip_up) + jnp.where(head, center_down, strip_down),
        )

    def above_below(cells):
        return pltpu.roll(cells, 1, 0) + pltpu.roll(cells, 79, 0)

    yy_sides = beside(yy, yy_strip)
    source = jnp.where(in_rows, -((above_below(xx) - 2.0 * xx) + (yy_sides[0] - 2.0 * yy)), 0.0)
    source_strip = jnp.where(
        in_strip, -((above_below(xx_strip) - 2.0 * xx_strip) + (yy_sides[1] - 2.0 * yy_strip)), 0.0
    )
    surge, surge_strip = source / 4.5, source_strip / 4.5
    for _ in range(JAC):
        sides = beside(surge, surge_strip)
        surge, surge_strip = (
            jnp.where(in_rows, (source + above_below(surge) + sides[0]) / 4.5, 0.0),
            jnp.where(in_strip, (source_strip + above_below(surge_strip) + sides[1]) / 4.5, 0.0),
        )
    surge = surge[8:72].reshape(8, 8, 128)
    reach = depth[...] + surge
    damping = 1.0 / (1.0 + 4.0 * final / (reach * reach + 1.0))
    for slot in range(3):
        factor_ref[slot] = rates[slot] * damping
    level_ref[...] = surge

    for copy in halo + rs + ag[0] + ag[1] + rim:
        copy.wait_send()


def damp_kernel(grown_ref, factor_ref, level_ref, out_ref, level_out, x, out_sem, small_sem):
    first = lax.axis_index("comp") % 4

    def store(group):
        rows = pl.ds(9 * group, 9)
        return pltpu.make_async_copy(x.at[rows], out_ref.at[rows], out_sem.at[group])

    surge = pltpu.make_async_copy(level_ref, level_out, small_sem.at[0])
    surge.start()
    for group in range(GROUPS):
        factor = factor_ref[(first + group) // 4]
        for i in range(9):
            x[9 * group + i] = grown_ref[9 * group + i] * factor
        store(group).start()
    surge.wait()
    for group in range(GROUPS):
        store(group).wait()


def local(spectrum, land_mask, ice_mask, wind_u, wind_v, depth):
    f32 = jnp.float32
    block = (8, 8, 128)
    anywhere = pl.BlockSpec(memory_space=pl.ANY)
    vmem = pl.BlockSpec(memory_space=pltpu.VMEM)
    dma = pltpu.SemaphoreType.DMA
    grown, factor, level = pl.pallas_call(
        step_kernel,
        out_shape=(
            pltpu.VMEM((LOCAL, *block), f32),
            pltpu.VMEM((3, *block), f32),
            pltpu.VMEM(block, f32),
        ),
        in_specs=[anywhere] * 7,
        out_specs=(vmem, vmem, vmem),
        scratch_shapes=[
            pltpu.VMEM(block, jnp.int32),
            pltpu.VMEM(block, jnp.int32),
            pltpu.VMEM(block, f32),
            pltpu.VMEM(block, f32),
            pltpu.VMEM(block, f32),
            pltpu.VMEM((T_END, 128), f32),
            pltpu.VMEM(block, f32),
            pltpu.VMEM((2, 12, 8, 128), f32),
            pltpu.VMEM((2, 12, 8, 128), f32),
            pltpu.VMEM((2, *block), f32),
            pltpu.VMEM((2, *block), f32),
            pltpu.VMEM((2, 2, 8, 128), f32),
            pltpu.VMEM((7, *block), f32),
            pltpu.VMEM((2, 12, 8, 128), f32),
            pltpu.VMEM((2, *block), f32),
            pltpu.VMEM((COMPS, 32, 128), f32),
            pltpu.VMEM((COMPS, 32, 128), f32),
            pltpu.VMEM((2, 8, 128), f32),
            pltpu.VMEM((2, COMPS, 8, 128), f32),
            pltpu.VMEM((2, *block), f32),
            pltpu.VMEM((2, 2, 8, 128), f32),
            pltpu.VMEM(block, f32),
            pltpu.VMEM((2, *block), f32),
            pltpu.VMEM((2, 2, 8, 128), f32),
            dma((GROUPS,)),
            dma((6,)),
            dma((8,)),
            dma((8,)),
            dma((COMPS,)),
            dma((COMPS,)),
            dma((2, COMPS)),
            dma((2, COMPS)),
            dma((8,)),
            dma((8,)),
        ],
        compiler_params=pltpu.CompilerParams(
            collective_id=0, has_side_effects=True, vmem_limit_bytes=24 * 1024 * 1024
        ),
        name="wave_step",
    )(
        *[
            pltpu.with_memory_space_constraint(operand, pltpu.HBM)
            for operand in (
                spectrum.reshape(LOCAL, *block),
                land_mask.reshape(block),
                ice_mask.reshape(block),
                wind_u.reshape(block),
                wind_v.reshape(block),
                depth.reshape(block),
                jnp.asarray(table()),
            )
        ]
    )
    damped, level = pl.pallas_call(
        damp_kernel,
        out_shape=(jax.ShapeDtypeStruct((LOCAL, *block), f32), jax.ShapeDtypeStruct(block, f32)),
        in_specs=[vmem] * 3,
        out_specs=(anywhere, anywhere),
        scratch_shapes=[
            pltpu.VMEM((LOCAL, *block), f32),
            dma((GROUPS,)),
            dma((1,)),
        ],
        compiler_params=pltpu.CompilerParams(vmem_limit_bytes=24 * 1024 * 1024),
        name="damp",
    )(*[pltpu.with_memory_space_constraint(operand, pltpu.VMEM) for operand in (grown, factor, level)])
    return damped.reshape(spectrum.shape), level.reshape(depth.shape)


def solution(mesh):
    cells = P("slab", "sect")
    spectra = P("comp", "slab", "sect")
    return jax.shard_map(
        local,
        mesh=mesh,
        in_specs=(spectra, cells, cells, cells, cells, cells),
        out_specs=(spectra, cells),
        check_vma=False,
    )
```

```python
import functools
import math

import jax
import jax.numpy as jnp
import numpy as np
from jax import lax
from jax.experimental import pallas as pl
from jax.experimental.pallas import tpu as pltpu
from jax.sharding import PartitionSpec as P

ND = 36
NF = 36
K = ND * NF
JAC = 4
LOCAL = 81
GROUPS = 9
COMPS = 16
SIDE = 4
AFTER = 13
FAR_FIRST = tuple(
    (chips, other) for far in (4, 3, 2, 1) for chips in ((far, -far) if far < 4 else (far,)) for other in (0, 1)
) + ((0, 1),)
MESH = pl.DeviceIdType.MESH
HIGHEST = lax.Precision.HIGHEST

ROW_DIR = (0, 1, 1, 0)
COL_DIR = (0, 0, 1, 1)
ROW_SLOT = (0, 0, 2, 2)
COL_SLOT = (0, 2, 0, 2)
EXTRA_SLOT = 4

LANE_ROWS = 8
T_LANE = 0
T_ROW = T_LANE + 2 * LANE_ROWS
T_PICK = T_ROW + 2 * 96
T_SUM = T_PICK + 2 * 96
T_COL = T_SUM + 2 * 64
T_END = T_COL + 4 * 32


def direction(index):
    heading = 2.0 * math.pi * index / ND
    return math.cos(heading), math.sin(heading)


@functools.cache
def table():
    whole = np.zeros((COMPS, T_END, 128), np.float64)
    for member in range(COMPS):
        first = member % 4
        start = 9 * member // 4
        for group in range(GROUPS):
            quad = (first + group) % 4
            turn = group // 4
            freq_slot = (first + group) // 4
            freq = start + freq_slot
            row_dir, col_dir = ROW_DIR[quad], COL_DIR[quad]
            row_slot = ROW_SLOT[quad] + turn if turn < 2 else EXTRA_SLOT
            col_slot = COL_SLOT[quad] + turn if turn < 2 else EXTRA_SLOT
            low = 1.1 ** (-freq)
            scale = math.sqrt(0.5 * 1.1 ** (freq - (NF - 1)))
            for i in range(9):
                cosine, sine = direction(9 * quad + i)
                along_x, along_y = 0.7 * low * abs(cosine), 0.7 * low * abs(sine)
                values = [1.0 - along_x - along_y, along_x, along_y, scale * cosine, scale * sine]
                row = 2 * (9 * row_slot + i)
                lane = 2 * (9 * col_slot + i)
                pair = slice(lane, lane + 2)
                at = T_LANE + LANE_ROWS * col_dir
                for v, value in enumerate(values):
                    whole[member, at + v, pair] = value
                whole[member, at + 5, pair] = 1.0 if row_dir == 0 else 0.0
                for side in (0, 1):
                    out = 2 + side if col_dir == 0 else side
                    at = T_COL + 64 * col_dir
                    whole[member, at + 4 * freq_slot + out, lane + side] = 1.0
                    whole[member, at + 16 + 4 * freq_slot + out, lane + side] = cosine * cosine
                    whole[member, at + 32 + 12 + out, lane + side] = 1.0
                at = T_ROW + 96 * row_dir + row
                for v, value in enumerate(values):
                    whole[member, at : at + 2, v] = value
                whole[member, at : at + 2, 5] = 1.0 if col_dir == 0 else 0.0
                near = lane + 1 if col_dir == 0 else lane
                whole[member, T_PICK + 96 * row_dir + row + row_dir, near] = 1.0
                at = T_SUM + 64 * row_dir
                for side in (0, 1):
                    out = side if row_dir == 0 else 6 + side
                    whole[member, at + 16 * freq_slot + out, row + side] = 1.0
                    whole[member, at + 16 * freq_slot + 8 + out, row + side] = cosine * cosine
                    whole[member, at + 48 + out, row + side] = 1.0
    return whole.astype(np.float32)


def power(base, exponent):
    result = jnp.float32(1.0)
    for bit in range(6):
        odd = (exponent // (2**bit)) % 2
        result = result * jnp.where(odd == 1, jnp.float32(base ** (2**bit)), jnp.float32(1.0))
    return result


def from_above(cells, above=None):
    turned = pltpu.roll(cells, 1, 1)
    if above is None:
        top = jnp.zeros((1, 8, 128), jnp.float32)
    else:
        top = pltpu.roll(above, 1, 0)[None]
    before = jnp.concatenate([top, turned[:-1]], axis=0)
    sub = lax.broadcasted_iota(jnp.int32, cells.shape, 1)
    return jnp.where(sub == 0, before, turned)


def from_below(cells, below=None):
    turned = pltpu.roll(cells, 7, 1)
    if below is None:
        bottom = jnp.zeros((1, 8, 128), jnp.float32)
    else:
        bottom = pltpu.roll(below, 7, 0)[None]
    after = jnp.concatenate([turned[1:], bottom], axis=0)
    sub = lax.broadcasted_iota(jnp.int32, cells.shape, 1)
    return jnp.where(sub == 7, after, turned)


def lanes(cells, shift):
    return pltpu.roll(cells, shift % 128, cells.ndim - 1)


def lane_index(shape):
    return lax.broadcasted_iota(jnp.int32, shape, len(shape) - 1)


def from_left(cells):
    return jnp.where(lane_index(cells.shape) == 0, 0.0, lanes(cells, 1))


def from_right(cells):
    return jnp.where(lane_index(cells.shape) == 127, 0.0, lanes(cells, 127))


def step_kernel(
    spec_ref, land_ref, ice_ref, wu_ref, wv_ref, depth_ref, table_ref,
    x, factor_ref, level_ref,
    land, ice, wu, wv, depth, tab, wet,
    row_send, row_recv, col_send, col_recv, corner_recv,
    acc, row_fix, col_fix, row_coef, row_gain, col_gain,
    rs_send, rs_recv, ag_send, ag_recv,
    edge_send, edge_recv, strip_send, strip_recv, tip_recv,
    load_sem, small_sem,
    halo_ssem, halo_rsem, rs_ssem, rs_rsem, ag_ssem, ag_rsem, rim_ssem, rim_rsem,
):
    comp = lax.axis_index("comp")
    slab = lax.axis_index("slab")
    sect = lax.axis_index("sect")
    first = comp % 4

    def place(down, right):
        return {"slab": (slab + down + SIDE) % SIDE, "sect": (sect + right + SIDE) % SIDE}

    around = [place(a, b) for a in (-1, 0, 1) for b in (-1, 0, 1) if (a, b) != (0, 0)]
    core = comp % 2

    def along(chips, other):
        return (comp - core + 2 * chips + COMPS) % COMPS + (core + other) % 2

    far_first = [along(*peer) for peer in FAR_FIRST]
    others = [{"comp": peer} for peer in far_first]
    barrier = pltpu.get_barrier_semaphore()
    for peer in around + others:
        pl.semaphore_signal(barrier, 1, device_id=peer, device_id_type=MESH)

    small = [
        pltpu.make_async_copy(src, dst, small_sem.at[n])
        for n, (src, dst) in enumerate(
            [(land_ref, land), (ice_ref, ice), (wu_ref, wu), (wv_ref, wv), (depth_ref, depth),
             (table_ref.at[comp], tab)]
        )
    ]
    for copy in small:
        copy.start()

    def load(group):
        rows = pl.ds(9 * group, 9)
        return pltpu.make_async_copy(spec_ref.at[rows], x.at[rows], load_sem.at[group])

    def group_of(quad, turn):
        return (quad - first + 4) % 4 + 4 * turn

    order = [(0, 0), (1, 0), (0, 1), (1, 1), (2, 0), (3, 0), (2, 1), (3, 1)]
    for quad, turn in order:
        load(group_of(quad, turn)).start()
    load(8).start()

    lane = lane_index((8, 128))
    lane_pair = lane // 2
    sub = lax.broadcasted_iota(jnp.int32, (8, 128), 0)
    even_lane = lane % 2 == 0
    even_sub = sub % 2 == 0

    row_send[0, 9:12] = jnp.zeros((3, 8, 128), jnp.float32)
    row_send[1, 9:12] = jnp.zeros((3, 8, 128), jnp.float32)
    acc[...] = jnp.zeros_like(acc)
    for copy in small:
        copy.wait()
    wet[...] = (1 - land[...]).astype(jnp.float32)
    open_sea = (1 - ice[...]).astype(jnp.float32)
    wu[...] = wu[...] * open_sea
    wv[...] = wv[...] * open_sea

    def pack(quad, turn, packed):
        group = group_of(quad, turn)
        row_slot = ROW_SLOT[quad] + turn if turn < 2 else EXTRA_SLOT
        col_slot = COL_SLOT[quad] + turn if turn < 2 else EXTRA_SLOT
        load(group).wait()
        for i in range(9):
            cells = x[9 * group + i]
            row = 2 * (9 * row_slot + i)
            to = (ROW_DIR[quad], row // 8, pl.ds(row % 8, 2))
            if ROW_DIR[quad] == 0:
                row_send[to] = cells[7, 6:8] * wet[7, 6:8, :]
            else:
                row_send[to] = cells[0, 0:2] * wet[0, 0:2, :]
            pair = 9 * col_slot + i
            shift = 2 * pair + 2 if COL_DIR[quad] == 0 else 2 * pair
            packed = jnp.where(lane_pair == pair, lanes(cells, shift), packed)
        return packed

    for way in (0, 1):
        packed = jnp.zeros((8, 8, 128), jnp.float32)
        for quad, turn in order:
            if COL_DIR[quad] == way:
                packed = pack(quad, turn, packed)
        col_send[way] = packed
    for quad in range(4):
        @pl.when(first == quad)
        def _(quad=quad):
            col_send[COL_DIR[quad]] = pack(quad, 2, col_send[COL_DIR[quad]])

    wet_now = wet[...]
    for way in (0, 1):
        at = 126 if way == 0 else 0
        one, two = wet_now[:, :, at : at + 1], wet_now[:, :, at + 1 : at + 2]
        pair_wet = jnp.where(even_lane, one, two)
        col_send[way] = jnp.where(lane_pair == 63, pair_wet, col_send[way] * pair_wet)
    row_send[0, 11, 2:4] = wet[7, 6:8, :]
    row_send[1, 11, 2:4] = wet[0, 0:2, :]

    pl.semaphore_wait(barrier, len(around) + len(others))

    def remote(src, dst, ssem, rsem, peer):
        return pltpu.make_async_remote_copy(
            src_ref=src, dst_ref=dst, send_sem=ssem, recv_sem=rsem, device_id=peer, device_id_type=MESH
        )

    halo = [
        remote(col_send.at[0], col_recv.at[0], halo_ssem.at[0], halo_rsem.at[0], place(0, 1)),
        remote(col_send.at[1], col_recv.at[1], halo_ssem.at[1], halo_rsem.at[1], place(0, -1)),
    ]
    for way in (0, 1):
        step = 1 if way == 0 else -1
        halo.append(
            remote(col_send.at[way, 7], corner_recv.at[way, 0], halo_ssem.at[2 + way], halo_rsem.at[2 + way],
                   place(1, step))
        )
        halo.append(
            remote(col_send.at[way, 0], corner_recv.at[way, 1], halo_ssem.at[4 + way], halo_rsem.at[4 + way],
                   place(-1, step))
        )
    halo.append(remote(row_send.at[0], row_recv.at[0], halo_ssem.at[6], halo_rsem.at[6], place(1, 0)))
    halo.append(remote(row_send.at[1], row_recv.at[1], halo_ssem.at[7], halo_rsem.at[7], place(-1, 0)))
    for copy in halo:
        copy.start()

    for quad in range(4):
        upwind_row = from_above if ROW_DIR[quad] == 0 else from_below
        upwind_col = from_left if COL_DIR[quad] == 0 else from_right

        def body(turn, carry, quad=quad, upwind_row=upwind_row, upwind_col=upwind_col):
            group = group_of(quad, turn)
            freq = (9 * comp + group) // 4
            slot = (first + group) // 4
            low = 0.7 * power(1.0 / 1.1, freq)
            scale = math.sqrt(0.5 * 1.1 ** (-(NF - 1))) * power(math.sqrt(1.1), freq)
            total_e = jnp.zeros((8, 8, 128), jnp.float32)
            total_f = jnp.zeros((8, 8, 128), jnp.float32)
            total_c = jnp.zeros((8, 8, 128), jnp.float32)
            for i in range(9):
                cosine, sine = direction(9 * quad + i)
                along_x, along_y = low * abs(cosine), low * abs(sine)
                stay = 1.0 - along_x - along_y
                cells = x[9 * group + i] * wet[...]
                for _ in range(2):
                    cells = wet[...] * (
                        stay * cells + along_x * upwind_row(cells) + along_y * upwind_col(cells)
                    )
                push = jnp.maximum((scale * cosine) * wu[...] + (scale * sine) * wv[...], 0.0)
                grown = cells + cells * (push * push)
                x[9 * group + i] = grown
                total_e += cells
                total_f += grown
                total_c += (cosine * cosine) * grown
            acc[6] += total_e
            acc[2 * slot] += total_f
            acc[2 * slot + 1] += total_c
            return carry

        lax.fori_loop(0, 2 + (first == quad).astype(jnp.int32), body, 0)

    for way in (0, 1):
        at = T_LANE + LANE_ROWS * way
        low_at = 0 if way == 0 else 126
        wind = [
            jnp.where(even_lane, w[:, :, low_at : low_at + 1], w[:, :, low_at + 1 : low_at + 2])
            for w in (wu, wv)
        ]
        push = jnp.maximum(tab[at + 3 : at + 4, :][None] * wind[0] + tab[at + 4 : at + 5, :][None] * wind[1], 0.0)
        col_gain[way] = 1.0 + push * push
        at = T_ROW + 96 * way
        spread = lambda n: jnp.broadcast_to(tab[at : at + 96, n : n + 1], (96, 128)).reshape(12, 8, 128)
        for n, source in enumerate((0, 1, 2, 5)):
            row_coef[way, n] = spread(source)
        tile, low_at = (0, 0) if way == 0 else (7, 6)
        wind = [
            jnp.where(even_sub, w[tile, low_at : low_at + 1, :], w[tile, low_at + 1 : low_at + 2, :])
            for w in (wu, wv)
        ]
        push = jnp.maximum(spread(3) * wind[0] + spread(4) * wind[1], 0.0)
        row_gain[way] = 1.0 + push * push

    for copy in halo:
        copy.wait_recv()

    has = {
        "up": (slab > 0).astype(jnp.float32), "down": (slab < SIDE - 1).astype(jnp.float32),
        "left": (sect > 0).astype(jnp.float32), "right": (sect < SIDE - 1).astype(jnp.float32),
    }
    col_terms, col_weights = [], []
    for way in (0, 1):
        lane_row = lambda n: tab[T_LANE + LANE_ROWS * way + n : T_LANE + LANE_ROWS * way + n + 1, :][None]
        stay, along_x, along_y, is_up = [lane_row(n) for n in (0, 1, 2, 5)]
        side = has["left"] if way == 0 else has["right"]
        got = col_recv[way] * side
        above = corner_recv[way, 0] * (side * has["up"])
        below = corner_recv[way, 1] * (side * has["down"])
        turn = 127 if way == 0 else 1
        near, near_above, near_below = lanes(got, turn), lanes(above, turn), lanes(below, turn)
        halo_wet = got[:, :, 127:128] if way == 0 else got[:, :, 126:127]
        at_near, at_far = (0, 1) if way == 0 else (127, 126)
        wet_near, wet_far = wet_now[:, :, at_near : at_near + 1], wet_now[:, :, at_far : at_far + 1]
        up_now = jnp.where(is_up > 0.5, from_above(near, near_above), from_below(near, near_below))
        outside = halo_wet * (stay * near + along_x * up_now + along_y * got)
        one = wet_near * (along_y * near)
        up_one = jnp.where(is_up > 0.5, from_above(one), from_below(one))
        two = wet_near * (stay * one + along_x * up_one + along_y * outside)
        far = lanes(wet_far * (along_y * one), 1 if way == 0 else 127)
        fix = jnp.where(even_lane, two, far) if way == 0 else jnp.where(even_lane, far, two)
        fix_grown = fix * col_gain[way]
        col_fix[way] = fix_grown
        col_terms += [fix_grown.reshape(64, 128), fix.reshape(64, 128)]
        at = T_COL + 64 * way
        col_weights += [tab[at : at + 32, :], tab[at + 32 : at + 64, :]]
    col_weights = jnp.concatenate(
        [jnp.concatenate(col_weights, axis=1), jnp.zeros((96, 512), jnp.float32)], axis=0
    )
    col_out = lax.dot_general(
        jnp.concatenate(col_terms, axis=1), col_weights, (((1,), (1,)), ((), ())),
        precision=HIGHEST, preferred_element_type=jnp.float32,
    ).reshape(8, 8, 128)
    rim_lane = (lane < 2) | (lane >= 126)
    for slot in range(3):
        acc[2 * slot] += jnp.where(rim_lane, lanes(col_out, 126 - 4 * slot), 0.0)
        acc[2 * slot + 1] += jnp.where(rim_lane, lanes(col_out, 110 - 4 * slot), 0.0)
    acc[6] += jnp.where(rim_lane, lanes(col_out, 114), 0.0)

    for way in (0, 1):
        stay, along_x, along_y, is_left = [row_coef[way, n] for n in range(4)]
        side = has["up"] if way == 0 else has["down"]
        got = row_recv[way] * side
        near = pltpu.roll(got, 7 if way == 0 else 1, 1)
        edge = 7 if way == 0 else 0
        left_corner = corner_recv[0, way, edge : edge + 1, :] * (side * has["left"])
        right_corner = corner_recv[1, way, edge : edge + 1, :] * (side * has["right"])
        choose = tab[T_PICK + 96 * way : T_PICK + 96 * way + 96, :].reshape(12, 8, 128)
        corner = jnp.sum(
            choose * jnp.where(is_left > 0.5, left_corner[None], right_corner[None]), axis=2, keepdims=True
        )
        halo_wet = got[11, 3:4, :] if way == 0 else got[11, 2:3, :]
        tile, near_row, far_row = (0, 0, 1) if way == 0 else (7, 7, 6)
        wet_near, wet_far = wet[tile, near_row : near_row + 1, :], wet[tile, far_row : far_row + 1, :]
        lane3 = lane_index((12, 8, 128))
        beside = jnp.where(
            is_left > 0.5,
            jnp.where(lane3 == 0, corner, lanes(near, 1)),
            jnp.where(lane3 == 127, corner, lanes(near, 127)),
        )
        outside = halo_wet * (stay * near + along_x * got + along_y * beside)
        one = wet_near * (along_x * near)
        beside_one = jnp.where(is_left > 0.5, from_left(one), from_right(one))
        two = wet_near * (stay * one + along_y * beside_one + along_x * outside)
        far = pltpu.roll(wet_far * (along_x * one), 1 if way == 0 else 7, 1)
        fix = jnp.where(even_sub, two, far) if way == 0 else jnp.where(even_sub, far, two)
        fix_grown = fix * row_gain[way]
        row_fix[way] = fix_grown
        at = T_SUM + 64 * way
        weights = tab[at : at + 48, 0:96]
        sum_grown = jnp.dot(weights, fix_grown.reshape(96, 128), precision=HIGHEST,
                            preferred_element_type=jnp.float32)
        sum_moved = jnp.dot(tab[at + 48 : at + 56, 0:96], fix.reshape(96, 128), precision=HIGHEST,
                            preferred_element_type=jnp.float32)
        for v in range(6):
            acc[v, tile] += sum_grown[8 * v : 8 * v + 8]
        acc[6, tile] += sum_moved

    low_half = sub < 4
    for slot in range(4):
        if slot < 3:
            one, two = acc[2 * slot], acc[2 * slot + 1]
            even_tile = jnp.where(low_half, one, pltpu.roll(two, 4, 1))
            odd_tile = jnp.where(low_half, pltpu.roll(one, 4, 1), two)
        else:
            even_tile, odd_tile = acc[6], pltpu.roll(acc[6], 4, 1)
        for tile in range(8):
            rs_send[2 * tile, 8 * slot : 8 * slot + 8] = even_tile[tile]
            rs_send[2 * tile + 1, 8 * slot : 8 * slot + 8] = odd_tile[tile]
    rs = []
    for n, peer in enumerate(far_first):
        rs.append(
            remote(rs_send.at[peer, pl.ds(0, 28)], rs_recv.at[comp, pl.ds(0, 28)], rs_ssem.at[n],
                   rs_rsem.at[n], {"comp": peer})
        )
    for copy in rs:
        copy.start()
    rs_recv[comp] = rs_send[comp]

    def amend(quad, turn):
        group = group_of(quad, turn)
        row_slot = ROW_SLOT[quad] + turn if turn < 2 else EXTRA_SLOT
        col_slot = COL_SLOT[quad] + turn if turn < 2 else EXTRA_SLOT
        way = COL_DIR[quad]
        fixes = col_fix[way]
        inside = lane < 2 if way == 0 else lane >= 126
        for i in range(9):
            at = 9 * group + i
            pair = 2 * (9 * col_slot + i)
            moved = lanes(fixes, -pair if way == 0 else 126 - pair)
            x[at] = x[at] + jnp.where(inside, moved, 0.0)
            row = 2 * (9 * row_slot + i)
            rows = row_fix[ROW_DIR[quad], row // 8, row % 8 : row % 8 + 2, :]
            if ROW_DIR[quad] == 0:
                x[at, 0, 0:2, :] += rows
            else:
                x[at, 7, 6:8, :] += rows

    for quad in range(4):
        for turn in (0, 1):
            amend(quad, turn)
        @pl.when(first == quad)
        def _(quad=quad):
            amend(quad, 2)

    for copy in halo + rs:
        copy.wait_send()
    for copy in rs:
        copy.wait_recv()

    energy = rs_recv[0, 24:28, :]
    for source in range(1, COMPS):
        energy = energy + rs_recv[source, 24:28, :]
    energy = energy / K
    energy = jnp.concatenate([energy, energy], axis=0)
    square = energy * energy
    plain = jnp.zeros((8, 128), jnp.float32)
    shoaled = jnp.zeros((8, 128), jnp.float32)
    for freq in range(NF):
        part = None
        for source in range(COMPS):
            slot = freq - 9 * source // 4
            if 0 <= slot < 3:
                tile = rs_recv[source, 8 * slot : 8 * slot + 8, :]
                part = tile if part is None else part + tile
        part = part / (1.0 + (2.0 * 1.1 ** (freq - (NF - 1))) * square)
        plain = plain + part
        shoaled = shoaled + (0.5 + 0.5 * freq / (NF - 1)) * part
    turned = pltpu.roll(shoaled, 4, 0)
    final = plain / K
    stress_x = (turned + shoaled - 0.5 * plain) / K
    stress_y = (2.0 * shoaled - turned - 0.5 * plain) / K
    ag_send[0] = jnp.where(low_half, stress_x, pltpu.roll(stress_y, 4, 0))
    ag_send[1] = jnp.where(low_half, energy, pltpu.roll(final, 4, 0))
    ag = [
        [
            remote(ag_send.at[n], ag_recv.at[n, comp], ag_ssem.at[n, at], ag_rsem.at[n, at], {"comp": peer})
            for at, peer in enumerate(far_first)
        ]
        for n in (0, 1)
    ]
    for copy in ag[0]:
        copy.start()
    ag_recv[0, comp] = ag_send[0]
    ag_recv[1, comp] = ag_send[1]
    for copy in ag[0][:AFTER:-1]:
        copy.wait_recv()
    for copy in ag[1]:
        copy.start()
    for copy in ag[0][AFTER::-1]:
        copy.wait_recv()

    def whole(n):
        gathered = ag_recv[n].reshape(8, 2, 8, 128)
        one, two = gathered[:, 0], gathered[:, 1]
        return (
            jnp.where(low_half, one, pltpu.roll(two, 4, 1)),
            jnp.where(low_half, pltpu.roll(one, 4, 1), two),
        )

    stress_x, stress_y = whole(0)

    edge_send[0] = stress_x
    edge_send[1] = stress_y
    strip_send[...] = jnp.where(
        (lane < 8) | (lane >= 120), stress_x, jnp.where(lane < 64, lanes(stress_y, 8), lanes(stress_y, 120))
    )
    rim = [
        remote(strip_send, strip_recv.at[0], rim_ssem.at[0], rim_rsem.at[0], place(0, 1)),
        remote(strip_send, strip_recv.at[1], rim_ssem.at[1], rim_rsem.at[1], place(0, -1)),
        remote(edge_send.at[:, 7], edge_recv.at[0], rim_ssem.at[2], rim_rsem.at[2], place(1, 0)),
        remote(edge_send.at[:, 0], edge_recv.at[1], rim_ssem.at[3], rim_rsem.at[3], place(-1, 0)),
        remote(strip_send.at[7], tip_recv.at[0, 0], rim_ssem.at[4], rim_rsem.at[4], place(1, 1)),
        remote(strip_send.at[7], tip_recv.at[1, 0], rim_ssem.at[5], rim_rsem.at[5], place(1, -1)),
        remote(strip_send.at[0], tip_recv.at[0, 1], rim_ssem.at[6], rim_rsem.at[6], place(-1, 1)),
        remote(strip_send.at[0], tip_recv.at[1, 1], rim_ssem.at[7], rim_rsem.at[7], place(-1, -1)),
    ]
    for copy in rim:
        copy.start()
    for copy in ag[1]:
        copy.wait_recv()
    energy, final = whole(1)
    start = (9 * comp) // 4
    high = 1.1 ** (-(NF - 1)) * power(1.1, start)
    rates = [
        1.0 / (1.0 + (2.0 * 1.1**slot * high) * (energy * energy)) for slot in range(3)
    ]
    for copy in ag[0] + ag[1]:
        copy.wait_send()
    for copy in rim:
        copy.wait_recv()

    big_lane = lane_index((80, 128))
    big_row = lax.broadcasted_iota(jnp.int32, (80, 128), 0)
    first_row = jnp.where(slab > 0, 0, 8)
    last_row = jnp.where(slab < SIDE - 1, 80, 72)
    in_rows = (big_row >= first_row) & (big_row < last_row)
    right_end = jnp.where(sect < SIDE - 1, 8, 0)
    left_start = jnp.where(sect > 0, 120, 128)
    in_strip = in_rows & ((big_lane < right_end) | (big_lane >= left_start))

    def middle(n, cells):
        return jnp.where(
            in_rows,
            jnp.concatenate([edge_recv[0, n], cells.reshape(64, 128), edge_recv[1, n]], axis=0),
            0.0,
        )

    left_strip = jnp.concatenate([tip_recv[0, 0], strip_recv[0].reshape(64, 128), tip_recv[0, 1]], axis=0)
    right_strip = jnp.concatenate([tip_recv[1, 0], strip_recv[1].reshape(64, 128), tip_recv[1, 1]], axis=0)
    xx = middle(0, stress_x)
    yy = middle(1, stress_y)
    xx_strip = jnp.where(in_strip, jnp.where(big_lane < 64, right_strip, left_strip), 0.0)
    yy_strip = jnp.where(
        in_strip, jnp.where(big_lane < 64, lanes(right_strip, 120), lanes(left_strip, 8)), 0.0
    )

    def beside(center, strip):
        center_up, strip_up = lanes(center, 127), lanes(strip, 127)
        center_down, strip_down = lanes(center, 1), lanes(strip, 1)
        last, head = big_lane == 127, big_lane == 0
        return (
            jnp.where(last, strip_up, center_up) + jnp.where(head, strip_down, center_down),
            jnp.where(last, center_up, strip_up) + jnp.where(head, center_down, strip_down),
        )

    def above_below(cells):
        return pltpu.roll(cells, 1, 0) + pltpu.roll(cells, 79, 0)

    yy_sides = beside(yy, yy_strip)
    source = jnp.where(in_rows, -((above_below(xx) - 2.0 * xx) + (yy_sides[0] - 2.0 * yy)), 0.0)
    source_strip = jnp.where(
        in_strip, -((above_below(xx_strip) - 2.0 * xx_strip) + (yy_sides[1] - 2.0 * yy_strip)), 0.0
    )
    surge, surge_strip = source * (1.0 / 4.5), source_strip * (1.0 / 4.5)
    for _ in range(JAC):
        sides = beside(surge, surge_strip)
        surge, surge_strip = (
            jnp.where(in_rows, (source + above_below(surge) + sides[0]) * (1.0 / 4.5), 0.0),
            jnp.where(in_strip, (source_strip + above_below(surge_strip) + sides[1]) * (1.0 / 4.5), 0.0),
        )
    surge = surge[8:72].reshape(8, 8, 128)
    reach = depth[...] + surge
    damping = 1.0 / (1.0 + 4.0 * final / (reach * reach + 1.0))
    for slot in range(3):
        factor_ref[slot] = rates[slot] * damping
    level_ref[...] = surge

    for copy in rim:
        copy.wait_send()


def damp_kernel(grown_ref, factor_ref, level_ref, out_ref, level_out, x, out_sem, small_sem):
    first = lax.axis_index("comp") % 4

    def store(group):
        rows = pl.ds(9 * group, 9)
        return pltpu.make_async_copy(x.at[rows], out_ref.at[rows], out_sem.at[group])

    surge = pltpu.make_async_copy(level_ref, level_out, small_sem.at[0])
    surge.start()
    for group in range(GROUPS):
        factor = factor_ref[(first + group) // 4]
        for i in range(9):
            x[9 * group + i] = grown_ref[9 * group + i] * factor
        store(group).start()
    surge.wait()
    for group in range(GROUPS):
        store(group).wait()


def local(spectrum, land_mask, ice_mask, wind_u, wind_v, depth):
    f32 = jnp.float32
    block = (8, 8, 128)
    anywhere = pl.BlockSpec(memory_space=pl.ANY)
    vmem = pl.BlockSpec(memory_space=pltpu.VMEM)
    dma = pltpu.SemaphoreType.DMA
    grown, factor, level = pl.pallas_call(
        step_kernel,
        out_shape=(
            pltpu.VMEM((LOCAL, *block), f32),
            pltpu.VMEM((3, *block), f32),
            pltpu.VMEM(block, f32),
        ),
        in_specs=[anywhere] * 7,
        out_specs=(vmem, vmem, vmem),
        scratch_shapes=[
            pltpu.VMEM(block, jnp.int32),
            pltpu.VMEM(block, jnp.int32),
            pltpu.VMEM(block, f32),
            pltpu.VMEM(block, f32),
            pltpu.VMEM(block, f32),
            pltpu.VMEM((T_END, 128), f32),
            pltpu.VMEM(block, f32),
            pltpu.VMEM((2, 12, 8, 128), f32),
            pltpu.VMEM((2, 12, 8, 128), f32),
            pltpu.VMEM((2, *block), f32),
            pltpu.VMEM((2, *block), f32),
            pltpu.VMEM((2, 2, 8, 128), f32),
            pltpu.VMEM((7, *block), f32),
            pltpu.VMEM((2, 12, 8, 128), f32),
            pltpu.VMEM((2, *block), f32),
            pltpu.VMEM((2, 4, 12, 8, 128), f32),
            pltpu.VMEM((2, 12, 8, 128), f32),
            pltpu.VMEM((2, *block), f32),
            pltpu.VMEM((COMPS, 32, 128), f32),
            pltpu.VMEM((COMPS, 32, 128), f32),
            pltpu.VMEM((2, 8, 128), f32),
            pltpu.VMEM((2, COMPS, 8, 128), f32),
            pltpu.VMEM((2, *block), f32),
            pltpu.VMEM((2, 2, 8, 128), f32),
            pltpu.VMEM(block, f32),
            pltpu.VMEM((2, *block), f32),
            pltpu.VMEM((2, 2, 8, 128), f32),
            dma((GROUPS,)),
            dma((6,)),
            dma((8,)),
            dma((8,)),
            dma((COMPS,)),
            dma((COMPS,)),
            dma((2, COMPS)),
            dma((2, COMPS)),
            dma((8,)),
            dma((8,)),
        ],
        compiler_params=pltpu.CompilerParams(
            collective_id=0, has_side_effects=True, vmem_limit_bytes=24 * 1024 * 1024
        ),
        name="wave_step",
    )(
        *[
            pltpu.with_memory_space_constraint(operand, pltpu.HBM)
            for operand in (
                spectrum.reshape(LOCAL, *block),
                land_mask.reshape(block),
                ice_mask.reshape(block),
                wind_u.reshape(block),
                wind_v.reshape(block),
                depth.reshape(block),
                jnp.asarray(table()),
            )
        ]
    )
    damped, level = pl.pallas_call(
        damp_kernel,
        out_shape=(jax.ShapeDtypeStruct((LOCAL, *block), f32), jax.ShapeDtypeStruct(block, f32)),
        in_specs=[vmem] * 3,
        out_specs=(anywhere, anywhere),
        scratch_shapes=[
            pltpu.VMEM((LOCAL, *block), f32),
            dma((GROUPS,)),
            dma((1,)),
        ],
        compiler_params=pltpu.CompilerParams(vmem_limit_bytes=24 * 1024 * 1024),
        name="damp",
    )(*[pltpu.with_memory_space_constraint(operand, pltpu.VMEM) for operand in (grown, factor, level)])
    return damped.reshape(spectrum.shape), level.reshape(depth.shape)


def solution(mesh):
    cells = P("slab", "sect")
    spectra = P("comp", "slab", "sect")
    return jax.shard_map(
        local,
        mesh=mesh,
        in_specs=(spectra, cells, cells, cells, cells, cells),
        out_specs=(spectra, cells),
        check_vma=False,
    )
```

```python
import functools
import math

import jax
import jax.numpy as jnp
import numpy as np
from jax import lax
from jax.experimental import pallas as pl
from jax.experimental.pallas import tpu as pltpu
from jax.sharding import PartitionSpec as P

ND = 36
NF = 36
K = ND * NF
JAC = 4
LOCAL = 81
GROUPS = 9
COMPS = 16
SIDE = 4
AFTER = 13
FAR_FIRST = tuple(
    (chips, other) for far in (4, 3, 2, 1) for chips in ((far, -far) if far < 4 else (far,)) for other in (0, 1)
) + ((0, 1),)
MESH = pl.DeviceIdType.MESH
HIGHEST = lax.Precision.HIGHEST

ROW_DIR = (0, 1, 1, 0)
COL_DIR = (0, 0, 1, 1)
ROW_SLOT = (0, 0, 2, 2)
COL_SLOT = (0, 2, 0, 2)
EXTRA_SLOT = 4

LANE_ROWS = 8
T_LANE = 0
T_ROW = T_LANE + 2 * LANE_ROWS
T_PICK = T_ROW + 2 * 96
T_SUM = T_PICK + 2 * 96
T_COL = T_SUM + 2 * 64
T_END = T_COL + 4 * 32


def direction(index):
    heading = 2.0 * math.pi * index / ND
    return math.cos(heading), math.sin(heading)


@functools.cache
def table():
    whole = np.zeros((COMPS, T_END, 128), np.float64)
    for member in range(COMPS):
        first = member % 4
        start = 9 * member // 4
        for group in range(GROUPS):
            quad = (first + group) % 4
            turn = group // 4
            freq_slot = (first + group) // 4
            freq = start + freq_slot
            row_dir, col_dir = ROW_DIR[quad], COL_DIR[quad]
            row_slot = ROW_SLOT[quad] + turn if turn < 2 else EXTRA_SLOT
            col_slot = COL_SLOT[quad] + turn if turn < 2 else EXTRA_SLOT
            low = 1.1 ** (-freq)
            scale = math.sqrt(0.5 * 1.1 ** (freq - (NF - 1)))
            for i in range(9):
                cosine, sine = direction(9 * quad + i)
                along_x, along_y = 0.7 * low * abs(cosine), 0.7 * low * abs(sine)
                values = [1.0 - along_x - along_y, along_x, along_y, scale * cosine, scale * sine]
                row = 2 * (9 * row_slot + i)
                lane = 2 * (9 * col_slot + i)
                pair = slice(lane, lane + 2)
                at = T_LANE + LANE_ROWS * col_dir
                for v, value in enumerate(values):
                    whole[member, at + v, pair] = value
                whole[member, at + 5, pair] = 1.0 if row_dir == 0 else 0.0
                for side in (0, 1):
                    out = 2 + side if col_dir == 0 else side
                    at = T_COL + 64 * col_dir
                    whole[member, at + 4 * freq_slot + out, lane + side] = 1.0
                    whole[member, at + 16 + 4 * freq_slot + out, lane + side] = cosine * cosine
                    whole[member, at + 32 + 12 + out, lane + side] = 1.0
                at = T_ROW + 96 * row_dir + row
                for v, value in enumerate(values):
                    whole[member, at : at + 2, v] = value
                whole[member, at : at + 2, 5] = 1.0 if col_dir == 0 else 0.0
                near = lane + 1 if col_dir == 0 else lane
                whole[member, T_PICK + 96 * row_dir + row + row_dir, near] = 1.0
                at = T_SUM + 64 * row_dir
                for side in (0, 1):
                    out = side if row_dir == 0 else 6 + side
                    whole[member, at + 16 * freq_slot + out, row + side] = 1.0
                    whole[member, at + 16 * freq_slot + 8 + out, row + side] = cosine * cosine
                    whole[member, at + 48 + out, row + side] = 1.0
    return whole.astype(np.float32)


def power(base, exponent):
    result = jnp.float32(1.0)
    for bit in range(6):
        odd = (exponent // (2**bit)) % 2
        result = result * jnp.where(odd == 1, jnp.float32(base ** (2**bit)), jnp.float32(1.0))
    return result


def from_above(cells, above=None):
    turned = pltpu.roll(cells, 1, 1)
    if above is None:
        top = jnp.zeros((1, 8, 128), jnp.float32)
    else:
        top = pltpu.roll(above, 1, 0)[None]
    before = jnp.concatenate([top, turned[:-1]], axis=0)
    sub = lax.broadcasted_iota(jnp.int32, cells.shape, 1)
    return jnp.where(sub == 0, before, turned)


def from_below(cells, below=None):
    turned = pltpu.roll(cells, 7, 1)
    if below is None:
        bottom = jnp.zeros((1, 8, 128), jnp.float32)
    else:
        bottom = pltpu.roll(below, 7, 0)[None]
    after = jnp.concatenate([turned[1:], bottom], axis=0)
    sub = lax.broadcasted_iota(jnp.int32, cells.shape, 1)
    return jnp.where(sub == 7, after, turned)


def lanes(cells, shift):
    return pltpu.roll(cells, shift % 128, cells.ndim - 1)


def lane_index(shape):
    return lax.broadcasted_iota(jnp.int32, shape, len(shape) - 1)


def from_left(cells):
    return jnp.where(lane_index(cells.shape) == 0, 0.0, lanes(cells, 1))


def from_right(cells):
    return jnp.where(lane_index(cells.shape) == 127, 0.0, lanes(cells, 127))


def step_kernel(
    spec_ref, land_ref, ice_ref, wu_ref, wv_ref, depth_ref, table_ref,
    x, factor_ref, level_ref,
    land, ice, wu, wv, depth, tab, wet,
    row_send, row_recv, col_send, col_recv, corner_recv,
    acc, row_fix, col_fix, row_coef, row_gain, col_gain,
    rs_send, rs_recv, ag_send, ag_recv,
    edge_send, edge_recv, strip_send, strip_recv, tip_recv,
    relay, load_sem, small_sem,
    halo_ssem, halo_rsem, rs_ssem, rs_rsem, ag_ssem, ag_rsem, rim_ssem, rim_rsem,
):
    comp = lax.axis_index("comp")
    slab = lax.axis_index("slab")
    sect = lax.axis_index("sect")
    first = comp % 4

    def place(down, right):
        return {"slab": (slab + down + SIDE) % SIDE, "sect": (sect + right + SIDE) % SIDE}

    around = [place(a, b) for a in (-1, 0, 1) for b in (-1, 0, 1) if (a, b) != (0, 0)]
    core = comp % 2

    def along(chips, other):
        return (comp - core + 2 * chips + COMPS) % COMPS + (core + other) % 2

    far_first = [along(*peer) for peer in FAR_FIRST]
    nearest = [{"comp": along(*peer)} for peer in ((1, 0), (-1, 0), (1, 1), (-1, 1), (0, 1))]
    barrier = pltpu.get_barrier_semaphore()
    for peer in around + nearest:
        pl.semaphore_signal(barrier, 1, device_id=peer, device_id_type=MESH)

    def tell(turn, chips):
        for peer in (along(chips, 0), along(-chips, 0)):
            pl.semaphore_signal(relay.at[turn], 1, device_id={"comp": peer}, device_id_type=MESH)

    small = [
        pltpu.make_async_copy(src, dst, small_sem.at[n])
        for n, (src, dst) in enumerate(
            [(land_ref, land), (ice_ref, ice), (wu_ref, wu), (wv_ref, wv), (depth_ref, depth),
             (table_ref.at[comp], tab)]
        )
    ]
    small[0].start()

    def load(group):
        rows = pl.ds(9 * group, 9)
        return pltpu.make_async_copy(spec_ref.at[rows], x.at[rows], load_sem.at[group])

    def group_of(quad, turn):
        return (quad - first + 4) % 4 + 4 * turn

    order = [(0, 0), (1, 0), (0, 1), (1, 1), (2, 0), (3, 0), (2, 1), (3, 1)]
    for quad, turn in order:
        load(group_of(quad, turn)).start()
    load(8).start()
    for copy in small[1:]:
        copy.start()

    lane = lane_index((8, 128))
    lane_pair = lane // 2
    sub = lax.broadcasted_iota(jnp.int32, (8, 128), 0)
    even_lane = lane % 2 == 0
    even_sub = sub % 2 == 0

    row_send[0, 9:12] = jnp.zeros((3, 8, 128), jnp.float32)
    row_send[1, 9:12] = jnp.zeros((3, 8, 128), jnp.float32)
    small[0].wait()
    wet[...] = (1 - land[...]).astype(jnp.float32)

    def pack(quad, turn, packed):
        group = group_of(quad, turn)
        row_slot = ROW_SLOT[quad] + turn if turn < 2 else EXTRA_SLOT
        col_slot = COL_SLOT[quad] + turn if turn < 2 else EXTRA_SLOT
        load(group).wait()
        for i in range(9):
            cells = x[9 * group + i]
            row = 2 * (9 * row_slot + i)
            to = (ROW_DIR[quad], row // 8, pl.ds(row % 8, 2))
            if ROW_DIR[quad] == 0:
                row_send[to] = cells[7, 6:8] * wet[7, 6:8, :]
            else:
                row_send[to] = cells[0, 0:2] * wet[0, 0:2, :]
            pair = 9 * col_slot + i
            shift = 2 * pair + 2 if COL_DIR[quad] == 0 else 2 * pair
            packed = jnp.where(lane_pair == pair, lanes(cells, shift), packed)
        return packed

    for way in (0, 1):
        packed = jnp.zeros((8, 8, 128), jnp.float32)
        for quad, turn in order:
            if COL_DIR[quad] == way:
                packed = pack(quad, turn, packed)
        col_send[way] = packed
    for quad in range(4):
        @pl.when(first == quad)
        def _(quad=quad):
            col_send[COL_DIR[quad]] = pack(quad, 2, col_send[COL_DIR[quad]])

    wet_now = wet[...]
    for way in (0, 1):
        at = 126 if way == 0 else 0
        one, two = wet_now[:, :, at : at + 1], wet_now[:, :, at + 1 : at + 2]
        pair_wet = jnp.where(even_lane, one, two)
        col_send[way] = jnp.where(lane_pair == 63, pair_wet, col_send[way] * pair_wet)
    row_send[0, 11, 2:4] = wet[7, 6:8, :]
    row_send[1, 11, 2:4] = wet[0, 0:2, :]

    pl.semaphore_wait(barrier, len(around) + len(nearest))

    def remote(src, dst, ssem, rsem, peer):
        return pltpu.make_async_remote_copy(
            src_ref=src, dst_ref=dst, send_sem=ssem, recv_sem=rsem, device_id=peer, device_id_type=MESH
        )

    halo = [
        remote(col_send.at[0], col_recv.at[0], halo_ssem.at[0], halo_rsem.at[0], place(0, 1)),
        remote(col_send.at[1], col_recv.at[1], halo_ssem.at[1], halo_rsem.at[1], place(0, -1)),
    ]
    for way in (0, 1):
        step = 1 if way == 0 else -1
        halo.append(
            remote(col_send.at[way, 7], corner_recv.at[way, 0], halo_ssem.at[2 + way], halo_rsem.at[2 + way],
                   place(1, step))
        )
        halo.append(
            remote(col_send.at[way, 0], corner_recv.at[way, 1], halo_ssem.at[4 + way], halo_rsem.at[4 + way],
                   place(-1, step))
        )
    halo.append(remote(row_send.at[0], row_recv.at[0], halo_ssem.at[6], halo_rsem.at[6], place(1, 0)))
    halo.append(remote(row_send.at[1], row_recv.at[1], halo_ssem.at[7], halo_rsem.at[7], place(-1, 0)))
    for copy in halo:
        copy.start()
    tell(0, 1)

    acc[...] = jnp.zeros_like(acc)
    for copy in small[1:]:
        copy.wait()
    open_sea = (1 - ice[...]).astype(jnp.float32)
    wu[...] = wu[...] * open_sea
    wv[...] = wv[...] * open_sea

    for quad in range(4):
        upwind_row = from_above if ROW_DIR[quad] == 0 else from_below
        upwind_col = from_left if COL_DIR[quad] == 0 else from_right

        def body(turn, carry, quad=quad, upwind_row=upwind_row, upwind_col=upwind_col):
            group = group_of(quad, turn)
            freq = (9 * comp + group) // 4
            slot = (first + group) // 4
            low = 0.7 * power(1.0 / 1.1, freq)
            scale = math.sqrt(0.5 * 1.1 ** (-(NF - 1))) * power(math.sqrt(1.1), freq)
            total_e = jnp.zeros((8, 8, 128), jnp.float32)
            total_f = jnp.zeros((8, 8, 128), jnp.float32)
            total_c = jnp.zeros((8, 8, 128), jnp.float32)
            for i in range(9):
                cosine, sine = direction(9 * quad + i)
                along_x, along_y = low * abs(cosine), low * abs(sine)
                stay = 1.0 - along_x - along_y
                cells = x[9 * group + i] * wet[...]
                for _ in range(2):
                    cells = wet[...] * (
                        stay * cells + along_x * upwind_row(cells) + along_y * upwind_col(cells)
                    )
                push = jnp.maximum((scale * cosine) * wu[...] + (scale * sine) * wv[...], 0.0)
                grown = cells + cells * (push * push)
                x[9 * group + i] = grown
                total_e += cells
                total_f += grown
                total_c += (cosine * cosine) * grown
            acc[6] += total_e
            acc[2 * slot] += total_f
            acc[2 * slot + 1] += total_c
            return carry

        lax.fori_loop(0, 2 + (first == quad).astype(jnp.int32), body, 0)
        if quad == 1:
            pl.semaphore_wait(relay.at[0], 2)
            tell(1, 2)

    for way in (0, 1):
        at = T_LANE + LANE_ROWS * way
        low_at = 0 if way == 0 else 126
        wind = [
            jnp.where(even_lane, w[:, :, low_at : low_at + 1], w[:, :, low_at + 1 : low_at + 2])
            for w in (wu, wv)
        ]
        push = jnp.maximum(tab[at + 3 : at + 4, :][None] * wind[0] + tab[at + 4 : at + 5, :][None] * wind[1], 0.0)
        col_gain[way] = 1.0 + push * push
        at = T_ROW + 96 * way
        spread = lambda n: jnp.broadcast_to(tab[at : at + 96, n : n + 1], (96, 128)).reshape(12, 8, 128)
        for n, source in enumerate((0, 1, 2, 5)):
            row_coef[way, n] = spread(source)
        tile, low_at = (0, 0) if way == 0 else (7, 6)
        wind = [
            jnp.where(even_sub, w[tile, low_at : low_at + 1, :], w[tile, low_at + 1 : low_at + 2, :])
            for w in (wu, wv)
        ]
        push = jnp.maximum(spread(3) * wind[0] + spread(4) * wind[1], 0.0)
        row_gain[way] = 1.0 + push * push

    for copy in halo:
        copy.wait_recv()

    has = {
        "up": (slab > 0).astype(jnp.float32), "down": (slab < SIDE - 1).astype(jnp.float32),
        "left": (sect > 0).astype(jnp.float32), "right": (sect < SIDE - 1).astype(jnp.float32),
    }
    col_terms, col_weights = [], []
    for way in (0, 1):
        lane_row = lambda n: tab[T_LANE + LANE_ROWS * way + n : T_LANE + LANE_ROWS * way + n + 1, :][None]
        stay, along_x, along_y, is_up = [lane_row(n) for n in (0, 1, 2, 5)]
        side = has["left"] if way == 0 else has["right"]
        got = col_recv[way] * side
        above = corner_recv[way, 0] * (side * has["up"])
        below = corner_recv[way, 1] * (side * has["down"])
        turn = 127 if way == 0 else 1
        near, near_above, near_below = lanes(got, turn), lanes(above, turn), lanes(below, turn)
        halo_wet = got[:, :, 127:128] if way == 0 else got[:, :, 126:127]
        at_near, at_far = (0, 1) if way == 0 else (127, 126)
        wet_near, wet_far = wet_now[:, :, at_near : at_near + 1], wet_now[:, :, at_far : at_far + 1]
        up_now = jnp.where(is_up > 0.5, from_above(near, near_above), from_below(near, near_below))
        outside = halo_wet * (stay * near + along_x * up_now + along_y * got)
        one = wet_near * (along_y * near)
        up_one = jnp.where(is_up > 0.5, from_above(one), from_below(one))
        two = wet_near * (stay * one + along_x * up_one + along_y * outside)
        far = lanes(wet_far * (along_y * one), 1 if way == 0 else 127)
        fix = jnp.where(even_lane, two, far) if way == 0 else jnp.where(even_lane, far, two)
        fix_grown = fix * col_gain[way]
        col_fix[way] = fix_grown
        col_terms += [fix_grown.reshape(64, 128), fix.reshape(64, 128)]
        at = T_COL + 64 * way
        col_weights += [tab[at : at + 32, :], tab[at + 32 : at + 64, :]]
    col_weights = jnp.concatenate(
        [jnp.concatenate(col_weights, axis=1), jnp.zeros((96, 512), jnp.float32)], axis=0
    )
    col_out = lax.dot_general(
        jnp.concatenate(col_terms, axis=1), col_weights, (((1,), (1,)), ((), ())),
        precision=HIGHEST, preferred_element_type=jnp.float32,
    ).reshape(8, 8, 128)
    rim_lane = (lane < 2) | (lane >= 126)
    for slot in range(3):
        acc[2 * slot] += jnp.where(rim_lane, lanes(col_out, 126 - 4 * slot), 0.0)
        acc[2 * slot + 1] += jnp.where(rim_lane, lanes(col_out, 110 - 4 * slot), 0.0)
    acc[6] += jnp.where(rim_lane, lanes(col_out, 114), 0.0)

    for way in (0, 1):
        stay, along_x, along_y, is_left = [row_coef[way, n] for n in range(4)]
        side = has["up"] if way == 0 else has["down"]
        got = row_recv[way] * side
        near = pltpu.roll(got, 7 if way == 0 else 1, 1)
        edge = 7 if way == 0 else 0
        left_corner = corner_recv[0, way, edge : edge + 1, :] * (side * has["left"])
        right_corner = corner_recv[1, way, edge : edge + 1, :] * (side * has["right"])
        choose = tab[T_PICK + 96 * way : T_PICK + 96 * way + 96, :].reshape(12, 8, 128)
        corner = jnp.sum(
            choose * jnp.where(is_left > 0.5, left_corner[None], right_corner[None]), axis=2, keepdims=True
        )
        halo_wet = got[11, 3:4, :] if way == 0 else got[11, 2:3, :]
        tile, near_row, far_row = (0, 0, 1) if way == 0 else (7, 7, 6)
        wet_near, wet_far = wet[tile, near_row : near_row + 1, :], wet[tile, far_row : far_row + 1, :]
        lane3 = lane_index((12, 8, 128))
        beside = jnp.where(
            is_left > 0.5,
            jnp.where(lane3 == 0, corner, lanes(near, 1)),
            jnp.where(lane3 == 127, corner, lanes(near, 127)),
        )
        outside = halo_wet * (stay * near + along_x * got + along_y * beside)
        one = wet_near * (along_x * near)
        beside_one = jnp.where(is_left > 0.5, from_left(one), from_right(one))
        two = wet_near * (stay * one + along_y * beside_one + along_x * outside)
        far = pltpu.roll(wet_far * (along_x * one), 1 if way == 0 else 7, 1)
        fix = jnp.where(even_sub, two, far) if way == 0 else jnp.where(even_sub, far, two)
        fix_grown = fix * row_gain[way]
        row_fix[way] = fix_grown
        at = T_SUM + 64 * way
        weights = tab[at : at + 48, 0:96]
        sum_grown = jnp.dot(weights, fix_grown.reshape(96, 128), precision=HIGHEST,
                            preferred_element_type=jnp.float32)
        sum_moved = jnp.dot(tab[at + 48 : at + 56, 0:96], fix.reshape(96, 128), precision=HIGHEST,
                            preferred_element_type=jnp.float32)
        for v in range(6):
            acc[v, tile] += sum_grown[8 * v : 8 * v + 8]
        acc[6, tile] += sum_moved

    low_half = sub < 4
    for slot in range(4):
        if slot < 3:
            one, two = acc[2 * slot], acc[2 * slot + 1]
            even_tile = jnp.where(low_half, one, pltpu.roll(two, 4, 1))
            odd_tile = jnp.where(low_half, pltpu.roll(one, 4, 1), two)
        else:
            even_tile, odd_tile = acc[6], pltpu.roll(acc[6], 4, 1)
        for tile in range(8):
            rs_send[2 * tile, 8 * slot : 8 * slot + 8] = even_tile[tile]
            rs_send[2 * tile + 1, 8 * slot : 8 * slot + 8] = odd_tile[tile]
    pl.semaphore_wait(relay.at[1], 2)
    rs = []
    for n, peer in enumerate(far_first):
        rs.append(
            remote(rs_send.at[peer, pl.ds(0, 28)], rs_recv.at[comp, pl.ds(0, 28)], rs_ssem.at[n],
                   rs_rsem.at[n], {"comp": peer})
        )
    for copy in rs:
        copy.start()
    rs_recv[comp] = rs_send[comp]

    def amend(quad, turn):
        group = group_of(quad, turn)
        row_slot = ROW_SLOT[quad] + turn if turn < 2 else EXTRA_SLOT
        col_slot = COL_SLOT[quad] + turn if turn < 2 else EXTRA_SLOT
        way = COL_DIR[quad]
        fixes = col_fix[way]
        inside = lane < 2 if way == 0 else lane >= 126
        for i in range(9):
            at = 9 * group + i
            pair = 2 * (9 * col_slot + i)
            moved = lanes(fixes, -pair if way == 0 else 126 - pair)
            x[at] = x[at] + jnp.where(inside, moved, 0.0)
            row = 2 * (9 * row_slot + i)
            rows = row_fix[ROW_DIR[quad], row // 8, row % 8 : row % 8 + 2, :]
            if ROW_DIR[quad] == 0:
                x[at, 0, 0:2, :] += rows
            else:
                x[at, 7, 6:8, :] += rows

    for quad in range(4):
        for turn in (0, 1):
            amend(quad, turn)
        @pl.when(first == quad)
        def _(quad=quad):
            amend(quad, 2)

    for copy in halo + rs:
        copy.wait_send()
    for copy in rs:
        copy.wait_recv()

    energy = rs_recv[0, 24:28, :]
    for source in range(1, COMPS):
        energy = energy + rs_recv[source, 24:28, :]
    energy = energy / K
    energy = jnp.concatenate([energy, energy], axis=0)
    square = energy * energy
    plain = jnp.zeros((8, 128), jnp.float32)
    shoaled = jnp.zeros((8, 128), jnp.float32)
    for freq in range(NF):
        part = None
        for source in range(COMPS):
            slot = freq - 9 * source // 4
            if 0 <= slot < 3:
                tile = rs_recv[source, 8 * slot : 8 * slot + 8, :]
                part = tile if part is None else part + tile
        part = part / (1.0 + (2.0 * 1.1 ** (freq - (NF - 1))) * square)
        plain = plain + part
        shoaled = shoaled + (0.5 + 0.5 * freq / (NF - 1)) * part
    turned = pltpu.roll(shoaled, 4, 0)
    final = plain / K
    stress_x = (turned + shoaled - 0.5 * plain) / K
    stress_y = (2.0 * shoaled - turned - 0.5 * plain) / K
    ag_send[0] = jnp.where(low_half, stress_x, pltpu.roll(stress_y, 4, 0))
    ag_send[1] = jnp.where(low_half, energy, pltpu.roll(final, 4, 0))
    ag = [
        [
            remote(ag_send.at[n], ag_recv.at[n, comp], ag_ssem.at[n, at], ag_rsem.at[n, at], {"comp": peer})
            for at, peer in enumerate(far_first)
        ]
        for n in (0, 1)
    ]
    for copy in ag[0]:
        copy.start()
    ag_recv[0, comp] = ag_send[0]
    ag_recv[1, comp] = ag_send[1]
    for copy in ag[0][:AFTER:-1]:
        copy.wait_recv()
    for copy in ag[1]:
        copy.start()
    for copy in ag[0][AFTER::-1]:
        copy.wait_recv()

    def whole(n):
        gathered = ag_recv[n].reshape(8, 2, 8, 128)
        one, two = gathered[:, 0], gathered[:, 1]
        return (
            jnp.where(low_half, one, pltpu.roll(two, 4, 1)),
            jnp.where(low_half, pltpu.roll(one, 4, 1), two),
        )

    stress_x, stress_y = whole(0)

    edge_send[0] = stress_x
    edge_send[1] = stress_y
    strip_send[...] = jnp.where(
        (lane < 8) | (lane >= 120), stress_x, jnp.where(lane < 64, lanes(stress_y, 8), lanes(stress_y, 120))
    )
    rim = [
        remote(strip_send, strip_recv.at[0], rim_ssem.at[0], rim_rsem.at[0], place(0, 1)),
        remote(strip_send, strip_recv.at[1], rim_ssem.at[1], rim_rsem.at[1], place(0, -1)),
        remote(edge_send.at[:, 7], edge_recv.at[0], rim_ssem.at[2], rim_rsem.at[2], place(1, 0)),
        remote(edge_send.at[:, 0], edge_recv.at[1], rim_ssem.at[3], rim_rsem.at[3], place(-1, 0)),
        remote(strip_send.at[7], tip_recv.at[0, 0], rim_ssem.at[4], rim_rsem.at[4], place(1, 1)),
        remote(strip_send.at[7], tip_recv.at[1, 0], rim_ssem.at[5], rim_rsem.at[5], place(1, -1)),
        remote(strip_send.at[0], tip_recv.at[0, 1], rim_ssem.at[6], rim_rsem.at[6], place(-1, 1)),
        remote(strip_send.at[0], tip_recv.at[1, 1], rim_ssem.at[7], rim_rsem.at[7], place(-1, -1)),
    ]
    for copy in rim:
        copy.start()
    for copy in ag[1]:
        copy.wait_recv()
    energy, final = whole(1)
    start = (9 * comp) // 4
    high = 1.1 ** (-(NF - 1)) * power(1.1, start)
    rates = [
        1.0 / (1.0 + (2.0 * 1.1**slot * high) * (energy * energy)) for slot in range(3)
    ]
    for copy in ag[0] + ag[1]:
        copy.wait_send()
    for copy in rim:
        copy.wait_recv()

    big_lane = lane_index((80, 128))
    big_row = lax.broadcasted_iota(jnp.int32, (80, 128), 0)
    first_row = jnp.where(slab > 0, 0, 8)
    last_row = jnp.where(slab < SIDE - 1, 80, 72)
    in_rows = (big_row >= first_row) & (big_row < last_row)
    right_end = jnp.where(sect < SIDE - 1, 8, 0)
    left_start = jnp.where(sect > 0, 120, 128)
    in_strip = in_rows & ((big_lane < right_end) | (big_lane >= left_start))

    def middle(n, cells):
        return jnp.where(
            in_rows,
            jnp.concatenate([edge_recv[0, n], cells.reshape(64, 128), edge_recv[1, n]], axis=0),
            0.0,
        )

    left_strip = jnp.concatenate([tip_recv[0, 0], strip_recv[0].reshape(64, 128), tip_recv[0, 1]], axis=0)
    right_strip = jnp.concatenate([tip_recv[1, 0], strip_recv[1].reshape(64, 128), tip_recv[1, 1]], axis=0)
    xx = middle(0, stress_x)
    yy = middle(1, stress_y)
    xx_strip = jnp.where(in_strip, jnp.where(big_lane < 64, right_strip, left_strip), 0.0)
    yy_strip = jnp.where(
        in_strip, jnp.where(big_lane < 64, lanes(right_strip, 120), lanes(left_strip, 8)), 0.0
    )

    def beside(center, strip):
        center_up, strip_up = lanes(center, 127), lanes(strip, 127)
        center_down, strip_down = lanes(center, 1), lanes(strip, 1)
        last, head = big_lane == 127, big_lane == 0
        return (
            jnp.where(last, strip_up, center_up) + jnp.where(head, strip_down, center_down),
            jnp.where(last, center_up, strip_up) + jnp.where(head, center_down, strip_down),
        )

    def above_below(cells):
        return pltpu.roll(cells, 1, 0) + pltpu.roll(cells, 79, 0)

    yy_sides = beside(yy, yy_strip)
    source = jnp.where(in_rows, -((above_below(xx) - 2.0 * xx) + (yy_sides[0] - 2.0 * yy)), 0.0)
    source_strip = jnp.where(
        in_strip, -((above_below(xx_strip) - 2.0 * xx_strip) + (yy_sides[1] - 2.0 * yy_strip)), 0.0
    )
    surge, surge_strip = source * (1.0 / 4.5), source_strip * (1.0 / 4.5)
    for _ in range(JAC):
        sides = beside(surge, surge_strip)
        surge, surge_strip = (
            jnp.where(in_rows, (source + above_below(surge) + sides[0]) * (1.0 / 4.5), 0.0),
            jnp.where(in_strip, (source_strip + above_below(surge_strip) + sides[1]) * (1.0 / 4.5), 0.0),
        )
    surge = surge[8:72].reshape(8, 8, 128)
    reach = depth[...] + surge
    damping = 1.0 / (1.0 + 4.0 * final / (reach * reach + 1.0))
    for slot in range(3):
        factor_ref[slot] = rates[slot] * damping
    level_ref[...] = surge

    for copy in rim:
        copy.wait_send()


def damp_kernel(grown_ref, factor_ref, level_ref, out_ref, level_out, x, out_sem, small_sem):
    first = lax.axis_index("comp") % 4

    def store(group):
        rows = pl.ds(9 * group, 9)
        return pltpu.make_async_copy(x.at[rows], out_ref.at[rows], out_sem.at[group])

    surge = pltpu.make_async_copy(level_ref, level_out, small_sem.at[0])
    surge.start()
    for group in range(GROUPS):
        factor = factor_ref[(first + group) // 4]
        for i in range(9):
            x[9 * group + i] = grown_ref[9 * group + i] * factor
        store(group).start()
    surge.wait()
    for group in range(GROUPS):
        store(group).wait()


def local(spectrum, land_mask, ice_mask, wind_u, wind_v, depth):
    f32 = jnp.float32
    block = (8, 8, 128)
    anywhere = pl.BlockSpec(memory_space=pl.ANY)
    vmem = pl.BlockSpec(memory_space=pltpu.VMEM)
    dma = pltpu.SemaphoreType.DMA
    grown, factor, level = pl.pallas_call(
        step_kernel,
        out_shape=(
            pltpu.VMEM((LOCAL, *block), f32),
            pltpu.VMEM((3, *block), f32),
            pltpu.VMEM(block, f32),
        ),
        in_specs=[anywhere] * 7,
        out_specs=(vmem, vmem, vmem),
        scratch_shapes=[
            pltpu.VMEM(block, jnp.int32),
            pltpu.VMEM(block, jnp.int32),
            pltpu.VMEM(block, f32),
            pltpu.VMEM(block, f32),
            pltpu.VMEM(block, f32),
            pltpu.VMEM((T_END, 128), f32),
            pltpu.VMEM(block, f32),
            pltpu.VMEM((2, 12, 8, 128), f32),
            pltpu.VMEM((2, 12, 8, 128), f32),
            pltpu.VMEM((2, *block), f32),
            pltpu.VMEM((2, *block), f32),
            pltpu.VMEM((2, 2, 8, 128), f32),
            pltpu.VMEM((7, *block), f32),
            pltpu.VMEM((2, 12, 8, 128), f32),
            pltpu.VMEM((2, *block), f32),
            pltpu.VMEM((2, 4, 12, 8, 128), f32),
            pltpu.VMEM((2, 12, 8, 128), f32),
            pltpu.VMEM((2, *block), f32),
            pltpu.VMEM((COMPS, 32, 128), f32),
            pltpu.VMEM((COMPS, 32, 128), f32),
            pltpu.VMEM((2, 8, 128), f32),
            pltpu.VMEM((2, COMPS, 8, 128), f32),
            pltpu.VMEM((2, *block), f32),
            pltpu.VMEM((2, 2, 8, 128), f32),
            pltpu.VMEM(block, f32),
            pltpu.VMEM((2, *block), f32),
            pltpu.VMEM((2, 2, 8, 128), f32),
            pltpu.SemaphoreType.REGULAR((2,)),
            dma((GROUPS,)),
            dma((6,)),
            dma((8,)),
            dma((8,)),
            dma((COMPS,)),
            dma((COMPS,)),
            dma((2, COMPS)),
            dma((2, COMPS)),
            dma((8,)),
            dma((8,)),
        ],
        compiler_params=pltpu.CompilerParams(
            collective_id=0, has_side_effects=True, vmem_limit_bytes=24 * 1024 * 1024
        ),
        name="wave_step",
    )(
        *[
            pltpu.with_memory_space_constraint(operand, pltpu.HBM)
            for operand in (
                spectrum.reshape(LOCAL, *block),
                land_mask.reshape(block),
                ice_mask.reshape(block),
                wind_u.reshape(block),
                wind_v.reshape(block),
                depth.reshape(block),
                jnp.asarray(table()),
            )
        ]
    )
    damped, level = pl.pallas_call(
        damp_kernel,
        out_shape=(jax.ShapeDtypeStruct((LOCAL, *block), f32), jax.ShapeDtypeStruct(block, f32)),
        in_specs=[vmem] * 3,
        out_specs=(anywhere, anywhere),
        scratch_shapes=[
            pltpu.VMEM((LOCAL, *block), f32),
            dma((GROUPS,)),
            dma((1,)),
        ],
        compiler_params=pltpu.CompilerParams(vmem_limit_bytes=24 * 1024 * 1024),
        name="damp",
    )(*[pltpu.with_memory_space_constraint(operand, pltpu.VMEM) for operand in (grown, factor, level)])
    return damped.reshape(spectrum.shape), level.reshape(depth.shape)


def solution(mesh):
    cells = P("slab", "sect")
    spectra = P("comp", "slab", "sect")
    return jax.shard_map(
        local,
        mesh=mesh,
        in_specs=(spectra, cells, cells, cells, cells, cells),
        out_specs=(spectra, cells),
        check_vma=False,
    )
```

```python
import functools
import math

import jax
import jax.numpy as jnp
import numpy as np
from jax import lax
from jax.experimental import pallas as pl
from jax.experimental.pallas import tpu as pltpu
from jax.sharding import PartitionSpec as P

ND = 36
NF = 36
K = ND * NF
JAC = 4
LOCAL = 81
GROUPS = 9
COMPS = 16
SIDE = 4
AFTER = 13
FAR_FIRST = tuple(
    (chips, other) for far in (4, 3, 2, 1) for chips in ((far, -far) if far < 4 else (far,)) for other in (0, 1)
) + ((0, 1),)
MESH = pl.DeviceIdType.MESH
HIGHEST = lax.Precision.HIGHEST

ROW_DIR = (0, 1, 1, 0)
COL_DIR = (0, 0, 1, 1)
ROW_SLOT = (0, 0, 2, 2)
COL_SLOT = (0, 2, 0, 2)
EXTRA_SLOT = 4

LANE_ROWS = 8
T_LANE = 0
T_ROW = T_LANE + 2 * LANE_ROWS
T_PICK = T_ROW + 2 * 96
T_SUM = T_PICK + 2 * 96
T_COL = T_SUM + 2 * 64
T_END = T_COL + 4 * 32


def direction(index):
    heading = 2.0 * math.pi * index / ND
    return math.cos(heading), math.sin(heading)


@functools.cache
def table():
    whole = np.zeros((COMPS, T_END, 128), np.float64)
    for member in range(COMPS):
        first = member % 4
        start = 9 * member // 4
        for group in range(GROUPS):
            quad = (first + group) % 4
            turn = group // 4
            freq_slot = (first + group) // 4
            freq = start + freq_slot
            row_dir, col_dir = ROW_DIR[quad], COL_DIR[quad]
            row_slot = ROW_SLOT[quad] + turn if turn < 2 else EXTRA_SLOT
            col_slot = COL_SLOT[quad] + turn if turn < 2 else EXTRA_SLOT
            low = 1.1 ** (-freq)
            scale = math.sqrt(0.5 * 1.1 ** (freq - (NF - 1)))
            for i in range(9):
                cosine, sine = direction(9 * quad + i)
                along_x, along_y = 0.7 * low * abs(cosine), 0.7 * low * abs(sine)
                values = [1.0 - along_x - along_y, along_x, along_y, scale * cosine, scale * sine]
                row = 2 * (9 * row_slot + i)
                lane = 2 * (9 * col_slot + i)
                pair = slice(lane, lane + 2)
                at = T_LANE + LANE_ROWS * col_dir
                for v, value in enumerate(values):
                    whole[member, at + v, pair] = value
                whole[member, at + 5, pair] = 1.0 if row_dir == 0 else 0.0
                for side in (0, 1):
                    out = 2 + side if col_dir == 0 else side
                    at = T_COL + 64 * col_dir
                    whole[member, at + 4 * freq_slot + out, lane + side] = 1.0
                    whole[member, at + 16 + 4 * freq_slot + out, lane + side] = cosine * cosine
                    whole[member, at + 32 + 12 + out, lane + side] = 1.0
                at = T_ROW + 96 * row_dir + row
                for v, value in enumerate(values):
                    whole[member, at : at + 2, v] = value
                whole[member, at : at + 2, 5] = 1.0 if col_dir == 0 else 0.0
                near = lane + 1 if col_dir == 0 else lane
                whole[member, T_PICK + 96 * row_dir + row + row_dir, near] = 1.0
                at = T_SUM + 64 * row_dir
                for side in (0, 1):
                    out = side if row_dir == 0 else 6 + side
                    whole[member, at + 16 * freq_slot + out, row + side] = 1.0
                    whole[member, at + 16 * freq_slot + 8 + out, row + side] = cosine * cosine
                    whole[member, at + 48 + out, row + side] = 1.0
    return whole.astype(np.float32)


def power(base, exponent):
    result = jnp.float32(1.0)
    for bit in range(6):
        odd = (exponent // (2**bit)) % 2
        result = result * jnp.where(odd == 1, jnp.float32(base ** (2**bit)), jnp.float32(1.0))
    return result


def tree_sum(terms):
    while len(terms) > 1:
        terms = [sum(terms[n + 1 : n + 2], terms[n]) for n in range(0, len(terms), 2)]
    return terms[0]


def from_above(cells, above=None):
    turned = pltpu.roll(cells, 1, 1)
    if above is None:
        top = jnp.zeros((1, 8, 128), jnp.float32)
    else:
        top = pltpu.roll(above, 1, 0)[None]
    before = jnp.concatenate([top, turned[:-1]], axis=0)
    sub = lax.broadcasted_iota(jnp.int32, cells.shape, 1)
    return jnp.where(sub == 0, before, turned)


def from_below(cells, below=None):
    turned = pltpu.roll(cells, 7, 1)
    if below is None:
        bottom = jnp.zeros((1, 8, 128), jnp.float32)
    else:
        bottom = pltpu.roll(below, 7, 0)[None]
    after = jnp.concatenate([turned[1:], bottom], axis=0)
    sub = lax.broadcasted_iota(jnp.int32, cells.shape, 1)
    return jnp.where(sub == 7, after, turned)


def lanes(cells, shift):
    return pltpu.roll(cells, shift % 128, cells.ndim - 1)


def lane_index(shape):
    return lax.broadcasted_iota(jnp.int32, shape, len(shape) - 1)


def from_left(cells):
    return jnp.where(lane_index(cells.shape) == 0, 0.0, lanes(cells, 1))


def from_right(cells):
    return jnp.where(lane_index(cells.shape) == 127, 0.0, lanes(cells, 127))


def step_kernel(
    spec_ref, land_ref, ice_ref, wu_ref, wv_ref, depth_ref, table_ref,
    x, factor_ref, level_ref,
    land, ice, wu, wv, depth, tab, wet,
    row_send, row_recv, col_send, col_recv, corner_recv,
    acc, row_fix, col_fix, row_coef, row_gain, col_gain,
    rs_send, rs_recv, ag_send, ag_recv,
    edge_send, edge_recv, strip_send, strip_recv, tip_recv,
    relay, load_sem, small_sem,
    halo_ssem, halo_rsem, rs_ssem, rs_rsem, ag_ssem, ag_rsem, rim_ssem, rim_rsem,
):
    comp = lax.axis_index("comp")
    slab = lax.axis_index("slab")
    sect = lax.axis_index("sect")
    first = comp % 4

    def place(down, right):
        return {"slab": (slab + down + SIDE) % SIDE, "sect": (sect + right + SIDE) % SIDE}

    around = [place(a, b) for a in (-1, 0, 1) for b in (-1, 0, 1) if (a, b) != (0, 0)]
    core = comp % 2

    def along(chips, other):
        return (comp - core + 2 * chips + COMPS) % COMPS + (core + other) % 2

    far_first = [along(*peer) for peer in FAR_FIRST]
    nearest = [{"comp": along(*peer)} for peer in ((1, 0), (-1, 0), (1, 1), (-1, 1), (0, 1))]
    barrier = pltpu.get_barrier_semaphore()
    for peer in around + nearest:
        pl.semaphore_signal(barrier, 1, device_id=peer, device_id_type=MESH)

    def tell(turn, chips):
        for peer in (along(chips, 0), along(-chips, 0)):
            pl.semaphore_signal(relay.at[turn], 1, device_id={"comp": peer}, device_id_type=MESH)

    small = [
        pltpu.make_async_copy(src, dst, small_sem.at[n])
        for n, (src, dst) in enumerate(
            [(land_ref, land), (ice_ref, ice), (wu_ref, wu), (wv_ref, wv), (depth_ref, depth),
             (table_ref.at[comp], tab)]
        )
    ]
    small[0].start()

    def load(group):
        rows = pl.ds(9 * group, 9)
        return pltpu.make_async_copy(spec_ref.at[rows], x.at[rows], load_sem.at[group])

    def group_of(quad, turn):
        return (quad - first + 4) % 4 + 4 * turn

    order = [(0, 0), (1, 0), (0, 1), (1, 1), (2, 0), (3, 0), (2, 1), (3, 1)]
    for quad, turn in order:
        load(group_of(quad, turn)).start()
    load(8).start()
    for copy in small[1:]:
        copy.start()

    lane = lane_index((8, 128))
    lane_pair = lane // 2
    sub = lax.broadcasted_iota(jnp.int32, (8, 128), 0)
    even_lane = lane % 2 == 0
    even_sub = sub % 2 == 0

    row_send[0, 9:12] = jnp.zeros((3, 8, 128), jnp.float32)
    row_send[1, 9:12] = jnp.zeros((3, 8, 128), jnp.float32)
    small[0].wait()
    wet[...] = (1 - land[...]).astype(jnp.float32)

    def pack(quad, turn, packed):
        group = group_of(quad, turn)
        row_slot = ROW_SLOT[quad] + turn if turn < 2 else EXTRA_SLOT
        col_slot = COL_SLOT[quad] + turn if turn < 2 else EXTRA_SLOT
        load(group).wait()
        for i in range(9):
            cells = x[9 * group + i]
            row = 2 * (9 * row_slot + i)
            to = (ROW_DIR[quad], row // 8, pl.ds(row % 8, 2))
            if ROW_DIR[quad] == 0:
                row_send[to] = cells[7, 6:8] * wet[7, 6:8, :]
            else:
                row_send[to] = cells[0, 0:2] * wet[0, 0:2, :]
            pair = 9 * col_slot + i
            shift = 2 * pair + 2 if COL_DIR[quad] == 0 else 2 * pair
            packed = jnp.where(lane_pair == pair, lanes(cells, shift), packed)
        return packed

    for way in (0, 1):
        packed = jnp.zeros((8, 8, 128), jnp.float32)
        for quad, turn in order:
            if COL_DIR[quad] == way:
                packed = pack(quad, turn, packed)
        col_send[way] = packed
    for quad in range(4):
        @pl.when(first == quad)
        def _(quad=quad):
            col_send[COL_DIR[quad]] = pack(quad, 2, col_send[COL_DIR[quad]])

    wet_now = wet[...]
    for way in (0, 1):
        at = 126 if way == 0 else 0
        one, two = wet_now[:, :, at : at + 1], wet_now[:, :, at + 1 : at + 2]
        pair_wet = jnp.where(even_lane, one, two)
        col_send[way] = jnp.where(lane_pair == 63, pair_wet, col_send[way] * pair_wet)
    row_send[0, 11, 2:4] = wet[7, 6:8, :]
    row_send[1, 11, 2:4] = wet[0, 0:2, :]

    pl.semaphore_wait(barrier, len(around) + len(nearest))

    def remote(src, dst, ssem, rsem, peer):
        return pltpu.make_async_remote_copy(
            src_ref=src, dst_ref=dst, send_sem=ssem, recv_sem=rsem, device_id=peer, device_id_type=MESH
        )

    halo = [
        remote(col_send.at[0], col_recv.at[0], halo_ssem.at[0], halo_rsem.at[0], place(0, 1)),
        remote(col_send.at[1], col_recv.at[1], halo_ssem.at[1], halo_rsem.at[1], place(0, -1)),
    ]
    for way in (0, 1):
        step = 1 if way == 0 else -1
        halo.append(
            remote(col_send.at[way, 7], corner_recv.at[way, 0], halo_ssem.at[2 + way], halo_rsem.at[2 + way],
                   place(1, step))
        )
        halo.append(
            remote(col_send.at[way, 0], corner_recv.at[way, 1], halo_ssem.at[4 + way], halo_rsem.at[4 + way],
                   place(-1, step))
        )
    halo.append(remote(row_send.at[0], row_recv.at[0], halo_ssem.at[6], halo_rsem.at[6], place(1, 0)))
    halo.append(remote(row_send.at[1], row_recv.at[1], halo_ssem.at[7], halo_rsem.at[7], place(-1, 0)))
    for copy in halo:
        copy.start()
    tell(0, 1)

    acc[...] = jnp.zeros_like(acc)
    for copy in small[1:]:
        copy.wait()
    open_sea = (1 - ice[...]).astype(jnp.float32)
    wu[...] = wu[...] * open_sea
    wv[...] = wv[...] * open_sea

    for quad in range(4):
        upwind_row = from_above if ROW_DIR[quad] == 0 else from_below
        upwind_col = from_left if COL_DIR[quad] == 0 else from_right

        def body(turn, carry, quad=quad, upwind_row=upwind_row, upwind_col=upwind_col):
            group = group_of(quad, turn)
            freq = (9 * comp + group) // 4
            slot = (first + group) // 4
            low = 0.7 * power(1.0 / 1.1, freq)
            scale = math.sqrt(0.5 * 1.1 ** (-(NF - 1))) * power(math.sqrt(1.1), freq)
            total_e = jnp.zeros((8, 8, 128), jnp.float32)
            total_f = jnp.zeros((8, 8, 128), jnp.float32)
            total_c = jnp.zeros((8, 8, 128), jnp.float32)
            for i in range(9):
                cosine, sine = direction(9 * quad + i)
                along_x, along_y = low * abs(cosine), low * abs(sine)
                stay = 1.0 - along_x - along_y
                cells = x[9 * group + i] * wet[...]
                for _ in range(2):
                    cells = wet[...] * (
                        stay * cells + along_x * upwind_row(cells) + along_y * upwind_col(cells)
                    )
                push = jnp.maximum((scale * cosine) * wu[...] + (scale * sine) * wv[...], 0.0)
                grown = cells + cells * (push * push)
                x[9 * group + i] = grown
                total_e += cells
                total_f += grown
                total_c += (cosine * cosine) * grown
            acc[6] += total_e
            acc[2 * slot] += total_f
            acc[2 * slot + 1] += total_c
            return carry

        lax.fori_loop(0, 2 + (first == quad).astype(jnp.int32), body, 0)
        if quad == 0:
            pl.semaphore_wait(relay.at[0], 2)
            tell(1, 2)

    for way in (0, 1):
        at = T_LANE + LANE_ROWS * way
        low_at = 0 if way == 0 else 126
        wind = [
            jnp.where(even_lane, w[:, :, low_at : low_at + 1], w[:, :, low_at + 1 : low_at + 2])
            for w in (wu, wv)
        ]
        push = jnp.maximum(tab[at + 3 : at + 4, :][None] * wind[0] + tab[at + 4 : at + 5, :][None] * wind[1], 0.0)
        col_gain[way] = 1.0 + push * push
        at = T_ROW + 96 * way
        spread = lambda n: jnp.broadcast_to(tab[at : at + 96, n : n + 1], (96, 128)).reshape(12, 8, 128)
        for n, source in enumerate((0, 1, 2, 5)):
            row_coef[way, n] = spread(source)
        tile, low_at = (0, 0) if way == 0 else (7, 6)
        wind = [
            jnp.where(even_sub, w[tile, low_at : low_at + 1, :], w[tile, low_at + 1 : low_at + 2, :])
            for w in (wu, wv)
        ]
        push = jnp.maximum(spread(3) * wind[0] + spread(4) * wind[1], 0.0)
        row_gain[way] = 1.0 + push * push

    for copy in halo:
        copy.wait_recv()

    has = {
        "up": (slab > 0).astype(jnp.float32), "down": (slab < SIDE - 1).astype(jnp.float32),
        "left": (sect > 0).astype(jnp.float32), "right": (sect < SIDE - 1).astype(jnp.float32),
    }
    col_terms, col_weights = [], []
    for way in (0, 1):
        lane_row = lambda n: tab[T_LANE + LANE_ROWS * way + n : T_LANE + LANE_ROWS * way + n + 1, :][None]
        stay, along_x, along_y, is_up = [lane_row(n) for n in (0, 1, 2, 5)]
        side = has["left"] if way == 0 else has["right"]
        got = col_recv[way] * side
        above = corner_recv[way, 0] * (side * has["up"])
        below = corner_recv[way, 1] * (side * has["down"])
        turn = 127 if way == 0 else 1
        near, near_above, near_below = lanes(got, turn), lanes(above, turn), lanes(below, turn)
        halo_wet = got[:, :, 127:128] if way == 0 else got[:, :, 126:127]
        at_near, at_far = (0, 1) if way == 0 else (127, 126)
        wet_near, wet_far = wet_now[:, :, at_near : at_near + 1], wet_now[:, :, at_far : at_far + 1]
        up_now = jnp.where(is_up > 0.5, from_above(near, near_above), from_below(near, near_below))
        outside = halo_wet * (stay * near + along_x * up_now + along_y * got)
        one = wet_near * (along_y * near)
        up_one = jnp.where(is_up > 0.5, from_above(one), from_below(one))
        two = wet_near * (stay * one + along_x * up_one + along_y * outside)
        far = lanes(wet_far * (along_y * one), 1 if way == 0 else 127)
        fix = jnp.where(even_lane, two, far) if way == 0 else jnp.where(even_lane, far, two)
        fix_grown = fix * col_gain[way]
        col_fix[way] = fix_grown
        col_terms += [fix_grown.reshape(64, 128), fix.reshape(64, 128)]
        at = T_COL + 64 * way
        col_weights += [tab[at : at + 32, :], tab[at + 32 : at + 64, :]]
    col_weights = jnp.concatenate(
        [jnp.concatenate(col_weights, axis=1), jnp.zeros((96, 512), jnp.float32)], axis=0
    )
    col_out = lax.dot_general(
        jnp.concatenate(col_terms, axis=1), col_weights, (((1,), (1,)), ((), ())),
        precision=HIGHEST, preferred_element_type=jnp.float32,
    ).reshape(8, 8, 128)
    rim_lane = (lane < 2) | (lane >= 126)
    for slot in range(3):
        acc[2 * slot] += jnp.where(rim_lane, lanes(col_out, 126 - 4 * slot), 0.0)
        acc[2 * slot + 1] += jnp.where(rim_lane, lanes(col_out, 110 - 4 * slot), 0.0)
    acc[6] += jnp.where(rim_lane, lanes(col_out, 114), 0.0)

    for way in (0, 1):
        stay, along_x, along_y, is_left = [row_coef[way, n] for n in range(4)]
        side = has["up"] if way == 0 else has["down"]
        got = row_recv[way] * side
        near = pltpu.roll(got, 7 if way == 0 else 1, 1)
        edge = 7 if way == 0 else 0
        left_corner = corner_recv[0, way, edge : edge + 1, :] * (side * has["left"])
        right_corner = corner_recv[1, way, edge : edge + 1, :] * (side * has["right"])
        choose = tab[T_PICK + 96 * way : T_PICK + 96 * way + 96, :].reshape(12, 8, 128)
        corner = jnp.sum(
            choose * jnp.where(is_left > 0.5, left_corner[None], right_corner[None]), axis=2, keepdims=True
        )
        halo_wet = got[11, 3:4, :] if way == 0 else got[11, 2:3, :]
        tile, near_row, far_row = (0, 0, 1) if way == 0 else (7, 7, 6)
        wet_near, wet_far = wet[tile, near_row : near_row + 1, :], wet[tile, far_row : far_row + 1, :]
        lane3 = lane_index((12, 8, 128))
        beside = jnp.where(
            is_left > 0.5,
            jnp.where(lane3 == 0, corner, lanes(near, 1)),
            jnp.where(lane3 == 127, corner, lanes(near, 127)),
        )
        outside = halo_wet * (stay * near + along_x * got + along_y * beside)
        one = wet_near * (along_x * near)
        beside_one = jnp.where(is_left > 0.5, from_left(one), from_right(one))
        two = wet_near * (stay * one + along_y * beside_one + along_x * outside)
        far = pltpu.roll(wet_far * (along_x * one), 1 if way == 0 else 7, 1)
        fix = jnp.where(even_sub, two, far) if way == 0 else jnp.where(even_sub, far, two)
        fix_grown = fix * row_gain[way]
        row_fix[way] = fix_grown
        at = T_SUM + 64 * way
        weights = tab[at : at + 48, 0:96]
        sum_grown = jnp.dot(weights, fix_grown.reshape(96, 128), precision=HIGHEST,
                            preferred_element_type=jnp.float32)
        sum_moved = jnp.dot(tab[at + 48 : at + 56, 0:96], fix.reshape(96, 128), precision=HIGHEST,
                            preferred_element_type=jnp.float32)
        for v in range(6):
            acc[v, tile] += sum_grown[8 * v : 8 * v + 8]
        acc[6, tile] += sum_moved

    low_half = sub < 4
    for slot in range(4):
        if slot < 3:
            one, two = acc[2 * slot], acc[2 * slot + 1]
            even_tile = jnp.where(low_half, one, pltpu.roll(two, 4, 1))
            odd_tile = jnp.where(low_half, pltpu.roll(one, 4, 1), two)
        else:
            even_tile, odd_tile = acc[6], pltpu.roll(acc[6], 4, 1)
        for tile in range(8):
            rs_send[2 * tile, 8 * slot : 8 * slot + 8] = even_tile[tile]
            rs_send[2 * tile + 1, 8 * slot : 8 * slot + 8] = odd_tile[tile]
    pl.semaphore_wait(relay.at[1], 2)
    rs = []
    for n, peer in enumerate(far_first):
        rs.append(
            remote(rs_send.at[peer, pl.ds(0, 28)], rs_recv.at[comp, pl.ds(0, 28)], rs_ssem.at[n],
                   rs_rsem.at[n], {"comp": peer})
        )
    for copy in rs:
        copy.start()
    rs_recv[comp] = rs_send[comp]

    def amend(quad, turn):
        group = group_of(quad, turn)
        row_slot = ROW_SLOT[quad] + turn if turn < 2 else EXTRA_SLOT
        col_slot = COL_SLOT[quad] + turn if turn < 2 else EXTRA_SLOT
        way = COL_DIR[quad]
        fixes = col_fix[way]
        inside = lane < 2 if way == 0 else lane >= 126
        for i in range(9):
            at = 9 * group + i
            pair = 2 * (9 * col_slot + i)
            moved = lanes(fixes, -pair if way == 0 else 126 - pair)
            x[at] = x[at] + jnp.where(inside, moved, 0.0)
            row = 2 * (9 * row_slot + i)
            rows = row_fix[ROW_DIR[quad], row // 8, row % 8 : row % 8 + 2, :]
            if ROW_DIR[quad] == 0:
                x[at, 0, 0:2, :] += rows
            else:
                x[at, 7, 6:8, :] += rows

    for quad in range(4):
        for turn in (0, 1):
            amend(quad, turn)
        @pl.when(first == quad)
        def _(quad=quad):
            amend(quad, 2)

    for copy in halo + rs:
        copy.wait_send()
    for copy in rs:
        copy.wait_recv()

    energy = tree_sum([rs_recv[source, 24:28, :] for source in range(COMPS)])
    energy = energy / K
    energy = jnp.concatenate([energy, energy], axis=0)
    square = energy * energy
    parts = []
    for freq in range(NF):
        part = None
        for source in range(COMPS):
            slot = freq - 9 * source // 4
            if 0 <= slot < 3:
                tile = rs_recv[source, 8 * slot : 8 * slot + 8, :]
                part = tile if part is None else part + tile
        part = part / (1.0 + (2.0 * 1.1 ** (freq - (NF - 1))) * square)
        parts.append(part)
    plain = tree_sum(parts)
    shoaled = tree_sum([(0.5 + 0.5 * freq / (NF - 1)) * part for freq, part in enumerate(parts)])
    turned = pltpu.roll(shoaled, 4, 0)
    final = plain / K
    stress_x = (turned + shoaled - 0.5 * plain) / K
    stress_y = (2.0 * shoaled - turned - 0.5 * plain) / K
    ag_send[0] = jnp.where(low_half, stress_x, pltpu.roll(stress_y, 4, 0))
    ag_send[1] = jnp.where(low_half, energy, pltpu.roll(final, 4, 0))
    ag = [
        [
            remote(ag_send.at[n], ag_recv.at[n, comp], ag_ssem.at[n, at], ag_rsem.at[n, at], {"comp": peer})
            for at, peer in enumerate(far_first)
        ]
        for n in (0, 1)
    ]
    for copy in ag[0]:
        copy.start()
    ag_recv[0, comp] = ag_send[0]
    ag_recv[1, comp] = ag_send[1]
    for copy in ag[0][:AFTER:-1]:
        copy.wait_recv()
    for copy in ag[1]:
        copy.start()
    for copy in ag[0][AFTER::-1]:
        copy.wait_recv()

    def whole(n):
        gathered = ag_recv[n].reshape(8, 2, 8, 128)
        one, two = gathered[:, 0], gathered[:, 1]
        return (
            jnp.where(low_half, one, pltpu.roll(two, 4, 1)),
            jnp.where(low_half, pltpu.roll(one, 4, 1), two),
        )

    stress_x, stress_y = whole(0)

    edge_send[0] = stress_x
    edge_send[1] = stress_y
    strip_send[...] = jnp.where(
        (lane < 8) | (lane >= 120), stress_x, jnp.where(lane < 64, lanes(stress_y, 8), lanes(stress_y, 120))
    )
    rim = [
        remote(strip_send, strip_recv.at[0], rim_ssem.at[0], rim_rsem.at[0], place(0, 1)),
        remote(strip_send, strip_recv.at[1], rim_ssem.at[1], rim_rsem.at[1], place(0, -1)),
        remote(edge_send.at[:, 7], edge_recv.at[0], rim_ssem.at[2], rim_rsem.at[2], place(1, 0)),
        remote(edge_send.at[:, 0], edge_recv.at[1], rim_ssem.at[3], rim_rsem.at[3], place(-1, 0)),
        remote(strip_send.at[7], tip_recv.at[0, 0], rim_ssem.at[4], rim_rsem.at[4], place(1, 1)),
        remote(strip_send.at[7], tip_recv.at[1, 0], rim_ssem.at[5], rim_rsem.at[5], place(1, -1)),
        remote(strip_send.at[0], tip_recv.at[0, 1], rim_ssem.at[6], rim_rsem.at[6], place(-1, 1)),
        remote(strip_send.at[0], tip_recv.at[1, 1], rim_ssem.at[7], rim_rsem.at[7], place(-1, -1)),
    ]
    for copy in rim:
        copy.start()
    for copy in ag[1]:
        copy.wait_recv()
    energy, final = whole(1)
    start = (9 * comp) // 4
    high = 1.1 ** (-(NF - 1)) * power(1.1, start)
    rates = [
        1.0 / (1.0 + (2.0 * 1.1**slot * high) * (energy * energy)) for slot in range(3)
    ]
    for copy in ag[0] + ag[1]:
        copy.wait_send()
    for copy in rim:
        copy.wait_recv()

    big_lane = lane_index((80, 128))
    big_row = lax.broadcasted_iota(jnp.int32, (80, 128), 0)
    first_row = jnp.where(slab > 0, 0, 8)
    last_row = jnp.where(slab < SIDE - 1, 80, 72)
    in_rows = (big_row >= first_row) & (big_row < last_row)
    right_end = jnp.where(sect < SIDE - 1, 8, 0)
    left_start = jnp.where(sect > 0, 120, 128)
    in_strip = in_rows & ((big_lane < right_end) | (big_lane >= left_start))

    def middle(n, cells):
        return jnp.where(
            in_rows,
            jnp.concatenate([edge_recv[0, n], cells.reshape(64, 128), edge_recv[1, n]], axis=0),
            0.0,
        )

    left_strip = jnp.concatenate([tip_recv[0, 0], strip_recv[0].reshape(64, 128), tip_recv[0, 1]], axis=0)
    right_strip = jnp.concatenate([tip_recv[1, 0], strip_recv[1].reshape(64, 128), tip_recv[1, 1]], axis=0)
    xx = middle(0, stress_x)
    yy = middle(1, stress_y)
    xx_strip = jnp.where(in_strip, jnp.where(big_lane < 64, right_strip, left_strip), 0.0)
    yy_strip = jnp.where(
        in_strip, jnp.where(big_lane < 64, lanes(right_strip, 120), lanes(left_strip, 8)), 0.0
    )

    def beside(center, strip):
        center_up, strip_up = lanes(center, 127), lanes(strip, 127)
        center_down, strip_down = lanes(center, 1), lanes(strip, 1)
        last, head = big_lane == 127, big_lane == 0
        return (
            jnp.where(last, strip_up, center_up) + jnp.where(head, strip_down, center_down),
            jnp.where(last, center_up, strip_up) + jnp.where(head, center_down, strip_down),
        )

    def above_below(cells):
        return pltpu.roll(cells, 1, 0) + pltpu.roll(cells, 79, 0)

    yy_sides = beside(yy, yy_strip)
    source = jnp.where(in_rows, -((above_below(xx) - 2.0 * xx) + (yy_sides[0] - 2.0 * yy)), 0.0)
    source_strip = jnp.where(
        in_strip, -((above_below(xx_strip) - 2.0 * xx_strip) + (yy_sides[1] - 2.0 * yy_strip)), 0.0
    )
    surge, surge_strip = source * (1.0 / 4.5), source_strip * (1.0 / 4.5)
    for _ in range(JAC):
        sides = beside(surge, surge_strip)
        surge, surge_strip = (
            jnp.where(in_rows, (source + above_below(surge) + sides[0]) * (1.0 / 4.5), 0.0),
            jnp.where(in_strip, (source_strip + above_below(surge_strip) + sides[1]) * (1.0 / 4.5), 0.0),
        )
    surge = surge[8:72].reshape(8, 8, 128)
    reach = depth[...] + surge
    depth_term = reach * reach + 1.0
    damping = depth_term / (depth_term + 4.0 * final)
    for slot in range(3):
        factor_ref[slot] = rates[slot] * damping
    level_ref[...] = surge

    for copy in rim:
        copy.wait_send()


def damp_kernel(grown_ref, factor_ref, level_ref, out_ref, level_out, x, out_sem, small_sem):
    first = lax.axis_index("comp") % 4

    def store(group):
        rows = pl.ds(9 * group, 9)
        return pltpu.make_async_copy(x.at[rows], out_ref.at[rows], out_sem.at[group])

    surge = pltpu.make_async_copy(level_ref, level_out, small_sem.at[0])
    surge.start()
    for group in range(GROUPS):
        factor = factor_ref[(first + group) // 4]
        for i in range(9):
            x[9 * group + i] = grown_ref[9 * group + i] * factor
        store(group).start()
    surge.wait()
    for group in range(GROUPS):
        store(group).wait()


def local(spectrum, land_mask, ice_mask, wind_u, wind_v, depth):
    f32 = jnp.float32
    block = (8, 8, 128)
    anywhere = pl.BlockSpec(memory_space=pl.ANY)
    vmem = pl.BlockSpec(memory_space=pltpu.VMEM)
    dma = pltpu.SemaphoreType.DMA
    grown, factor, level = pl.pallas_call(
        step_kernel,
        out_shape=(
            pltpu.VMEM((LOCAL, *block), f32),
            pltpu.VMEM((3, *block), f32),
            pltpu.VMEM(block, f32),
        ),
        in_specs=[anywhere] * 7,
        out_specs=(vmem, vmem, vmem),
        scratch_shapes=[
            pltpu.VMEM(block, jnp.int32),
            pltpu.VMEM(block, jnp.int32),
            pltpu.VMEM(block, f32),
            pltpu.VMEM(block, f32),
            pltpu.VMEM(block, f32),
            pltpu.VMEM((T_END, 128), f32),
            pltpu.VMEM(block, f32),
            pltpu.VMEM((2, 12, 8, 128), f32),
            pltpu.VMEM((2, 12, 8, 128), f32),
            pltpu.VMEM((2, *block), f32),
            pltpu.VMEM((2, *block), f32),
            pltpu.VMEM((2, 2, 8, 128), f32),
            pltpu.VMEM((7, *block), f32),
            pltpu.VMEM((2, 12, 8, 128), f32),
            pltpu.VMEM((2, *block), f32),
            pltpu.VMEM((2, 4, 12, 8, 128), f32),
            pltpu.VMEM((2, 12, 8, 128), f32),
            pltpu.VMEM((2, *block), f32),
            pltpu.VMEM((COMPS, 32, 128), f32),
            pltpu.VMEM((COMPS, 32, 128), f32),
            pltpu.VMEM((2, 8, 128), f32),
            pltpu.VMEM((2, COMPS, 8, 128), f32),
            pltpu.VMEM((2, *block), f32),
            pltpu.VMEM((2, 2, 8, 128), f32),
            pltpu.VMEM(block, f32),
            pltpu.VMEM((2, *block), f32),
            pltpu.VMEM((2, 2, 8, 128), f32),
            pltpu.SemaphoreType.REGULAR((2,)),
            dma((GROUPS,)),
            dma((6,)),
            dma((8,)),
            dma((8,)),
            dma((COMPS,)),
            dma((COMPS,)),
            dma((2, COMPS)),
            dma((2, COMPS)),
            dma((8,)),
            dma((8,)),
        ],
        compiler_params=pltpu.CompilerParams(
            collective_id=0, has_side_effects=True, vmem_limit_bytes=24 * 1024 * 1024
        ),
        name="wave_step",
    )(
        *[
            pltpu.with_memory_space_constraint(operand, pltpu.HBM)
            for operand in (
                spectrum.reshape(LOCAL, *block),
                land_mask.reshape(block),
                ice_mask.reshape(block),
                wind_u.reshape(block),
                wind_v.reshape(block),
                depth.reshape(block),
                jnp.asarray(table()),
            )
        ]
    )
    damped, level = pl.pallas_call(
        damp_kernel,
        out_shape=(jax.ShapeDtypeStruct((LOCAL, *block), f32), jax.ShapeDtypeStruct(block, f32)),
        in_specs=[vmem] * 3,
        out_specs=(anywhere, anywhere),
        scratch_shapes=[
            pltpu.VMEM((LOCAL, *block), f32),
            dma((GROUPS,)),
            dma((1,)),
        ],
        compiler_params=pltpu.CompilerParams(vmem_limit_bytes=24 * 1024 * 1024),
        name="damp",
    )(*[pltpu.with_memory_space_constraint(operand, pltpu.VMEM) for operand in (grown, factor, level)])
    return damped.reshape(spectrum.shape), level.reshape(depth.shape)


def solution(mesh):
    cells = P("slab", "sect")
    spectra = P("comp", "slab", "sect")
    return jax.shard_map(
        local,
        mesh=mesh,
        in_specs=(spectra, cells, cells, cells, cells, cells),
        out_specs=(spectra, cells),
        check_vma=False,
    )
```

```python
import functools
import math

import jax
import jax.numpy as jnp
import numpy as np
from jax import lax
from jax.experimental import pallas as pl
from jax.experimental.pallas import tpu as pltpu
from jax.sharding import PartitionSpec as P

ND = 36
NF = 36
K = ND * NF
JAC = 4
LOCAL = 81
GROUPS = 9
COMPS = 16
SIDE = 4
AFTER = 13
FAR_FIRST = tuple(
    (chips, other) for far in (4, 3, 2, 1) for chips in ((far, -far) if far < 4 else (far,)) for other in (0, 1)
) + ((0, 1),)
MESH = pl.DeviceIdType.MESH
HIGHEST = lax.Precision.HIGHEST

ROW_DIR = (0, 1, 1, 0)
COL_DIR = (0, 0, 1, 1)
ROW_SLOT = (0, 0, 2, 2)
COL_SLOT = (0, 2, 0, 2)
EXTRA_SLOT = 4

LANE_ROWS = 8
T_LANE = 0
T_ROW = T_LANE + 2 * LANE_ROWS
T_PICK = T_ROW + 2 * 96
T_SUM = T_PICK + 2 * 96
T_COL = T_SUM + 2 * 64
T_END = T_COL + 4 * 32


def direction(index):
    heading = 2.0 * math.pi * index / ND
    return math.cos(heading), math.sin(heading)


@functools.cache
def table():
    whole = np.zeros((COMPS, T_END, 128), np.float64)
    for member in range(COMPS):
        first = member % 4
        start = 9 * member // 4
        for group in range(GROUPS):
            quad = (first + group) % 4
            turn = group // 4
            freq_slot = (first + group) // 4
            freq = start + freq_slot
            row_dir, col_dir = ROW_DIR[quad], COL_DIR[quad]
            row_slot = ROW_SLOT[quad] + turn if turn < 2 else EXTRA_SLOT
            col_slot = COL_SLOT[quad] + turn if turn < 2 else EXTRA_SLOT
            low = 1.1 ** (-freq)
            scale = math.sqrt(0.5 * 1.1 ** (freq - (NF - 1)))
            for i in range(9):
                cosine, sine = direction(9 * quad + i)
                along_x, along_y = 0.7 * low * abs(cosine), 0.7 * low * abs(sine)
                values = [1.0 - along_x - along_y, along_x, along_y, scale * cosine, scale * sine]
                row = 2 * (9 * row_slot + i)
                lane = 2 * (9 * col_slot + i)
                pair = slice(lane, lane + 2)
                at = T_LANE + LANE_ROWS * col_dir
                for v, value in enumerate(values):
                    whole[member, at + v, pair] = value
                whole[member, at + 5, pair] = 1.0 if row_dir == 0 else 0.0
                for side in (0, 1):
                    out = 2 + side if col_dir == 0 else side
                    at = T_COL + 64 * col_dir
                    whole[member, at + 4 * freq_slot + out, lane + side] = 1.0
                    whole[member, at + 16 + 4 * freq_slot + out, lane + side] = cosine * cosine
                    whole[member, at + 32 + 12 + out, lane + side] = 1.0
                at = T_ROW + 96 * row_dir + row
                for v, value in enumerate(values):
                    whole[member, at : at + 2, v] = value
                whole[member, at : at + 2, 5] = 1.0 if col_dir == 0 else 0.0
                near = lane + 1 if col_dir == 0 else lane
                whole[member, T_PICK + 96 * row_dir + row + row_dir, near] = 1.0
                at = T_SUM + 64 * row_dir
                for side in (0, 1):
                    out = side if row_dir == 0 else 6 + side
                    whole[member, at + 16 * freq_slot + out, row + side] = 1.0
                    whole[member, at + 16 * freq_slot + 8 + out, row + side] = cosine * cosine
                    whole[member, at + 48 + out, row + side] = 1.0
    return whole.astype(np.float32)


def power(base, exponent):
    result = jnp.float32(1.0)
    for bit in range(6):
        odd = (exponent // (2**bit)) % 2
        result = result * jnp.where(odd == 1, jnp.float32(base ** (2**bit)), jnp.float32(1.0))
    return result


def tree_sum(terms):
    while len(terms) > 1:
        terms = [sum(terms[n + 1 : n + 2], terms[n]) for n in range(0, len(terms), 2)]
    return terms[0]


def from_above(cells, above=None):
    turned = pltpu.roll(cells, 1, 1)
    if above is None:
        top = jnp.zeros((1, 8, 128), jnp.float32)
    else:
        top = pltpu.roll(above, 1, 0)[None]
    before = jnp.concatenate([top, turned[:-1]], axis=0)
    sub = lax.broadcasted_iota(jnp.int32, cells.shape, 1)
    return jnp.where(sub == 0, before, turned)


def from_below(cells, below=None):
    turned = pltpu.roll(cells, 7, 1)
    if below is None:
        bottom = jnp.zeros((1, 8, 128), jnp.float32)
    else:
        bottom = pltpu.roll(below, 7, 0)[None]
    after = jnp.concatenate([turned[1:], bottom], axis=0)
    sub = lax.broadcasted_iota(jnp.int32, cells.shape, 1)
    return jnp.where(sub == 7, after, turned)


def lanes(cells, shift):
    return pltpu.roll(cells, shift % 128, cells.ndim - 1)


def lane_index(shape):
    return lax.broadcasted_iota(jnp.int32, shape, len(shape) - 1)


def from_left(cells):
    return jnp.where(lane_index(cells.shape) == 0, 0.0, lanes(cells, 1))


def from_right(cells):
    return jnp.where(lane_index(cells.shape) == 127, 0.0, lanes(cells, 127))


def step_kernel(
    spec_ref, land_ref, ice_ref, wu_ref, wv_ref, depth_ref, table_ref,
    x, factor_ref, level_ref,
    land, ice, wu, wv, depth, tab, wet,
    row_send, row_recv, col_send, col_recv, corner_recv,
    acc, row_fix, col_fix, row_coef, row_gain, col_gain,
    rs_send, rs_recv, ag_send, ag_recv,
    edge_send, edge_recv, strip_send, strip_recv, tip_recv,
    relay, load_sem, small_sem,
    halo_ssem, halo_rsem, rs_ssem, rs_rsem, ag_ssem, ag_rsem, rim_ssem, rim_rsem,
):
    comp = lax.axis_index("comp")
    slab = lax.axis_index("slab")
    sect = lax.axis_index("sect")
    first = comp % 4

    def place(down, right):
        return {"slab": (slab + down + SIDE) % SIDE, "sect": (sect + right + SIDE) % SIDE}

    around = [place(a, b) for a in (-1, 0, 1) for b in (-1, 0, 1) if (a, b) != (0, 0)]
    core = comp % 2

    def along(chips, other):
        return (comp - core + 2 * chips + COMPS) % COMPS + (core + other) % 2

    far_first = [along(*peer) for peer in FAR_FIRST]
    nearest = [{"comp": along(*peer)} for peer in ((1, 0), (-1, 0), (1, 1), (-1, 1), (0, 1))]
    barrier = pltpu.get_barrier_semaphore()
    for peer in around + nearest:
        pl.semaphore_signal(barrier, 1, device_id=peer, device_id_type=MESH)

    def tell(turn, chips):
        for peer in (along(chips, 0), along(-chips, 0)):
            pl.semaphore_signal(relay.at[turn], 1, device_id={"comp": peer}, device_id_type=MESH)

    small = [
        pltpu.make_async_copy(src, dst, small_sem.at[n])
        for n, (src, dst) in enumerate(
            [(land_ref, land), (ice_ref, ice), (wu_ref, wu), (wv_ref, wv), (depth_ref, depth),
             (table_ref.at[comp], tab)]
        )
    ]
    small[0].start()

    def load(group):
        rows = pl.ds(9 * group, 9)
        return pltpu.make_async_copy(spec_ref.at[rows], x.at[rows], load_sem.at[group])

    def group_of(quad, turn):
        return (quad - first + 4) % 4 + 4 * turn

    order = [(0, 0), (1, 0), (0, 1), (1, 1), (2, 0), (3, 0), (2, 1), (3, 1)]
    for quad, turn in order:
        load(group_of(quad, turn)).start()
    load(8).start()
    for copy in small[1:]:
        copy.start()

    lane = lane_index((8, 128))
    lane_pair = lane // 2
    sub = lax.broadcasted_iota(jnp.int32, (8, 128), 0)
    even_lane = lane % 2 == 0
    even_sub = sub % 2 == 0

    row_send[0, 9:12] = jnp.zeros((3, 8, 128), jnp.float32)
    row_send[1, 9:12] = jnp.zeros((3, 8, 128), jnp.float32)
    small[0].wait()
    wet[...] = (1 - land[...]).astype(jnp.float32)

    def pack(quad, turn, packed):
        group = group_of(quad, turn)
        row_slot = ROW_SLOT[quad] + turn if turn < 2 else EXTRA_SLOT
        col_slot = COL_SLOT[quad] + turn if turn < 2 else EXTRA_SLOT
        load(group).wait()
        for i in range(9):
            cells = x[9 * group + i]
            row = 2 * (9 * row_slot + i)
            to = (ROW_DIR[quad], row // 8, pl.ds(row % 8, 2))
            if ROW_DIR[quad] == 0:
                row_send[to] = cells[7, 6:8] * wet[7, 6:8, :]
            else:
                row_send[to] = cells[0, 0:2] * wet[0, 0:2, :]
            pair = 9 * col_slot + i
            shift = 2 * pair + 2 if COL_DIR[quad] == 0 else 2 * pair
            packed = jnp.where(lane_pair == pair, lanes(cells, shift), packed)
        return packed

    for way in (0, 1):
        packed = jnp.zeros((8, 8, 128), jnp.float32)
        for quad, turn in order:
            if COL_DIR[quad] == way:
                packed = pack(quad, turn, packed)
        col_send[way] = packed
    for quad in range(4):
        @pl.when(first == quad)
        def _(quad=quad):
            col_send[COL_DIR[quad]] = pack(quad, 2, col_send[COL_DIR[quad]])

    wet_now = wet[...]
    for way in (0, 1):
        at = 126 if way == 0 else 0
        one, two = wet_now[:, :, at : at + 1], wet_now[:, :, at + 1 : at + 2]
        pair_wet = jnp.where(even_lane, one, two)
        col_send[way] = jnp.where(lane_pair == 63, pair_wet, col_send[way] * pair_wet)
    row_send[0, 11, 2:4] = wet[7, 6:8, :]
    row_send[1, 11, 2:4] = wet[0, 0:2, :]

    pl.semaphore_wait(barrier, len(around) + len(nearest))

    def remote(src, dst, ssem, rsem, peer):
        return pltpu.make_async_remote_copy(
            src_ref=src, dst_ref=dst, send_sem=ssem, recv_sem=rsem, device_id=peer, device_id_type=MESH
        )

    halo = [
        remote(col_send.at[0], col_recv.at[0], halo_ssem.at[0], halo_rsem.at[0], place(0, 1)),
        remote(col_send.at[1], col_recv.at[1], halo_ssem.at[1], halo_rsem.at[1], place(0, -1)),
    ]
    for way in (0, 1):
        step = 1 if way == 0 else -1
        halo.append(
            remote(col_send.at[way, 7], corner_recv.at[way, 0], halo_ssem.at[2 + way], halo_rsem.at[2 + way],
                   place(1, step))
        )
        halo.append(
            remote(col_send.at[way, 0], corner_recv.at[way, 1], halo_ssem.at[4 + way], halo_rsem.at[4 + way],
                   place(-1, step))
        )
    halo.append(remote(row_send.at[0], row_recv.at[0], halo_ssem.at[6], halo_rsem.at[6], place(1, 0)))
    halo.append(remote(row_send.at[1], row_recv.at[1], halo_ssem.at[7], halo_rsem.at[7], place(-1, 0)))
    for copy in halo:
        copy.start()
    tell(0, 1)

    acc[...] = jnp.zeros_like(acc)
    for copy in small[1:]:
        copy.wait()
    open_sea = (1 - ice[...]).astype(jnp.float32)
    wu[...] = wu[...] * open_sea
    wv[...] = wv[...] * open_sea

    for quad in range(4):
        upwind_row = from_above if ROW_DIR[quad] == 0 else from_below
        upwind_col = from_left if COL_DIR[quad] == 0 else from_right

        def body(turn, carry, quad=quad, upwind_row=upwind_row, upwind_col=upwind_col):
            group = group_of(quad, turn)
            freq = (9 * comp + group) // 4
            slot = (first + group) // 4
            low = 0.7 * power(1.0 / 1.1, freq)
            scale = math.sqrt(0.5 * 1.1 ** (-(NF - 1))) * power(math.sqrt(1.1), freq)
            total_e = jnp.zeros((8, 8, 128), jnp.float32)
            total_f = jnp.zeros((8, 8, 128), jnp.float32)
            total_c = jnp.zeros((8, 8, 128), jnp.float32)
            for i in range(9):
                cosine, sine = direction(9 * quad + i)
                along_x, along_y = low * abs(cosine), low * abs(sine)
                stay = 1.0 - along_x - along_y
                cells = x[9 * group + i] * wet[...]
                for _ in range(2):
                    cells = wet[...] * (
                        stay * cells + along_x * upwind_row(cells) + along_y * upwind_col(cells)
                    )
                push = jnp.maximum((scale * cosine) * wu[...] + (scale * sine) * wv[...], 0.0)
                grown = cells + cells * (push * push)
                x[9 * group + i] = grown
                total_e += cells
                total_f += grown
                total_c += (cosine * cosine) * grown
            acc[6] += total_e
            acc[2 * slot] += total_f
            acc[2 * slot + 1] += total_c
            return carry

        lax.fori_loop(0, 2 + (first == quad).astype(jnp.int32), body, 0)
        if quad == 0:
            pl.semaphore_wait(relay.at[0], 2)
            tell(1, 2)

    for way in (0, 1):
        at = T_LANE + LANE_ROWS * way
        low_at = 0 if way == 0 else 126
        wind = [
            jnp.where(even_lane, w[:, :, low_at : low_at + 1], w[:, :, low_at + 1 : low_at + 2])
            for w in (wu, wv)
        ]
        push = jnp.maximum(tab[at + 3 : at + 4, :][None] * wind[0] + tab[at + 4 : at + 5, :][None] * wind[1], 0.0)
        col_gain[way] = 1.0 + push * push
        at = T_ROW + 96 * way
        spread = lambda n: jnp.broadcast_to(tab[at : at + 96, n : n + 1], (96, 128)).reshape(12, 8, 128)
        for n, source in enumerate((0, 1, 2, 5)):
            row_coef[way, n] = spread(source)
        tile, low_at = (0, 0) if way == 0 else (7, 6)
        wind = [
            jnp.where(even_sub, w[tile, low_at : low_at + 1, :], w[tile, low_at + 1 : low_at + 2, :])
            for w in (wu, wv)
        ]
        push = jnp.maximum(spread(3) * wind[0] + spread(4) * wind[1], 0.0)
        row_gain[way] = 1.0 + push * push

    for copy in halo:
        copy.wait_recv()

    has = {
        "up": (slab > 0).astype(jnp.float32), "down": (slab < SIDE - 1).astype(jnp.float32),
        "left": (sect > 0).astype(jnp.float32), "right": (sect < SIDE - 1).astype(jnp.float32),
    }
    col_terms, col_weights = [], []
    for way in (0, 1):
        lane_row = lambda n: tab[T_LANE + LANE_ROWS * way + n : T_LANE + LANE_ROWS * way + n + 1, :][None]
        stay, along_x, along_y, is_up = [lane_row(n) for n in (0, 1, 2, 5)]
        side = has["left"] if way == 0 else has["right"]
        got = col_recv[way] * side
        above = corner_recv[way, 0] * (side * has["up"])
        below = corner_recv[way, 1] * (side * has["down"])
        turn = 127 if way == 0 else 1
        near, near_above, near_below = lanes(got, turn), lanes(above, turn), lanes(below, turn)
        halo_wet = got[:, :, 127:128] if way == 0 else got[:, :, 126:127]
        at_near, at_far = (0, 1) if way == 0 else (127, 126)
        wet_near, wet_far = wet_now[:, :, at_near : at_near + 1], wet_now[:, :, at_far : at_far + 1]
        up_now = jnp.where(is_up > 0.5, from_above(near, near_above), from_below(near, near_below))
        outside = halo_wet * (stay * near + along_x * up_now + along_y * got)
        one = wet_near * (along_y * near)
        up_one = jnp.where(is_up > 0.5, from_above(one), from_below(one))
        two = wet_near * (stay * one + along_x * up_one + along_y * outside)
        far = lanes(wet_far * (along_y * one), 1 if way == 0 else 127)
        fix = jnp.where(even_lane, two, far) if way == 0 else jnp.where(even_lane, far, two)
        fix_grown = fix * col_gain[way]
        col_fix[way] = fix_grown
        col_terms += [fix_grown.reshape(64, 128), fix.reshape(64, 128)]
        at = T_COL + 64 * way
        col_weights += [tab[at : at + 32, :], tab[at + 32 : at + 64, :]]
    col_weights = jnp.concatenate(
        [jnp.concatenate(col_weights, axis=1), jnp.zeros((96, 512), jnp.float32)], axis=0
    )
    col_out = lax.dot_general(
        jnp.concatenate(col_terms, axis=1), col_weights, (((1,), (1,)), ((), ())),
        precision=HIGHEST, preferred_element_type=jnp.float32,
    ).reshape(8, 8, 128)
    rim_lane = (lane < 2) | (lane >= 126)
    for slot in range(3):
        acc[2 * slot] += jnp.where(rim_lane, lanes(col_out, 126 - 4 * slot), 0.0)
        acc[2 * slot + 1] += jnp.where(rim_lane, lanes(col_out, 110 - 4 * slot), 0.0)
    acc[6] += jnp.where(rim_lane, lanes(col_out, 114), 0.0)

    for way in (0, 1):
        stay, along_x, along_y, is_left = [row_coef[way, n] for n in range(4)]
        side = has["up"] if way == 0 else has["down"]
        got = row_recv[way] * side
        near = pltpu.roll(got, 7 if way == 0 else 1, 1)
        edge = 7 if way == 0 else 0
        left_corner = corner_recv[0, way, edge : edge + 1, :] * (side * has["left"])
        right_corner = corner_recv[1, way, edge : edge + 1, :] * (side * has["right"])
        choose = tab[T_PICK + 96 * way : T_PICK + 96 * way + 96, :].reshape(12, 8, 128)
        corner = jnp.sum(
            choose * jnp.where(is_left > 0.5, left_corner[None], right_corner[None]), axis=2, keepdims=True
        )
        halo_wet = got[11, 3:4, :] if way == 0 else got[11, 2:3, :]
        tile, near_row, far_row = (0, 0, 1) if way == 0 else (7, 7, 6)
        wet_near, wet_far = wet[tile, near_row : near_row + 1, :], wet[tile, far_row : far_row + 1, :]
        lane3 = lane_index((12, 8, 128))
        beside = jnp.where(
            is_left > 0.5,
            jnp.where(lane3 == 0, corner, lanes(near, 1)),
            jnp.where(lane3 == 127, corner, lanes(near, 127)),
        )
        outside = halo_wet * (stay * near + along_x * got + along_y * beside)
        one = wet_near * (along_x * near)
        beside_one = jnp.where(is_left > 0.5, from_left(one), from_right(one))
        two = wet_near * (stay * one + along_y * beside_one + along_x * outside)
        far = pltpu.roll(wet_far * (along_x * one), 1 if way == 0 else 7, 1)
        fix = jnp.where(even_sub, two, far) if way == 0 else jnp.where(even_sub, far, two)
        fix_grown = fix * row_gain[way]
        row_fix[way] = fix_grown
        at = T_SUM + 64 * way
        weights = tab[at : at + 48, 0:96]
        sum_grown = jnp.dot(weights, fix_grown.reshape(96, 128), precision=HIGHEST,
                            preferred_element_type=jnp.float32)
        sum_moved = jnp.dot(tab[at + 48 : at + 56, 0:96], fix.reshape(96, 128), precision=HIGHEST,
                            preferred_element_type=jnp.float32)
        for v in range(6):
            acc[v, tile] += sum_grown[8 * v : 8 * v + 8]
        acc[6, tile] += sum_moved

    low_half = sub < 4
    for slot in range(4):
        if slot < 3:
            one, two = acc[2 * slot], acc[2 * slot + 1]
            even_tile = jnp.where(low_half, one, pltpu.roll(two, 4, 1))
            odd_tile = jnp.where(low_half, pltpu.roll(one, 4, 1), two)
        else:
            even_tile, odd_tile = acc[6], pltpu.roll(acc[6], 4, 1)
        for tile in range(8):
            rs_send[2 * tile, 8 * slot : 8 * slot + 8] = even_tile[tile]
            rs_send[2 * tile + 1, 8 * slot : 8 * slot + 8] = odd_tile[tile]
    pl.semaphore_wait(relay.at[1], 2)
    rs = []
    for n, peer in enumerate(far_first):
        rs.append(
            remote(rs_send.at[peer, pl.ds(0, 28)], rs_recv.at[comp, pl.ds(0, 28)], rs_ssem.at[n],
                   rs_rsem.at[n], {"comp": peer})
        )
    for copy in rs:
        copy.start()
    rs_recv[comp] = rs_send[comp]

    def amend(quad, turn):
        group = group_of(quad, turn)
        row_slot = ROW_SLOT[quad] + turn if turn < 2 else EXTRA_SLOT
        col_slot = COL_SLOT[quad] + turn if turn < 2 else EXTRA_SLOT
        way = COL_DIR[quad]
        fixes = col_fix[way]
        inside = lane < 2 if way == 0 else lane >= 126
        for i in range(9):
            at = 9 * group + i
            pair = 2 * (9 * col_slot + i)
            moved = lanes(fixes, -pair if way == 0 else 126 - pair)
            x[at] = x[at] + jnp.where(inside, moved, 0.0)
            row = 2 * (9 * row_slot + i)
            rows = row_fix[ROW_DIR[quad], row // 8, row % 8 : row % 8 + 2, :]
            if ROW_DIR[quad] == 0:
                x[at, 0, 0:2, :] += rows
            else:
                x[at, 7, 6:8, :] += rows

    for quad in range(4):
        for turn in (0, 1):
            amend(quad, turn)
        @pl.when(first == quad)
        def _(quad=quad):
            amend(quad, 2)

    for copy in halo + rs:
        copy.wait_send()
    for copy in rs:
        copy.wait_recv()

    energy = tree_sum([rs_recv[source, 24:28, :] for source in range(COMPS)])
    energy = energy / K
    energy = jnp.concatenate([energy, energy], axis=0)
    square = energy * energy
    parts = []
    for freq in range(NF):
        part = None
        for source in range(COMPS):
            slot = freq - 9 * source // 4
            if 0 <= slot < 3:
                tile = rs_recv[source, 8 * slot : 8 * slot + 8, :]
                part = tile if part is None else part + tile
        part = part / (1.0 + (2.0 * 1.1 ** (freq - (NF - 1))) * square)
        parts.append(part)
    plain = tree_sum(parts)
    shoaled = tree_sum([(0.5 + 0.5 * freq / (NF - 1)) * part for freq, part in enumerate(parts)])
    turned = pltpu.roll(shoaled, 4, 0)
    final = plain / K
    stress_x = (turned + shoaled - 0.5 * plain) / K
    stress_y = (2.0 * shoaled - turned - 0.5 * plain) / K
    ag_send[0] = jnp.where(low_half, stress_x, pltpu.roll(stress_y, 4, 0))
    ag_send[1] = jnp.where(low_half, energy, pltpu.roll(final, 4, 0))
    ag = [
        [
            remote(ag_send.at[n], ag_recv.at[n, comp], ag_ssem.at[n, at], ag_rsem.at[n, at], {"comp": peer})
            for at, peer in enumerate(far_first)
        ]
        for n in (0, 1)
    ]
    for copy in ag[0]:
        copy.start()
    ag_recv[0, comp] = ag_send[0]
    ag_recv[1, comp] = ag_send[1]
    for copy in ag[0][:AFTER:-1]:
        copy.wait_recv()
    for copy in ag[1]:
        copy.start()
    for copy in ag[0][AFTER::-1]:
        copy.wait_recv()

    def whole(n):
        gathered = ag_recv[n].reshape(8, 2, 8, 128)
        one, two = gathered[:, 0], gathered[:, 1]
        return (
            jnp.where(low_half, one, pltpu.roll(two, 4, 1)),
            jnp.where(low_half, pltpu.roll(one, 4, 1), two),
        )

    stress_x, stress_y = whole(0)

    edge_send[0] = stress_x
    edge_send[1] = stress_y
    strip_send[...] = jnp.where(
        (lane < 8) | (lane >= 120), stress_x, jnp.where(lane < 64, lanes(stress_y, 8), lanes(stress_y, 120))
    )
    rim = [
        remote(strip_send, strip_recv.at[0], rim_ssem.at[0], rim_rsem.at[0], place(0, 1)),
        remote(strip_send, strip_recv.at[1], rim_ssem.at[1], rim_rsem.at[1], place(0, -1)),
        remote(edge_send.at[:, 7], edge_recv.at[0], rim_ssem.at[2], rim_rsem.at[2], place(1, 0)),
        remote(edge_send.at[:, 0], edge_recv.at[1], rim_ssem.at[3], rim_rsem.at[3], place(-1, 0)),
        remote(strip_send.at[7], tip_recv.at[0, 0], rim_ssem.at[4], rim_rsem.at[4], place(1, 1)),
        remote(strip_send.at[7], tip_recv.at[1, 0], rim_ssem.at[5], rim_rsem.at[5], place(1, -1)),
        remote(strip_send.at[0], tip_recv.at[0, 1], rim_ssem.at[6], rim_rsem.at[6], place(-1, 1)),
        remote(strip_send.at[0], tip_recv.at[1, 1], rim_ssem.at[7], rim_rsem.at[7], place(-1, -1)),
    ]
    for copy in rim:
        copy.start()
    for copy in ag[1]:
        copy.wait_recv()
    energy, final = whole(1)
    start = (9 * comp) // 4
    high = 1.1 ** (-(NF - 1)) * power(1.1, start)
    rates = [
        1.0 / (1.0 + (2.0 * 1.1**slot * high) * (energy * energy)) for slot in range(3)
    ]
    for copy in ag[0] + ag[1]:
        copy.wait_send()
    for copy in rim:
        copy.wait_recv()

    big_lane = lane_index((80, 128))
    big_row = lax.broadcasted_iota(jnp.int32, (80, 128), 0)
    first_row = jnp.where(slab > 0, 0, 8)
    last_row = jnp.where(slab < SIDE - 1, 80, 72)
    in_rows = (big_row >= first_row) & (big_row < last_row)
    right_end = jnp.where(sect < SIDE - 1, 8, 0)
    left_start = jnp.where(sect > 0, 120, 128)
    in_strip = in_rows & ((big_lane < right_end) | (big_lane >= left_start))

    def middle(n, cells):
        return jnp.where(
            in_rows,
            jnp.concatenate([edge_recv[0, n], cells.reshape(64, 128), edge_recv[1, n]], axis=0),
            0.0,
        )

    left_strip = jnp.concatenate([tip_recv[0, 0], strip_recv[0].reshape(64, 128), tip_recv[0, 1]], axis=0)
    right_strip = jnp.concatenate([tip_recv[1, 0], strip_recv[1].reshape(64, 128), tip_recv[1, 1]], axis=0)
    xx = middle(0, stress_x)
    yy = middle(1, stress_y)
    xx_strip = jnp.where(in_strip, jnp.where(big_lane < 64, right_strip, left_strip), 0.0)
    yy_strip = jnp.where(
        in_strip, jnp.where(big_lane < 64, lanes(right_strip, 120), lanes(left_strip, 8)), 0.0
    )

    def beside(center, strip):
        center_up, strip_up = lanes(center, 127), lanes(strip, 127)
        center_down, strip_down = lanes(center, 1), lanes(strip, 1)
        last, head = big_lane == 127, big_lane == 0
        return (
            jnp.where(last, strip_up, center_up) + jnp.where(head, strip_down, center_down),
            jnp.where(last, center_up, strip_up) + jnp.where(head, center_down, strip_down),
        )

    def above_below(cells):
        return pltpu.roll(cells, 1, 0) + pltpu.roll(cells, 79, 0)

    yy_sides = beside(yy, yy_strip)
    source = jnp.where(in_rows, -((above_below(xx) - 2.0 * xx) + (yy_sides[0] - 2.0 * yy)), 0.0)
    source_strip = jnp.where(
        in_strip, -((above_below(xx_strip) - 2.0 * xx_strip) + (yy_sides[1] - 2.0 * yy_strip)), 0.0
    )
    surge, surge_strip = source * (1.0 / 4.5), source_strip * (1.0 / 4.5)
    for _ in range(JAC):
        sides = beside(surge, surge_strip)
        surge, surge_strip = (
            jnp.where(in_rows, (source + above_below(surge) + sides[0]) * (1.0 / 4.5), 0.0),
            jnp.where(in_strip, (source_strip + above_below(surge_strip) + sides[1]) * (1.0 / 4.5), 0.0),
        )
    surge = surge[8:72].reshape(8, 8, 128)
    reach = depth[...] + surge
    depth_term = reach * reach + 1.0
    damping = depth_term / (depth_term + 4.0 * final)
    for slot in range(3):
        factor_ref[slot] = rates[slot] * damping
    level_ref[...] = surge

    for copy in rim:
        copy.wait_send()


def damp_kernel(grown_ref, factor_ref, level_ref, out_ref, level_out, x, out_sem, small_sem):
    first = lax.axis_index("comp") % 4

    def store(part):
        rows = pl.ds(27 * part, 27)
        return pltpu.make_async_copy(x.at[rows], out_ref.at[rows], out_sem.at[part])

    surge = pltpu.make_async_copy(level_ref, level_out, small_sem.at[0])
    for group in range(GROUPS):
        factor = factor_ref[(first + group) // 4]
        for i in range(9):
            x[9 * group + i] = grown_ref[9 * group + i] * factor
        if group % 3 == 2:
            store(group // 3).start()
        if group == 2:
            surge.start()
    surge.wait()
    for part in range(3):
        store(part).wait()


def local(spectrum, land_mask, ice_mask, wind_u, wind_v, depth):
    f32 = jnp.float32
    block = (8, 8, 128)
    anywhere = pl.BlockSpec(memory_space=pl.ANY)
    vmem = pl.BlockSpec(memory_space=pltpu.VMEM)
    dma = pltpu.SemaphoreType.DMA
    grown, factor, level = pl.pallas_call(
        step_kernel,
        out_shape=(
            pltpu.VMEM((LOCAL, *block), f32),
            pltpu.VMEM((3, *block), f32),
            pltpu.VMEM(block, f32),
        ),
        in_specs=[anywhere] * 7,
        out_specs=(vmem, vmem, vmem),
        scratch_shapes=[
            pltpu.VMEM(block, jnp.int32),
            pltpu.VMEM(block, jnp.int32),
            pltpu.VMEM(block, f32),
            pltpu.VMEM(block, f32),
            pltpu.VMEM(block, f32),
            pltpu.VMEM((T_END, 128), f32),
            pltpu.VMEM(block, f32),
            pltpu.VMEM((2, 12, 8, 128), f32),
            pltpu.VMEM((2, 12, 8, 128), f32),
            pltpu.VMEM((2, *block), f32),
            pltpu.VMEM((2, *block), f32),
            pltpu.VMEM((2, 2, 8, 128), f32),
            pltpu.VMEM((7, *block), f32),
            pltpu.VMEM((2, 12, 8, 128), f32),
            pltpu.VMEM((2, *block), f32),
            pltpu.VMEM((2, 4, 12, 8, 128), f32),
            pltpu.VMEM((2, 12, 8, 128), f32),
            pltpu.VMEM((2, *block), f32),
            pltpu.VMEM((COMPS, 32, 128), f32),
            pltpu.VMEM((COMPS, 32, 128), f32),
            pltpu.VMEM((2, 8, 128), f32),
            pltpu.VMEM((2, COMPS, 8, 128), f32),
            pltpu.VMEM((2, *block), f32),
            pltpu.VMEM((2, 2, 8, 128), f32),
            pltpu.VMEM(block, f32),
            pltpu.VMEM((2, *block), f32),
            pltpu.VMEM((2, 2, 8, 128), f32),
            pltpu.SemaphoreType.REGULAR((2,)),
            dma((GROUPS,)),
            dma((6,)),
            dma((8,)),
            dma((8,)),
            dma((COMPS,)),
            dma((COMPS,)),
            dma((2, COMPS)),
            dma((2, COMPS)),
            dma((8,)),
            dma((8,)),
        ],
        compiler_params=pltpu.CompilerParams(
            collective_id=0, has_side_effects=True, vmem_limit_bytes=24 * 1024 * 1024
        ),
        name="wave_step",
    )(
        *[
            pltpu.with_memory_space_constraint(operand, pltpu.HBM)
            for operand in (
                spectrum.reshape(LOCAL, *block),
                land_mask.reshape(block),
                ice_mask.reshape(block),
                wind_u.reshape(block),
                wind_v.reshape(block),
                depth.reshape(block),
                jnp.asarray(table()),
            )
        ]
    )
    damped, level = pl.pallas_call(
        damp_kernel,
        out_shape=(jax.ShapeDtypeStruct((LOCAL, *block), f32), jax.ShapeDtypeStruct(block, f32)),
        in_specs=[vmem] * 3,
        out_specs=(anywhere, anywhere),
        scratch_shapes=[
            pltpu.VMEM((LOCAL, *block), f32),
            dma((3,)),
            dma((1,)),
        ],
        compiler_params=pltpu.CompilerParams(vmem_limit_bytes=24 * 1024 * 1024),
        name="damp",
    )(*[pltpu.with_memory_space_constraint(operand, pltpu.VMEM) for operand in (grown, factor, level)])
    return damped.reshape(spectrum.shape), level.reshape(depth.shape)


def solution(mesh):
    cells = P("slab", "sect")
    spectra = P("comp", "slab", "sect")
    return jax.shard_map(
        local,
        mesh=mesh,
        in_specs=(spectra, cells, cells, cells, cells, cells),
        out_specs=(spectra, cells),
        check_vma=False,
    )
```
